32 devices in a mesh: sec: 4 (over y, x), seq: 4 (over z), tp: 2 (over core).
Axes of the slice: x: 2, y: 2, z: 4, core: 2. Of those that a mesh axis runs over, the one named last changes fastest.
Arguments:
- hidden: bfloat16 [1024, 5120], P('seq', ('sec', 'tp')), may hold values from -6 to 6
- projection: bfloat16 [5120, 5120], P('seq', ('sec', 'tp')), may hold values from -0.078125 to 0.078125
- norm_gain: float32 [5120], replicated, may hold values from 0.1 to 1.9
- old_logp: float32 [1024], P('seq'), may hold values from -2.5 to 0
- ref_logp: float32 [1024], P('seq'), may hold values from -2.5 to 0
- lengths: int32 [16], P('seq'), may hold values from 1 to 64, 512 in all
- group_of: int32 [16], P('seq'), may hold values from 0 to 1, as said below
- rewards: int32 [16], P('seq'), may hold values from 0 to 4
Outputs:
- ref_states: bfloat16 [512, 5120], P('seq', ('sec', 'tp'))
- token_terms: bfloat16 [512, 2], P('seq')
The draws below stay inside these ranges and needn't reach their ends.
Inputs may be any that keep to these rules, and one draw needn't show every extreme that they name: `group_of`: each group number names exactly 8 responses. The lengths sum to 512; the longest is exactly 64.
All inputs are finite; a program needn't handle non-finite values. No bound on the sum of `lengths` on one device may be relied on, other than what follows from the above.
Results may differ from the reference program's by a relative error of at most 0.0039.
Values may be sent and summed in bfloat16 or wider, within the bound.
No kernel may reach another device: no remote copies, remote signals or barrier semaphores. Data moves between devices by JAX's collectives and lax.ppermute only.
A program may use at most 64 MiB of HBM per device.

```python
import math
import jax
import jax.numpy as jnp
import numpy as np
from jax import lax

D = 5120
TOK_DEV = 128
GROUP = 8
LMAX = 64
TILE = 64
RESPONSES = 16
TOKENS = 512
N_SEQ = 4


def draw_group_of(key, part):
    order = jax.random.permutation(key, RESPONSES)
    return (order // GROUP).astype(jnp.int32)


def touch_ends(drawn, own_key, smallest, top_value):
    shape = drawn.shape
    place = [jax.random.randint(jax.random.fold_in(own_key, axis), (), 0, shape[axis]) for axis in range(len(shape))]
    drawn = drawn.at[tuple(place)].set(smallest)
    longest = shape.index(max(shape))
    place[longest] = (place[longest] + 1) % shape[longest]
    return drawn.at[tuple(place)].set(top_value)


def levels(key, dims, split, smallest, top_value):
    gain, own = 1.0, jax.random.fold_in(key, 6)
    for position, shards_of in split:
        draws = jnp.exp(jax.random.uniform(jax.random.fold_in(own, position), (shards_of,), jnp.float32, smallest / len(split), top_value / len(split)))
        gain = gain * jnp.repeat(draws, dims[position] // shards_of).reshape([-1 if axis == position else 1 for axis in range(len(dims))])
    return gain


def profile(number_of, total, bound, lean):
    portions = [(1 << 20) // math.isqrt(standing ** lean) + 1 for standing in range(2, number_of + 1)]
    spare, given = total - bound - (number_of - 1), [1] * (number_of - 1)
    while spare > 0:
        free = [i for i in range(number_of - 1) if given[i] < bound]
        mass, left = sum([portions[i] for i in free]), spare
        for i in free:
            more = min(bound - given[i], max(1, left * portions[i] // mass), spare)
            given[i] = given[i] + more
            spare = spare - more
    return np.array([bound] + given)


def uneven_parts(stream_key, count, total, limit, lean):
    if count == 2:
        one = jax.random.randint(stream_key, (), max(1, total - limit), min(limit, total - 1) + 1)
        return jnp.stack([one, total - one])
    sizes = jnp.asarray(profile(count, total, limit, lean), jnp.int32)
    pairs = (count - 1) // 2
    source_of, receiver = sizes[1:1 + 2 * pairs:2], sizes[2:2 + 2 * pairs:2]
    margin = jnp.minimum(source_of - 1, limit - receiver)
    moved = jax.random.randint(jax.random.fold_in(stream_key, 1), (pairs,), 0, 1 << 20) % (margin + 1)
    sizes = sizes.at[1:1 + 2 * pairs:2].set(source_of - moved).at[2:2 + 2 * pairs:2].set(receiver + moved)
    return sizes[jax.random.permutation(jax.random.fold_in(stream_key, 2), count)]


def gaussian(own_key, extent, width, reach, cuts=(), kind=jnp.bfloat16):
    entries = jax.random.normal(own_key, extent, jnp.float32) * width
    if len(cuts) > 0:
        entries = levels(own_key, extent, cuts, -0.22, 0.18) * entries
    return jnp.clip(entries, min=-reach, max=reach).astype(kind)


def setup_inputs(seed: int = 0) -> dict:
    arg_keys = jax.random.split(jax.random.key(seed), 9)
    return {
        "hidden": gaussian(arg_keys[0], (RESPONSES * LMAX, D), 1.0, 6.0, ((0, 4), (1, 8))),
        "projection": gaussian(arg_keys[1], (D, D), D ** -0.5, 0.078125, ((0, 4), (1, 8))),
        "norm_gain": jnp.clip(1.0 + 0.18 * jax.random.normal(arg_keys[2], (D,), jnp.float32), 0.1, 1.9),
        "old_logp": jnp.clip(-2.5 + 2.5 * jax.random.uniform(arg_keys[3], (RESPONSES * LMAX,), jnp.float32) ** levels(arg_keys[3], (RESPONSES * LMAX,), ((0, 4),), -0.2, 0.2), -2.5, 0.0),
        "ref_logp": jnp.clip(-2.5 + 2.5 * jax.random.uniform(arg_keys[4], (RESPONSES * LMAX,), jnp.float32) ** levels(arg_keys[4], (RESPONSES * LMAX,), ((0, 4),), -0.2, 0.2), -2.5, 0.0),
        "lengths": uneven_parts(arg_keys[5], RESPONSES, TOKENS, LMAX, 2).astype(jnp.int32),
        "group_of": draw_group_of(jax.random.fold_in(arg_keys[8], 71), 0),
        "rewards": touch_ends(jax.random.randint(arg_keys[7], (RESPONSES,), 0, 5), jax.random.fold_in(arg_keys[7], 1), 0, 4).astype(jnp.int32),
    }


def refine_block(block_rows, projection, norm_gain):
    widened = block_rows.astype(jnp.float32)
    squares = lax.optimization_barrier(jnp.sum(widened * widened, axis=1, keepdims=True))
    normed = (widened * lax.rsqrt(squares / D + 1e-06) * norm_gain).astype(jnp.bfloat16)
    mixing = jnp.dot(normed, projection, preferred_element_type=jnp.float32)
    return (widened + mixing).astype(jnp.bfloat16)

def reference(hidden, projection, norm_gain, old_logp, ref_logp, lengths, group_of, rewards):
    finish = jnp.cumsum(lengths).astype(jnp.int32)
    opening = (finish - lengths).astype(jnp.int32)
    learner_row = jnp.arange(TOKENS, dtype=jnp.int32)
    shard_of = learner_row // TOK_DEV
    within = learner_row % TOK_DEV
    packed = within // TILE * (TILE * N_SEQ) + shard_of * TILE + within % TILE
    response = jnp.searchsorted(finish, packed, side='right').astype(jnp.int32)
    source = (response * LMAX + packed - jnp.take(opening, response)).astype(jnp.int32)
    gathered = jnp.take(hidden, source, axis=0)
    step_rows = math.gcd(TOKENS, 512)
    blocks = gathered.reshape(TOKENS // step_rows, step_rows, D)
    ref_states = lax.map(lambda block_rows: refine_block(block_rows, projection, norm_gain), blocks).reshape(TOKENS, D)
    member_table = (group_of[:, None] == jnp.arange(RESPONSES // GROUP, dtype=jnp.int32)[None, :]).astype(jnp.float32)
    reward_value = rewards.astype(jnp.float32)
    group_total = jnp.dot(reward_value, member_table, precision=lax.Precision.HIGHEST)
    group_square = jnp.dot(reward_value * reward_value, member_table, precision=lax.Precision.HIGHEST)
    group_mean = group_total / GROUP
    spread = jnp.maximum(jnp.sqrt(group_square / GROUP - group_mean * group_mean), 1.0)
    advantage = (reward_value - jnp.dot(member_table, group_mean, precision=lax.Precision.HIGHEST)) / jnp.dot(member_table, spread, precision=lax.Precision.HIGHEST)
    log_ratio = jnp.take(ref_logp, source) - jnp.take(old_logp, source)
    penalty = jnp.exp(log_ratio) - log_ratio - 1.0
    token_terms = jnp.stack([jnp.take(advantage, response), penalty], axis=1).astype(jnp.bfloat16)
    return (ref_states, token_terms)
```

```python
import functools

import jax
import jax.numpy as jnp
from jax import lax
from jax.experimental import pallas as pl
from jax.experimental.pallas import tpu as pltpu
from jax.sharding import PartitionSpec as P

D = 5120
TOK_DEV = 128
RESP_DEV = 4
GROUP = 8
LMAX = 64
TILE = 64
SLOTS = 256
EPS = 1e-06
BF16 = jnp.bfloat16
F32 = jnp.float32
I32 = jnp.int32

VMEM = pl.BlockSpec(memory_space=pltpu.VMEM)
SMEM = pl.BlockSpec(memory_space=pltpu.SMEM)


def iota(shape, dim):
    return lax.broadcasted_iota(I32, shape, dim)


def swap(x, axis, k):
    n = lax.axis_size(axis)
    return lax.ppermute(x, axis, [(i, i ^ k) for i in range(n)])


def info_kernel(lengths, group_of, rewards, old_logp, ref_logp, out):
    n = lengths.shape[0]
    rows = old_logp.shape[0]
    log_ratio = ref_logp[...] - old_logp[...]
    penalty = jnp.exp(log_ratio) - log_ratio - 1.0
    lane = iota((1, 128), 1)
    last = jnp.zeros((1, 128), F32)
    for r in range(n):
        for place, ref in enumerate((lengths, group_of, rewards)):
            last = jnp.where(lane == place * n + r, ref[r].astype(F32), last)
    out[...] = jnp.zeros_like(out)
    out[0:rows, :] = penalty.astype(BF16).astype(F32)
    out[rows : rows + 1, :] = last


def spread_kernel(n_sec, n_tp, lengths, own, sibling, *outs):
    a = lax.axis_index("sec")
    t = lax.axis_index("tp")
    n_class = n_sec * n_tp
    slots, width = outs[0].shape[0], own.shape[1]
    rows = own.shape[0]
    place = iota((n_sec * slots, 1), 0)
    index = (place % slots) * n_class + ((place // slots) ^ a) * n_tp + t
    source, finish = index, 0
    for r in range(lengths.shape[0]):
        finish = finish + lengths[r]
        source = source + jnp.where(index >= finish, LMAX - lengths[r], 0)
    source = jnp.where(index < finish, source, -1)
    pick = (iota((n_sec * slots, rows), 1) == source).astype(BF16)
    mine = jnp.dot(pick, own[...], preferred_element_type=F32)
    other = jnp.dot(pick, sibling[...], preferred_element_type=F32)
    first = jnp.where(t == 0, mine, other).astype(BF16)
    second = jnp.where(t == 0, other, mine).astype(BF16)
    for k, out in enumerate(outs):
        out[:, 0:width] = first[k * slots : (k + 1) * slots]
        out[:, width : 2 * width] = second[k * slots : (k + 1) * slots]


def norm_kernel(n, gain, *refs):
    inputs, outs, held = refs[:n], refs[n : 2 * n], refs[2 * n]
    a = lax.axis_index("sec")
    s = lax.axis_index("seq")
    width = inputs[0].shape[1]
    squares = 0.0
    for ref in inputs:
        x = ref[...].astype(F32)
        squares = squares + jnp.sum(x * x, axis=1, keepdims=True)
    scale = lax.rsqrt(squares / D + EPS)
    for k, ref in enumerate(inputs):
        start = pl.multiple_of((a ^ k) * width, 128)
        held[k] = (ref[...].astype(F32) * scale * gain[:, pl.ds(start, width)]).astype(BF16)
    for m, out in enumerate(outs):
        out[...] = held[a ^ s ^ m]


def put_counts(infos, row, n, counts):
    s = lax.axis_index("seq")
    for m, info in enumerate(infos):
        total = 0.0
        for r in range(n):
            total = total + info[row, r]
        counts[s ^ m] = total.astype(I32)


def pack_kernel(n, n_class, n_resp, row, *refs):
    infos, inputs, out, held, counts = refs[:n], refs[n : 2 * n], refs[2 * n], refs[2 * n + 1], refs[2 * n + 2]
    s = lax.axis_index("seq")
    c = lax.axis_index("sec") * lax.axis_size("tp") + lax.axis_index("tp")
    slots = inputs[0].shape[0]
    put_counts(infos, row, n_resp, counts)
    lane = iota((1, n * slots), 1)
    place = jnp.zeros((1, n * slots), I32)
    first = 0
    for b in range(n):
        live = (counts[b] - c + n_class - 1) // n_class
        block = lane // slots == (s ^ b)
        q = lane % slots
        place = jnp.where(block, jnp.where(q < live, first + q, -1), place)
        first = first + live
    for m, ref in enumerate(inputs):
        held[m * slots : (m + 1) * slots, :] = ref[...]
    pick = (iota((out.shape[0], n * slots), 0) == place).astype(BF16)
    out[...] = jnp.dot(pick, held[...], preferred_element_type=F32).astype(BF16)


def mix_kernel(n, n_class, n_resp, row, *refs):
    infos = refs[:n]
    lengths, hidden, projection, mine, other = refs[n : n + 5]
    outs = refs[n + 5 : 2 * n + 5]
    counts = refs[2 * n + 5]
    s = lax.axis_index("seq")
    t = lax.axis_index("tp")
    n_tp = lax.axis_size("tp")
    put_counts(infos, row, n_resp, counts)
    tok = outs[0].shape[0]
    tokens = n * tok
    per_sec = mine.shape[0] * n_tp // n_class
    place = iota((tokens, 1), 0)
    w = place % tok
    packed = w // TILE * (TILE * n) + ((place // tok) ^ s) * TILE + w % TILE
    seq_of = jnp.zeros((tokens, 1), I32)
    start = jnp.zeros((tokens, 1), I32)
    finish = 0
    for b in range(n):
        finish = finish + counts[b]
        passed = packed >= finish
        seq_of = seq_of + passed.astype(I32)
        start = jnp.where(passed, finish, start)
    index = packed - start
    cls = index % n_class
    position = index // n_class
    for b in range(n - 1):
        live = (counts[b] - cls + n_class - 1) // n_class
        position = position + jnp.where(seq_of > b, live, 0)
    column = ((cls % n_tp) ^ t) * mine.shape[0] + (cls // n_tp) * per_sec + position
    half = mine.shape[0]
    pick_mine = (iota((tokens, half), 1) == column).astype(BF16)
    pick_other = (iota((tokens, half), 1) + half == column).astype(BF16)
    normed = jnp.dot(pick_mine, mine[...], preferred_element_type=F32) + jnp.dot(
        pick_other, other[...], preferred_element_type=F32
    )
    mixing = jnp.dot(normed.astype(BF16), projection[...], preferred_element_type=F32)
    source, ends = index, 0
    for r in range(n_resp):
        ends = ends + lengths[r]
        source = source + jnp.where(index >= ends, LMAX - lengths[r], 0)
    source = jnp.where(seq_of == s, source, -1)
    pick = (iota((tokens, hidden.shape[0]), 1) == source).astype(BF16)
    total = mixing + jnp.dot(pick, hidden[...], preferred_element_type=F32)
    for m, out in enumerate(outs):
        out[...] = total[m * tok : (m + 1) * tok].astype(out.dtype)


def terms_kernel(n, n_resp, row, *refs):
    infos, out, words, table = refs[:n], refs[n], refs[n + 1], refs[n + 2]
    s = lax.axis_index("seq")
    tok = out.shape[1]
    group_count = n * n_resp // GROUP
    for m, info in enumerate(infos):
        table[pl.ds((s ^ m) * row, row), :] = info[0:row, :]
        for r in range(3 * n_resp):
            words[s ^ m, r] = jnp.sum(jnp.where(iota((1, 128), 1) == r, info[row : row + 1, :], 0.0)).astype(I32)
    w = iota((1, tok), 1)
    packed = w // TILE * (TILE * n) + s * TILE + w % TILE
    source, finish = packed, 0
    reward = jnp.zeros((1, tok), F32)
    group = jnp.zeros((1, tok), I32)
    total = [0] * group_count
    square = [0] * group_count
    for b in range(n):
        for r in range(n_resp):
            length, number, gain = words[b, r], words[b, n_resp + r], words[b, 2 * n_resp + r]
            within = packed >= finish
            reward = jnp.where(within, gain.astype(F32), reward)
            group = jnp.where(within, number, group)
            finish = finish + length
            source = source + jnp.where(packed >= finish, LMAX - length, 0)
            for g in range(group_count):
                total[g] = total[g] + jnp.where(number == g, gain, 0)
                square[g] = square[g] + jnp.where(number == g, gain * gain, 0)
    total_of = jnp.zeros((1, tok), F32)
    square_of = jnp.zeros((1, tok), F32)
    for g in range(group_count):
        total_of = jnp.where(group == g, total[g].astype(F32), total_of)
        square_of = jnp.where(group == g, square[g].astype(F32), square_of)
    mean = total_of / GROUP
    spread = jnp.maximum(jnp.sqrt(square_of / GROUP - mean * mean), 1.0)
    advantage = (reward - mean) / spread
    pick = (iota((128, tok), 0) == source % 128).astype(BF16)
    found = jnp.dot(table[...].astype(BF16), pick, preferred_element_type=F32)
    chosen = iota(found.shape, 0) == source // 128
    penalty = jnp.sum(jnp.where(chosen, found, 0.0), axis=0, keepdims=True)
    out[0:1, :] = advantage
    out[1:2, :] = penalty


def call(kernel, out_shape, in_specs, out_specs, scratch=()):
    return pl.pallas_call(
        kernel,
        out_shape=out_shape,
        in_specs=in_specs,
        out_specs=out_specs,
        scratch_shapes=list(scratch),
        compiler_params=pltpu.CompilerParams(vmem_limit_bytes=48 * 1024 * 1024),
    )


def shards_in_place(hidden, projection, norm_gain, old_logp, ref_logp, lengths, group_of, rewards):
    n = lax.axis_size("seq")
    n_tp = lax.axis_size("tp")
    n_class = n * n_tp
    rows, cols = hidden.shape
    n_resp = lengths.shape[0]
    width = cols * n_tp
    slots = rows // n_class
    row = rows // 128
    tokens = TOK_DEV * n
    packed_rows = -(-((tokens + (n_class - 1) * n) // n_class) // 16) * 16
    shape = jax.ShapeDtypeStruct

    sibling = swap(hidden, "tp", 1)
    info = call(info_kernel, shape((8, 128), F32), [SMEM] * 3 + [VMEM] * 2, VMEM)(
        lengths, group_of, rewards, old_logp.reshape(row, 128), ref_logp.reshape(row, 128)
    )
    dealt = call(
        functools.partial(spread_kernel, n, n_tp),
        [shape((slots, width), BF16)] * n,
        [SMEM, VMEM, VMEM],
        [VMEM] * n,
    )(lengths, hidden, sibling)
    whole = [dealt[0]] + [swap(dealt[k], "sec", k) for k in range(1, n)]
    infos = [info] + [swap(info, "seq", m) for m in range(1, n)]
    normed = call(
        functools.partial(norm_kernel, n),
        [shape((slots, width), BF16)] * n,
        [VMEM] * (n + 1),
        [VMEM] * n,
        [pltpu.VMEM((n, slots, width), BF16)],
    )(norm_gain.reshape(1, D), *whole)
    moved = [normed[0]] + [swap(normed[m], "seq", m) for m in range(1, n)]
    packed = call(
        functools.partial(pack_kernel, n, n_class, n_resp, row),
        shape((packed_rows, width), BF16),
        [SMEM] * n + [VMEM] * n,
        VMEM,
        [pltpu.VMEM((n * slots, width), BF16), pltpu.SMEM((n,), I32)],
    )(*infos, *moved)
    mine = lax.all_gather(packed, "sec", axis=0, tiled=True)
    other = swap(mine, "tp", 1)
    partial = call(
        functools.partial(mix_kernel, n, n_class, n_resp, row),
        [shape((TOK_DEV, cols), F32)] + [shape((TOK_DEV, cols), BF16)] * (n - 1),
        [SMEM] * (n + 1) + [VMEM] * 4,
        [VMEM] * n,
        [pltpu.SMEM((n,), I32)],
    )(*infos, lengths, hidden, projection, mine, other)
    arrived = [swap(partial[m], "seq", m) for m in range(n - 1, 0, -1)]
    terms = call(
        functools.partial(terms_kernel, n, n_resp, row),
        shape((2, TOK_DEV), F32),
        [VMEM] * n,
        VMEM,
        [pltpu.SMEM((n, 3 * n_resp), I32), pltpu.VMEM((n * row, 128), F32)],
    )(*infos)
    states = partial[0]
    for part in arrived:
        states = states + part.astype(F32)
    return states.astype(BF16), terms.astype(BF16).T


def refine(input_rows, projection, norm_gain):
    widened = input_rows.astype(jnp.float32)
    full_rows = lax.all_gather(input_rows, ("sec", "tp"), axis=1, tiled=True).astype(jnp.float32)
    squares = jnp.sum(full_rows * full_rows, axis=1, keepdims=True)
    normed = (full_rows * lax.rsqrt(squares / D + 1e-06) * norm_gain).astype(jnp.bfloat16)
    mixing = jnp.dot(
        normed,
        lax.all_gather(projection, "seq", axis=0, tiled=True),
        preferred_element_type=jnp.float32,
    )
    return (widened + mixing).astype(jnp.bfloat16)


def deliver(
    input_rows, token_terms, lengths, first_index, own_total, starts, seq_index, tile_rows, n_seq
):
    slot_count = input_rows.shape[0]
    slot_index = jnp.arange(slot_count, dtype=jnp.int32)
    offset = jnp.mod(slot_index - first_index, slot_count)
    filled = offset < own_total
    finish = jnp.cumsum(lengths)
    response = jnp.sum((finish[None, :] <= offset[:, None]).astype(jnp.int32), axis=1)
    response = jnp.minimum(response, lengths.shape[0] - 1)
    opening = jnp.take(finish - lengths, response)
    source = jnp.where(filled, response * LMAX + offset - opening, 0)
    send_rows = jnp.where(
        filled[:, None], jnp.take(input_rows, source, axis=0), jnp.zeros((), input_rows.dtype)
    )
    send_terms = jnp.where(
        filled[:, None], jnp.take(token_terms, source, axis=0), jnp.zeros((), token_terms.dtype)
    )
    arrived, arrived_terms = (
        lax.all_to_all(
            send_rows.reshape(n_seq, tile_rows, -1), "seq", split_axis=0, concat_axis=0, tiled=True
        ),
        lax.all_to_all(
            send_terms.reshape(n_seq, tile_rows, 2), "seq", split_axis=0, concat_axis=0, tiled=True
        ),
    )
    learner_row = jnp.arange(TOK_DEV, dtype=jnp.int32)
    packed = learner_row // tile_rows * slot_count + seq_index * tile_rows + learner_row % tile_rows
    sender = jnp.sum((starts[None, :] <= packed[:, None]).astype(jnp.int32), axis=1) - 1
    pick_index = sender * tile_rows + learner_row % tile_rows
    states = jnp.take(arrived.reshape(slot_count, -1), pick_index, axis=0)
    moved_terms = jnp.take(arrived_terms.reshape(slot_count, 2), pick_index, axis=0)
    return (states, moved_terms)


def shards(hidden, projection, norm_gain, old_logp, ref_logp, lengths, group_of, rewards):
    n_seq = lax.axis_size("seq")
    seq_index = lax.axis_index("seq")
    tile_rows = SLOTS // n_seq
    group_count = RESP_DEV * n_seq // GROUP
    member_table = (group_of[:, None] == jnp.arange(group_count, dtype=jnp.int32)[None, :]).astype(
        jnp.float32
    )
    reward_value = rewards.astype(jnp.float32)
    partial_value = jnp.stack(
        [
            jnp.dot(reward_value, member_table, precision=lax.Precision.HIGHEST),
            jnp.dot(reward_value * reward_value, member_table, precision=lax.Precision.HIGHEST),
        ]
    )
    own_total = jnp.sum(lengths)
    group_sums = lax.psum(partial_value, "seq")
    counts = lax.all_gather(jnp.reshape(own_total, (1,)), "seq", axis=0, tiled=True)
    group_mean = group_sums[0] / GROUP
    spread = jnp.maximum(jnp.sqrt(group_sums[1] / GROUP - group_mean * group_mean), 1.0)
    advantage = (
        reward_value - jnp.dot(member_table, group_mean, precision=lax.Precision.HIGHEST)
    ) / jnp.dot(member_table, spread, precision=lax.Precision.HIGHEST)
    log_ratio = ref_logp - old_logp
    penalty = jnp.exp(log_ratio) - log_ratio - 1.0
    token_terms = jnp.stack([jnp.repeat(advantage, LMAX), penalty], axis=1).astype(jnp.bfloat16)
    starts = jnp.cumsum(counts) - counts
    first_index = jnp.take(starts, seq_index)
    refined = refine(hidden, projection, norm_gain)
    return deliver(
        refined, token_terms, lengths, first_index, own_total, starts, seq_index, tile_rows, n_seq
    )


def solution(mesh):
    in_specs = (
        P("seq", ("sec", "tp")),
        P("seq", ("sec", "tp")),
        P(),
        P("seq"),
        P("seq"),
        P("seq"),
        P("seq"),
        P("seq"),
    )
    out_specs = (P("seq", ("sec", "tp")), P("seq", None))
    body = shards_in_place if mesh.shape["sec"] == mesh.shape["seq"] else shards
    return jax.shard_map(body, mesh=mesh, in_specs=in_specs, out_specs=out_specs, check_vma=False)
```

```python
import functools

import jax
import jax.numpy as jnp
from jax import lax
from jax.experimental import pallas as pl
from jax.experimental.pallas import tpu as pltpu
from jax.sharding import PartitionSpec as P

D = 5120
TOK_DEV = 128
RESP_DEV = 4
GROUP = 8
LMAX = 64
TILE = 64
SLOTS = 256
EPS = 1e-06
BF16 = jnp.bfloat16
F32 = jnp.float32
I32 = jnp.int32
LANES = 128
INFO = 16

VMEM = pl.BlockSpec(memory_space=pltpu.VMEM)
SMEM = pl.BlockSpec(memory_space=pltpu.SMEM)
ANY = pl.BlockSpec(memory_space=pl.ANY)


def iota(shape, dim):
    return lax.broadcasted_iota(I32, shape, dim)


def bits(n):
    return n.bit_length() - 1


def div(x, n):
    return lax.shift_right_arithmetic(x, jnp.full(jnp.shape(x), bits(n), I32))


def mod(x, n):
    return x & (n - 1)


def swap(x, axis, k):
    n = lax.axis_size(axis)
    return lax.ppermute(x, axis, [(i, i ^ k) for i in range(n)])


def early_kernel(n_sec, n_tp, hidden, lengths, group_of, rewards, old_logp, ref_logp, gain, *refs):
    pick, mine, info, gain_out = refs[:4]
    rows_in, length, group, reward, old, ref, sems = refs[4:]
    copies = []
    for i, (src, dst) in enumerate(
        (
            (lengths, length),
            (hidden, rows_in),
            (old_logp, old),
            (ref_logp, ref),
            (group_of, group),
            (rewards, reward),
            (gain, gain_out),
        )
    ):
        copies.append(pltpu.make_async_copy(src, dst, sems.at[i]))
        copies[-1].start()
    a = lax.axis_index("sec")
    t = lax.axis_index("tp")
    n_class = n_sec * n_tp
    rows = rows_in.shape[0]
    n_resp = length.shape[0]
    total = pick.shape[0]
    slots = total // n_sec
    place = iota((total, rows), 0)
    index = mod(place, slots) * n_class + (div(place, slots) ^ a) * n_tp + t
    copies[0].wait()
    source, finish = index, 0
    for r in range(n_resp):
        finish = finish + length[r]
        source = source + jnp.where(index >= finish, LMAX - length[r], 0)
    source = jnp.where(index < finish, source, -1)
    chosen = (iota((total, rows), 1) == source).astype(BF16)
    pick[...] = chosen
    for copy in copies[1:]:
        copy.wait()
    mine[...] = jnp.dot(chosen, rows_in[...], preferred_element_type=F32).astype(BF16)
    log_ratio = ref[...] - old[...]
    penalty = jnp.exp(log_ratio) - log_ratio - 1.0
    lane = iota((1, LANES), 1)
    words = jnp.zeros((1, LANES), F32)
    for r in range(n_resp):
        for i, held in enumerate((length, group, reward)):
            words = jnp.where(lane == i * n_resp + r, held[r].astype(F32), words)
    n_pen = penalty.shape[0]
    filler = jnp.zeros((info.shape[0] - n_pen - 1, LANES), F32)
    info[...] = jnp.concatenate([penalty, words, filler], axis=0).astype(BF16)


def spread_kernel(n_tp, pick, mine, sibling, *outs):
    t = lax.axis_index("tp")
    slots, width = outs[0].shape[0], mine.shape[1]
    own = mine[...].astype(F32)
    other = jnp.dot(pick[...], sibling[...], preferred_element_type=F32)
    first = jnp.where(t == 0, own, other).astype(BF16)
    second = jnp.where(t == 0, other, own).astype(BF16)
    for k, out in enumerate(outs):
        out[:, 0:width] = first[k * slots : (k + 1) * slots]
        out[:, width : 2 * width] = second[k * slots : (k + 1) * slots]


def norm_kernel(n, gain, info, *refs):
    inputs, outs, held = refs[:n], refs[n : 2 * n], refs[2 * n]
    a = lax.axis_index("sec")
    s = lax.axis_index("seq")
    slots, width = inputs[0].shape
    squares = 0.0
    for ref in inputs:
        x = ref[...].astype(F32)
        squares = squares + jnp.sum(x * x, axis=1, keepdims=True)
    scale = lax.rsqrt(squares / D + EPS)
    for k, ref in enumerate(inputs):
        start = pl.multiple_of((a ^ k) * width, LANES)
        held[k] = (ref[...].astype(F32) * scale * gain[:, pl.ds(start, width)]).astype(BF16)
    beside = jnp.concatenate([info[...]] * (slots // info.shape[0]), axis=0)
    for m, out in enumerate(outs):
        out[:, 0:width] = held[a ^ s ^ m]
        out[:, width : width + LANES] = beside


def info_of(ref, width):
    return ref[0:INFO, width : width + LANES].astype(F32)


def word_sum(block, row, first, last):
    lane = iota(block.shape, 1)
    inside = (iota(block.shape, 0) == row) & (lane >= first) & (lane < last)
    return jnp.sum(jnp.where(inside, block, 0.0)).astype(I32)


def put_counts(moved, width, row, n_resp, counts):
    s = lax.axis_index("seq")
    for m, ref in enumerate(moved):
        counts[s ^ m] = word_sum(info_of(ref, width), row, 0, n_resp)


def class_rows(x, c, n_class):
    return div(x - c + n_class - 1, n_class)


def list_place(counts, n, n_class, tok, s, c, seq_of, position, packed):
    span = tok * n // 4
    edges = []
    for j in range(5):
        edge, start = 0, 0
        for b in range(n):
            edge = edge + class_rows(jnp.clip(j * span - start, 0, counts[b]), c, n_class)
            start = start + counts[b]
        edges.append(edge)
    size = [edges[j + 1] - edges[j] for j in range(4)]
    high = div(s, n // 2)
    far_first = jnp.where(high == 0, size[1], size[0])
    far_rows = jnp.where(high == 0, size[1] + size[3], size[0] + size[2])
    near_first = jnp.where(high == 0, size[0], size[1])
    prefix = 0
    before = jnp.zeros_like(position)
    for b in range(n):
        before = jnp.where(seq_of == b, prefix, before)
        prefix = prefix + class_rows(counts[b], c, n_class)
    group = div(packed, span)
    opening = jnp.where(group == 0, edges[0], jnp.where(group == 1, edges[1], jnp.where(group == 2, edges[2], edges[3])))
    within = before + position - opening
    later = group >= 2
    far = mod(group, 2) != high
    far_place = within + jnp.where(later, far_first, 0)
    near_place = far_rows + within + jnp.where(later, near_first, 0)
    return jnp.where(far, far_place, near_place)


def pack_kernel(n, n_class, n_resp, tok, row, *refs):
    moved, first, second, held, counts = refs[:n], refs[n], refs[n + 1], refs[n + 2], refs[n + 3]
    s = lax.axis_index("seq")
    c = lax.axis_index("sec") * lax.axis_size("tp") + lax.axis_index("tp")
    slots, width = moved[0].shape[0], first.shape[1]
    put_counts(moved, width, row, n_resp, counts)
    lane = iota((1, n * slots), 1)
    seq_of = div(lane, slots) ^ s
    q = mod(lane, slots)
    live = jnp.zeros(lane.shape, jnp.bool_)
    start = jnp.zeros(lane.shape, I32)
    total = 0
    for b in range(n):
        live = live | ((seq_of == b) & (q < class_rows(counts[b], c, n_class)))
        start = jnp.where(seq_of == b, total, start)
        total = total + counts[b]
    packed = start + q * n_class + c
    place = list_place(counts, n, n_class, tok, s, c, seq_of, q, packed)
    place = jnp.where(live, place, -1)
    for m, ref in enumerate(moved):
        held[m * slots : (m + 1) * slots, :] = ref[:, 0:width]
    r1, r2 = first.shape[0], second.shape[0]
    pick = (iota((r1 + r2, n * slots), 0) == place).astype(BF16)
    out = jnp.dot(pick, held[...], preferred_element_type=F32).astype(BF16)
    first[...] = out[0:r1]
    second[...] = out[r1 : r1 + r2]


def upright(x):
    return jnp.transpose(jnp.broadcast_to(x.astype(F32), (LANES, x.shape[1]))).astype(I32)


def one_hot(column, out):
    for j in range(out.shape[1] // LANES):
        out[:, j * LANES : (j + 1) * LANES] = (iota(column.shape, 1) + j * LANES == column).astype(BF16)


def index_kernel(n, n_class, n_resp, tok, row, r1, r2, *refs):
    moved, hidden = refs[:n], refs[n]
    pick_far, pick_near, rest_far, rest_near, counts, lens, own = refs[n + 1 :]
    a = lax.axis_index("sec")
    s = lax.axis_index("seq")
    t = lax.axis_index("tp")
    n_tp = lax.axis_size("tp")
    width = moved[0].shape[1] - LANES
    put_counts(moved, width, row, n_resp, counts)
    block = info_of(moved[0], width)
    for r in range(n_resp):
        lens[r] = word_sum(block, row, r, r + 1)
    half = n // 2 * tok
    for far, pick, rest in ((True, pick_far, rest_far), (False, pick_near, rest_near)):
        lane = iota((1, half), 1)
        w = mod(lane, tok)
        shard = (div(lane, tok) + (n // 2 if far else 0)) ^ s
        packed = div(w, TILE) * (TILE * n) + shard * TILE + mod(w, TILE)
        seq_of = jnp.zeros(lane.shape, I32)
        start = jnp.zeros(lane.shape, I32)
        finish = 0
        for b in range(n):
            finish = finish + counts[b]
            passed = packed >= finish
            seq_of = seq_of + passed.astype(I32)
            start = jnp.where(passed, finish, start)
        index = packed - start
        c = mod(index, n_class)
        place = list_place(counts, n, n_class, tok, s, c, seq_of, div(index, n_class), packed)
        side = (mod(c, n_tp) ^ t) * n + (div(c, n_tp) ^ a)
        column = side * r1 + place
        if not far:
            column = jnp.where(place < r1, column, n_class * r1 + side * r2 + place - r1)
        one_hot(upright(column), pick)
        source, ends = index, 0
        for r in range(n_resp):
            ends = ends + lens[r]
            source = source + jnp.where(index >= ends, LMAX - lens[r], 0)
        one_hot(upright(jnp.where(seq_of == s, source, -1)), own)
        rest[...] = jnp.dot(own[...], hidden[...], preferred_element_type=F32)


def mix_kernel(n_lists, sizes, pick, rest, projection, *refs):
    pieces, outs, held = refs[:n_lists], refs[n_lists:-1], refs[-1]
    offset = 0
    for piece in pieces:
        size = piece.shape[0]
        held[offset : offset + size, :] = piece[...]
        offset += size
    tokens = jnp.dot(pick[...], held[...], preferred_element_type=F32).astype(BF16)
    total = jnp.dot(tokens, projection[...], preferred_element_type=F32) + rest[...]
    tok = outs[0].shape[0]
    for m, out in enumerate(outs):
        out[...] = total[m * tok : (m + 1) * tok].astype(out.dtype)


def terms_kernel(n, n_resp, row, *refs):
    moved, out, words, table = refs[:n], refs[n], refs[n + 1], refs[n + 2]
    s = lax.axis_index("seq")
    width = moved[0].shape[1] - LANES
    tok = out.shape[1]
    group_count = n * n_resp // GROUP
    for m, ref in enumerate(moved):
        block = info_of(ref, width)
        table[pl.ds((s ^ m) * INFO, INFO), :] = block
        for r in range(3 * n_resp):
            words[s ^ m, r] = word_sum(block, row, r, r + 1)
    w = iota((1, tok), 1)
    packed = div(w, TILE) * (TILE * n) + s * TILE + mod(w, TILE)
    source, finish = packed, 0
    reward = jnp.zeros((1, tok), F32)
    group = jnp.zeros((1, tok), I32)
    total = [0] * group_count
    square = [0] * group_count
    for b in range(n):
        for r in range(n_resp):
            length, number, gain = words[b, r], words[b, n_resp + r], words[b, 2 * n_resp + r]
            within = packed >= finish
            reward = jnp.where(within, gain.astype(F32), reward)
            group = jnp.where(within, number, group)
            finish = finish + length
            source = source + jnp.where(packed >= finish, LMAX - length, 0)
            for g in range(group_count):
                total[g] = total[g] + jnp.where(number == g, gain, 0)
                square[g] = square[g] + jnp.where(number == g, gain * gain, 0)
    total_of = jnp.zeros((1, tok), F32)
    square_of = jnp.zeros((1, tok), F32)
    for g in range(group_count):
        total_of = jnp.where(group == g, total[g].astype(F32), total_of)
        square_of = jnp.where(group == g, square[g].astype(F32), square_of)
    mean = total_of / GROUP
    spread = jnp.maximum(jnp.sqrt(square_of / GROUP - mean * mean), 1.0)
    advantage = (reward - mean) / spread
    pick = (iota((LANES, tok), 0) == mod(source, LANES)).astype(BF16)
    found = jnp.dot(table[...].astype(BF16), pick, preferred_element_type=F32)
    line = div(source, LANES)
    chosen = iota(found.shape, 0) == div(line, row) * INFO + mod(line, row)
    penalty = jnp.sum(jnp.where(chosen, found, 0.0), axis=0, keepdims=True)
    out[0:1, :] = advantage
    out[1:2, :] = penalty


def call(kernel, out_shape, in_specs, out_specs, scratch=()):
    return pl.pallas_call(
        kernel,
        out_shape=out_shape,
        in_specs=in_specs,
        out_specs=out_specs,
        scratch_shapes=list(scratch),
        compiler_params=pltpu.CompilerParams(vmem_limit_bytes=48 * 1024 * 1024),
    )


def shards_in_place(hidden, projection, norm_gain, old_logp, ref_logp, lengths, group_of, rewards):
    n = lax.axis_size("seq")
    n_tp = lax.axis_size("tp")
    n_class = n * n_tp
    rows, cols = hidden.shape
    n_resp = lengths.shape[0]
    width = cols * n_tp
    slots = rows // n_class
    row = rows // LANES
    tok = TOK_DEV
    tokens = tok * n
    up16 = lambda x: -(-x // 16) * 16
    far_rows = up16((tokens // 2 + (n_class - 1) * (n + 1)) // n_class)
    all_rows = up16((tokens + (n_class - 1) * n) // n_class)
    r1, r2 = far_rows, max(16, all_rows - far_rows)
    shape = jax.ShapeDtypeStruct
    info_like = shape((slots, width + LANES), BF16)

    sibling = swap(hidden, "tp", 1)
    pick, mine, info, gain = call(
        functools.partial(early_kernel, n, n_tp),
        [
            shape((rows // n_tp, rows), BF16),
            shape((rows // n_tp, cols), BF16),
            shape((INFO, LANES), BF16),
            shape((1, D), F32),
        ],
        [ANY] * 7,
        [VMEM] * 4,
        [
            pltpu.VMEM((rows, cols), BF16),
            pltpu.SMEM((n_resp,), I32),
            pltpu.SMEM((n_resp,), I32),
            pltpu.SMEM((n_resp,), I32),
            pltpu.VMEM((row, LANES), F32),
            pltpu.VMEM((row, LANES), F32),
            pltpu.SemaphoreType.DMA((7,)),
        ],
    )(
        hidden,
        lengths,
        group_of,
        rewards,
        old_logp.reshape(row, LANES),
        ref_logp.reshape(row, LANES),
        norm_gain.reshape(1, D),
    )
    dealt = call(
        functools.partial(spread_kernel, n_tp), [shape((slots, width), BF16)] * n, [VMEM] * 3, [VMEM] * n
    )(pick, mine, sibling)
    whole = [dealt[0]] + [swap(dealt[k], "sec", k) for k in range(1, n)]
    normed = call(
        functools.partial(norm_kernel, n),
        [info_like] * n,
        [VMEM] * (n + 2),
        [VMEM] * n,
        [pltpu.VMEM((n, slots, width), BF16)],
    )(gain, info, *whole)
    moved = [normed[0]] + [swap(normed[m], "seq", m) for m in range(n - 1, 0, -1)][::-1]
    lists = call(
        functools.partial(pack_kernel, n, n_class, n_resp, tok, row),
        [shape((r1, width), BF16), shape((r2, width), BF16)],
        [VMEM] * n,
        [VMEM] * 2,
        [pltpu.VMEM((n * slots, width), BF16), pltpu.SMEM((n,), I32)],
    )(*moved)
    half = n // 2 * tok
    pick_far, pick_near, rest_far, rest_near = call(
        functools.partial(index_kernel, n, n_class, n_resp, tok, row, r1, r2),
        [
            shape((half, n_class * r1), BF16),
            shape((half, n_class * (r1 + r2)), BF16),
            shape((half, cols), F32),
            shape((half, cols), F32),
        ],
        [VMEM] * (n + 1),
        [VMEM] * 4,
        [pltpu.SMEM((n,), I32), pltpu.SMEM((n_resp,), I32), pltpu.VMEM((half, rows), BF16)],
    )(*moved, hidden)
    terms = call(
        functools.partial(terms_kernel, n, n_resp, row),
        shape((2, tok), F32),
        [VMEM] * n,
        VMEM,
        [pltpu.SMEM((n, 3 * n_resp), I32), pltpu.VMEM((n * INFO, LANES), F32)],
    )(*moved)
    pieces = []
    for part in lists:
        same = [part] + [swap(part, "sec", k) for k in range(1, n)]
        pieces.append(same + [swap(x, "tp", 1) for x in same])
    far = call(
        functools.partial(mix_kernel, n_class, None),
        [shape((tok, cols), BF16)] * (n // 2),
        [VMEM] * (n_class + 3),
        [VMEM] * (n // 2),
        [pltpu.VMEM((n_class * r1, width), BF16)],
    )(pick_far, rest_far, projection, *pieces[0])
    near = call(
        functools.partial(mix_kernel, 2 * n_class, None),
        [shape((tok, cols), F32)] + [shape((tok, cols), BF16)] * (n // 2 - 1),
        [VMEM] * (2 * n_class + 3),
        [VMEM] * (n // 2),
        [pltpu.VMEM((n_class * (r1 + r2), width), BF16)],
    )(pick_near, rest_near, projection, *pieces[0], *pieces[1])
    partial = [*near, *far]
    arrived = [swap(partial[m], "seq", m) for m in range(n - 1, 0, -1)]
    states = partial[0]
    for part in arrived:
        states = states + part.astype(F32)
    return states.astype(BF16), terms.astype(BF16).T


def refine(input_rows, projection, norm_gain):
    widened = input_rows.astype(jnp.float32)
    full_rows = lax.all_gather(input_rows, ("sec", "tp"), axis=1, tiled=True).astype(jnp.float32)
    squares = jnp.sum(full_rows * full_rows, axis=1, keepdims=True)
    normed = (full_rows * lax.rsqrt(squares / D + 1e-06) * norm_gain).astype(jnp.bfloat16)
    mixing = jnp.dot(
        normed,
        lax.all_gather(projection, "seq", axis=0, tiled=True),
        preferred_element_type=jnp.float32,
    )
    return (widened + mixing).astype(jnp.bfloat16)


def deliver(
    input_rows, token_terms, lengths, first_index, own_total, starts, seq_index, tile_rows, n_seq
):
    slot_count = input_rows.shape[0]
    slot_index = jnp.arange(slot_count, dtype=jnp.int32)
    offset = jnp.mod(slot_index - first_index, slot_count)
    filled = offset < own_total
    finish = jnp.cumsum(lengths)
    response = jnp.sum((finish[None, :] <= offset[:, None]).astype(jnp.int32), axis=1)
    response = jnp.minimum(response, lengths.shape[0] - 1)
    opening = jnp.take(finish - lengths, response)
    source = jnp.where(filled, response * LMAX + offset - opening, 0)
    send_rows = jnp.where(
        filled[:, None], jnp.take(input_rows, source, axis=0), jnp.zeros((), input_rows.dtype)
    )
    send_terms = jnp.where(
        filled[:, None], jnp.take(token_terms, source, axis=0), jnp.zeros((), token_terms.dtype)
    )
    arrived, arrived_terms = (
        lax.all_to_all(
            send_rows.reshape(n_seq, tile_rows, -1), "seq", split_axis=0, concat_axis=0, tiled=True
        ),
        lax.all_to_all(
            send_terms.reshape(n_seq, tile_rows, 2), "seq", split_axis=0, concat_axis=0, tiled=True
        ),
    )
    learner_row = jnp.arange(TOK_DEV, dtype=jnp.int32)
    packed = learner_row // tile_rows * slot_count + seq_index * tile_rows + learner_row % tile_rows
    sender = jnp.sum((starts[None, :] <= packed[:, None]).astype(jnp.int32), axis=1) - 1
    pick_index = sender * tile_rows + learner_row % tile_rows
    states = jnp.take(arrived.reshape(slot_count, -1), pick_index, axis=0)
    moved_terms = jnp.take(arrived_terms.reshape(slot_count, 2), pick_index, axis=0)
    return (states, moved_terms)


def shards(hidden, projection, norm_gain, old_logp, ref_logp, lengths, group_of, rewards):
    n_seq = lax.axis_size("seq")
    seq_index = lax.axis_index("seq")
    tile_rows = SLOTS // n_seq
    group_count = RESP_DEV * n_seq // GROUP
    member_table = (group_of[:, None] == jnp.arange(group_count, dtype=jnp.int32)[None, :]).astype(
        jnp.float32
    )
    reward_value = rewards.astype(jnp.float32)
    partial_value = jnp.stack(
        [
            jnp.dot(reward_value, member_table, precision=lax.Precision.HIGHEST),
            jnp.dot(reward_value * reward_value, member_table, precision=lax.Precision.HIGHEST),
        ]
    )
    own_total = jnp.sum(lengths)
    group_sums = lax.psum(partial_value, "seq")
    counts = lax.all_gather(jnp.reshape(own_total, (1,)), "seq", axis=0, tiled=True)
    group_mean = group_sums[0] / GROUP
    spread = jnp.maximum(jnp.sqrt(group_sums[1] / GROUP - group_mean * group_mean), 1.0)
    advantage = (
        reward_value - jnp.dot(member_table, group_mean, precision=lax.Precision.HIGHEST)
    ) / jnp.dot(member_table, spread, precision=lax.Precision.HIGHEST)
    log_ratio = ref_logp - old_logp
    penalty = jnp.exp(log_ratio) - log_ratio - 1.0
    token_terms = jnp.stack([jnp.repeat(advantage, LMAX), penalty], axis=1).astype(jnp.bfloat16)
    starts = jnp.cumsum(counts) - counts
    first_index = jnp.take(starts, seq_index)
    refined = refine(hidden, projection, norm_gain)
    return deliver(
        refined, token_terms, lengths, first_index, own_total, starts, seq_index, tile_rows, n_seq
    )


def solution(mesh):
    in_specs = (
        P("seq", ("sec", "tp")),
        P("seq", ("sec", "tp")),
        P(),
        P("seq"),
        P("seq"),
        P("seq"),
        P("seq"),
        P("seq"),
    )
    out_specs = (P("seq", ("sec", "tp")), P("seq", None))
    n = mesh.shape["seq"]
    in_place = mesh.shape["sec"] == n and n >= 4 and n & (n - 1) == 0
    body = shards_in_place if in_place else shards
    return jax.shard_map(body, mesh=mesh, in_specs=in_specs, out_specs=out_specs, check_vma=False)
```

```python
import functools

import jax
import jax.numpy as jnp
from jax import lax
from jax.experimental import pallas as pl
from jax.experimental.pallas import tpu as pltpu
from jax.sharding import PartitionSpec as P

D = 5120
TOK_DEV = 128
RESP_DEV = 4
GROUP = 8
LMAX = 64
TILE = 64
SLOTS = 256
EPS = 1e-06
BF16 = jnp.bfloat16
F32 = jnp.float32
I32 = jnp.int32
LANES = 128
INFO = 16

VMEM = pl.BlockSpec(memory_space=pltpu.VMEM)
SMEM = pl.BlockSpec(memory_space=pltpu.SMEM)
HBM = pl.BlockSpec(memory_space=pltpu.HBM)


def iota(shape, dim):
    return lax.broadcasted_iota(I32, shape, dim)


def bits(n):
    return n.bit_length() - 1


def div(x, n):
    return lax.shift_right_arithmetic(x, jnp.full(jnp.shape(x), bits(n), I32))


def mod(x, n):
    return x & (n - 1)


def swap(x, axis, k):
    n = lax.axis_size(axis)
    return lax.ppermute(x, axis, [(i, i ^ k) for i in range(n)])


def early_kernel(n_sec, n_tp, hidden, lengths, group_of, rewards, old_logp, ref_logp, gain, *refs):
    pick, mine, info, gain_out = refs[:4]
    rows_in, length, group, reward, old, ref, sems = refs[4:]
    copies = []
    for i, (src, dst) in enumerate(
        (
            (lengths, length),
            (hidden, rows_in),
            (old_logp, old),
            (ref_logp, ref),
            (group_of, group),
            (rewards, reward),
            (gain, gain_out),
        )
    ):
        copies.append(pltpu.make_async_copy(src, dst, sems.at[i]))
        copies[-1].start()
    a = lax.axis_index("sec")
    t = lax.axis_index("tp")
    n_class = n_sec * n_tp
    rows = rows_in.shape[0]
    n_resp = length.shape[0]
    total = pick.shape[0]
    slots = total // n_sec
    place = iota((total, rows), 0)
    index = mod(place, slots) * n_class + (div(place, slots) ^ a) * n_tp + t
    copies[0].wait()
    source, finish = index, 0
    for r in range(n_resp):
        finish = finish + length[r]
        source = source + jnp.where(index >= finish, LMAX - length[r], 0)
    source = jnp.where(index < finish, source, -1)
    chosen = (iota((total, rows), 1) == source).astype(BF16)
    pick[...] = chosen
    for copy in copies[1:]:
        copy.wait()
    mine[...] = jnp.dot(chosen, rows_in[...], preferred_element_type=F32).astype(BF16)
    log_ratio = ref[...] - old[...]
    penalty = jnp.exp(log_ratio) - log_ratio - 1.0
    lane = iota((1, LANES), 1)
    words = jnp.zeros((1, LANES), F32)
    for r in range(n_resp):
        for i, held in enumerate((length, group, reward)):
            words = jnp.where(lane == i * n_resp + r, held[r].astype(F32), words)
    n_pen = penalty.shape[0]
    filler = jnp.zeros((info.shape[0] - n_pen - 1, LANES), F32)
    info[...] = jnp.concatenate([penalty, words, filler], axis=0).astype(BF16)


def spread_kernel(n_tp, pick, mine, sibling, *outs):
    t = lax.axis_index("tp")
    slots, width = outs[0].shape[0], mine.shape[1]
    own = mine[...].astype(F32)
    other = jnp.dot(pick[...], sibling[...], preferred_element_type=F32)
    first = jnp.where(t == 0, own, other).astype(BF16)
    second = jnp.where(t == 0, other, own).astype(BF16)
    for k, out in enumerate(outs):
        out[:, 0:width] = first[k * slots : (k + 1) * slots]
        out[:, width : 2 * width] = second[k * slots : (k + 1) * slots]


def norm_kernel(n, gain, info, *refs):
    inputs, outs, held = refs[n - 1 :: -1], refs[n : 2 * n], refs[2 * n]
    a = lax.axis_index("sec")
    s = lax.axis_index("seq")
    slots, width = inputs[0].shape
    squares = 0.0
    for ref in inputs:
        x = ref[...].astype(F32)
        squares = squares + jnp.sum(x * x, axis=1, keepdims=True)
    scale = lax.rsqrt(squares / D + EPS)
    for k, ref in enumerate(inputs):
        start = pl.multiple_of((a ^ k) * width, LANES)
        held[k] = (ref[...].astype(F32) * scale * gain[:, pl.ds(start, width)]).astype(BF16)
    beside = jnp.concatenate([info[...]] * (slots // info.shape[0]), axis=0)
    for m, out in enumerate(outs):
        out[:, 0:width] = held[a ^ s ^ m]
        out[:, width : width + LANES] = beside


def info_of(ref, width):
    return ref[0:INFO, width : width + LANES].astype(F32)


def word_sum(block, row, first, last):
    lane = iota(block.shape, 1)
    inside = (iota(block.shape, 0) == row) & (lane >= first) & (lane < last)
    return jnp.sum(jnp.where(inside, block, 0.0)).astype(I32)


def put_counts(moved, width, row, n_resp, counts):
    s = lax.axis_index("seq")
    for m, ref in enumerate(moved):
        counts[s ^ m] = word_sum(info_of(ref, width), row, 0, n_resp)


def class_rows(x, c, n_class):
    return div(x - c + n_class - 1, n_class)


def list_place(counts, n, n_class, tok, s, c, seq_of, position, packed):
    span = tok * n // 4
    edges = []
    for j in range(5):
        edge, start = 0, 0
        for b in range(n):
            edge = edge + class_rows(jnp.clip(j * span - start, 0, counts[b]), c, n_class)
            start = start + counts[b]
        edges.append(edge)
    size = [edges[j + 1] - edges[j] for j in range(4)]
    high = div(s, n // 2)
    far_first = jnp.where(high == 0, size[1], size[0])
    far_rows = jnp.where(high == 0, size[1] + size[3], size[0] + size[2])
    near_first = jnp.where(high == 0, size[0], size[1])
    prefix = 0
    before = jnp.zeros_like(position)
    for b in range(n):
        before = jnp.where(seq_of == b, prefix, before)
        prefix = prefix + class_rows(counts[b], c, n_class)
    group = div(packed, span)
    opening = jnp.where(group == 0, edges[0], jnp.where(group == 1, edges[1], jnp.where(group == 2, edges[2], edges[3])))
    within = before + position - opening
    later = group >= 2
    far = mod(group, 2) != high
    far_place = within + jnp.where(later, far_first, 0)
    near_place = far_rows + within + jnp.where(later, near_first, 0)
    return jnp.where(far, far_place, near_place)


def pack_kernel(n, n_class, n_resp, tok, row, *refs):
    moved, (first, second, both, held, counts) = refs[n - 1 :: -1], refs[n:]
    s = lax.axis_index("seq")
    c = lax.axis_index("sec") * lax.axis_size("tp") + lax.axis_index("tp")
    slots, width = moved[0].shape[0], first.shape[1]
    put_counts(moved, width, row, n_resp, counts)
    lane = iota((1, n * slots), 1)
    seq_of = div(lane, slots) ^ s
    q = mod(lane, slots)
    live = jnp.zeros(lane.shape, jnp.bool_)
    start = jnp.zeros(lane.shape, I32)
    total = 0
    for b in range(n):
        live = live | ((seq_of == b) & (q < class_rows(counts[b], c, n_class)))
        start = jnp.where(seq_of == b, total, start)
        total = total + counts[b]
    packed = start + q * n_class + c
    place = list_place(counts, n, n_class, tok, s, c, seq_of, q, packed)
    place = jnp.where(live, place, -1)
    for m, ref in enumerate(moved):
        held[m * slots : (m + 1) * slots, :] = ref[:, 0:width]
    r1, r2 = first.shape[0], second.shape[0]
    pick = (iota((r1 + r2, n * slots), 0) == place).astype(BF16)
    out = jnp.dot(pick, held[...], preferred_element_type=F32).astype(BF16)
    both[...] = out
    first[...] = out[0:r1]
    second[...] = out[r1 : r1 + r2]


def upright(x):
    return jnp.transpose(jnp.broadcast_to(x.astype(F32), (LANES, x.shape[1]))).astype(I32)


def one_hot(column, out):
    for j in range(out.shape[1] // LANES):
        out[:, j * LANES : (j + 1) * LANES] = (iota(column.shape, 1) + j * LANES == column).astype(BF16)


def index_kernel(n, n_class, n_resp, tok, row, r1, r2, *refs):
    moved, hidden = refs[:n], refs[n]
    pick_far, pick_near, rest_far, rest_near, counts, lens, own = refs[n + 1 :]
    a = lax.axis_index("sec")
    s = lax.axis_index("seq")
    t = lax.axis_index("tp")
    n_tp = lax.axis_size("tp")
    width = moved[0].shape[1] - LANES
    put_counts(moved, width, row, n_resp, counts)
    block = info_of(moved[0], width)
    for r in range(n_resp):
        lens[r] = word_sum(block, row, r, r + 1)
    half = n // 2 * tok
    for far, pick, rest in ((True, pick_far, rest_far), (False, pick_near, rest_near)):
        lane = iota((1, half), 1)
        w = mod(lane, tok)
        shard = (div(lane, tok) + (n // 2 if far else 0)) ^ s
        packed = div(w, TILE) * (TILE * n) + shard * TILE + mod(w, TILE)
        seq_of = jnp.zeros(lane.shape, I32)
        start = jnp.zeros(lane.shape, I32)
        finish = 0
        for b in range(n):
            finish = finish + counts[b]
            passed = packed >= finish
            seq_of = seq_of + passed.astype(I32)
            start = jnp.where(passed, finish, start)
        index = packed - start
        c = mod(index, n_class)
        place = list_place(counts, n, n_class, tok, s, c, seq_of, div(index, n_class), packed)
        core, k = mod(c, n_tp) ^ t, div(c, n_tp) ^ a
        if far:
            column = (core * n + k) * r1 + place
        else:
            column = core * (n * r1 + r2) + k * r1 + jnp.where(k > 0, r2, 0) + place
            rest_of = n_class * r1 + n_tp * r2 + (core * (n - 1) + k - 1) * r2 + place - r1
            column = jnp.where((k > 0) & (place >= r1), rest_of, column)
        one_hot(upright(column), pick)
        source, ends = index, 0
        for r in range(n_resp):
            ends = ends + lens[r]
            source = source + jnp.where(index >= ends, LMAX - lens[r], 0)
        one_hot(upright(jnp.where(seq_of == s, source, -1)), own)
        rest[...] = jnp.dot(own[...], hidden[...], preferred_element_type=F32)


def mix_kernel(sizes, pick, rest, projection, *refs):
    pieces, outs, held = refs[: len(sizes)], refs[len(sizes) : -1], refs[-1]
    offset = 0
    for size, piece in zip(sizes, pieces, strict=True):
        held[offset : offset + size, :] = piece[0:size, :]
        offset += size
    tokens = jnp.dot(pick[...], held[...], preferred_element_type=F32).astype(BF16)
    total = jnp.dot(tokens, projection[...], preferred_element_type=F32) + rest[...]
    tok = outs[0].shape[0]
    for m, out in enumerate(outs):
        out[...] = total[m * tok : (m + 1) * tok].astype(out.dtype)


def terms_kernel(n, n_resp, row, *refs):
    moved, out, words, table = refs[:n], refs[n], refs[n + 1], refs[n + 2]
    s = lax.axis_index("seq")
    width = moved[0].shape[1] - LANES
    tok = out.shape[1]
    group_count = n * n_resp // GROUP
    for m, ref in enumerate(moved):
        block = info_of(ref, width)
        table[pl.ds((s ^ m) * INFO, INFO), :] = block
        for r in range(3 * n_resp):
            words[s ^ m, r] = word_sum(block, row, r, r + 1)
    w = iota((1, tok), 1)
    packed = div(w, TILE) * (TILE * n) + s * TILE + mod(w, TILE)
    source, finish = packed, 0
    reward = jnp.zeros((1, tok), F32)
    group = jnp.zeros((1, tok), I32)
    total = [0] * group_count
    square = [0] * group_count
    for b in range(n):
        for r in range(n_resp):
            length, number, gain = words[b, r], words[b, n_resp + r], words[b, 2 * n_resp + r]
            within = packed >= finish
            reward = jnp.where(within, gain.astype(F32), reward)
            group = jnp.where(within, number, group)
            finish = finish + length
            source = source + jnp.where(packed >= finish, LMAX - length, 0)
            for g in range(group_count):
                total[g] = total[g] + jnp.where(number == g, gain, 0)
                square[g] = square[g] + jnp.where(number == g, gain * gain, 0)
    total_of = jnp.zeros((1, tok), F32)
    square_of = jnp.zeros((1, tok), F32)
    for g in range(group_count):
        total_of = jnp.where(group == g, total[g].astype(F32), total_of)
        square_of = jnp.where(group == g, square[g].astype(F32), square_of)
    mean = total_of / GROUP
    spread = jnp.maximum(jnp.sqrt(square_of / GROUP - mean * mean), 1.0)
    advantage = (reward - mean) / spread
    pick = (iota((LANES, tok), 0) == mod(source, LANES)).astype(BF16)
    found = jnp.dot(table[...].astype(BF16), pick, preferred_element_type=F32)
    line = div(source, LANES)
    chosen = iota(found.shape, 0) == div(line, row) * INFO + mod(line, row)
    penalty = jnp.sum(jnp.where(chosen, found, 0.0), axis=0, keepdims=True)
    out[0:1, :] = advantage
    out[1:2, :] = penalty


def call(kernel, out_shape, in_specs, out_specs, scratch=()):
    return pl.pallas_call(
        kernel,
        out_shape=out_shape,
        in_specs=in_specs,
        out_specs=out_specs,
        scratch_shapes=list(scratch),
        compiler_params=pltpu.CompilerParams(vmem_limit_bytes=48 * 1024 * 1024),
    )


def shards_in_place(hidden, projection, norm_gain, old_logp, ref_logp, lengths, group_of, rewards):
    n = lax.axis_size("seq")
    n_tp = lax.axis_size("tp")
    n_class = n * n_tp
    rows, cols = hidden.shape
    n_resp = lengths.shape[0]
    width = cols * n_tp
    slots = rows // n_class
    row = rows // LANES
    tok = TOK_DEV
    tokens = tok * n
    up16 = lambda x: -(-x // 16) * 16
    far_rows = up16((tokens // 2 + (n_class - 1) * (n + 1)) // n_class)
    all_rows = up16((tokens + (n_class - 1) * n) // n_class)
    r1, r2 = far_rows, max(16, all_rows - far_rows)
    shape = jax.ShapeDtypeStruct
    info_like = shape((slots, width + LANES), BF16)

    sibling = swap(hidden, "tp", 1)
    pick, mine, info, gain = call(
        functools.partial(early_kernel, n, n_tp),
        [
            shape((rows // n_tp, rows), BF16),
            shape((rows // n_tp, cols), BF16),
            shape((INFO, LANES), BF16),
            shape((1, D), F32),
        ],
        [HBM] * 7,
        [VMEM] * 4,
        [
            pltpu.VMEM((rows, cols), BF16),
            pltpu.SMEM((n_resp,), I32),
            pltpu.SMEM((n_resp,), I32),
            pltpu.SMEM((n_resp,), I32),
            pltpu.VMEM((row, LANES), F32),
            pltpu.VMEM((row, LANES), F32),
            pltpu.SemaphoreType.DMA((7,)),
        ],
    )(
        *(
            pltpu.with_memory_space_constraint(x, pltpu.HBM)
            for x in (
                hidden,
                lengths,
                group_of,
                rewards,
                old_logp.reshape(row, LANES),
                ref_logp.reshape(row, LANES),
                norm_gain.reshape(1, D),
            )
        )
    )
    dealt = call(
        functools.partial(spread_kernel, n_tp), [shape((slots, width), BF16)] * n, [VMEM] * 3, [VMEM] * n
    )(pick, mine, sibling)
    whole = [dealt[0]] + [swap(dealt[k], "sec", k) for k in range(1, n)]
    normed = call(
        functools.partial(norm_kernel, n),
        [info_like] * n,
        [VMEM] * (n + 2),
        [VMEM] * n,
        [pltpu.VMEM((n, slots, width), BF16)],
    )(gain, info, *whole[::-1])
    moved = [normed[0]] + [swap(normed[m], "seq", m) for m in range(n - 1, 0, -1)][::-1]
    first, second, both = call(
        functools.partial(pack_kernel, n, n_class, n_resp, tok, row),
        [shape((r, width), BF16) for r in (r1, r2, r1 + r2)],
        [VMEM] * n,
        [VMEM] * 3,
        [pltpu.VMEM((n * slots, width), BF16), pltpu.SMEM((n,), I32)],
    )(*moved[::-1])
    half = n // 2 * tok
    pick_far, pick_near, rest_far, rest_near = call(
        functools.partial(index_kernel, n, n_class, n_resp, tok, row, r1, r2),
        [
            shape((half, n_class * r1), BF16),
            shape((half, n_class * (r1 + r2)), BF16),
            shape((half, cols), F32),
            shape((half, cols), F32),
        ],
        [VMEM] * (n + 1),
        [VMEM] * 4,
        [pltpu.SMEM((n,), I32), pltpu.SMEM((n_resp,), I32), pltpu.VMEM((half, rows), BF16)],
    )(*moved, hidden)
    terms = call(
        functools.partial(terms_kernel, n, n_resp, row),
        shape((2, tok), F32),
        [VMEM] * n,
        VMEM,
        [pltpu.SMEM((n, 3 * n_resp), I32), pltpu.VMEM((n * INFO, LANES), F32)],
    )(*moved)
    after = lambda x, *ys: lax.optimization_barrier((x, *ys))[0]
    other = swap(both, "tp", 1)
    far_in = [swap(first, "sec", k) for k in range(1, n)]
    far_other = [swap(x, "tp", 1) for x in far_in]
    second = after(second, *far_in)
    near_in = [swap(second, "sec", k) for k in range(1, n)]
    far = call(
        functools.partial(mix_kernel, (r1,) * n_class),
        [shape((tok, cols), BF16)] * (n // 2),
        [VMEM] * (n_class + 3),
        [VMEM] * (n // 2),
        [pltpu.VMEM((n_class * r1, width), BF16)],
    )(pick_far, rest_far, projection, both, *far_in, other, *far_other)
    near_other = [swap(after(x, *far), "tp", 1) for x in near_in]
    near = call(
        functools.partial(mix_kernel, (r1 + r2, *(r1,) * (n - 1)) * 2 + (r2,) * (2 * n - 2)),
        [shape((tok, cols), F32)] + [shape((tok, cols), BF16)] * (n // 2 - 1),
        [VMEM] * (2 * n_class + 1),
        [VMEM] * (n // 2),
        [pltpu.VMEM((n_class * (r1 + r2), width), BF16)],
    )(pick_near, rest_near, projection, both, *far_in, other, *far_other, *near_in, *near_other)
    partial = [*near, *far]
    arrived = [swap(partial[m], "seq", m) for m in range(n - 1, 0, -1)]
    states = partial[0]
    for part in arrived:
        states = states + part.astype(F32)
    return states.astype(BF16), terms.astype(BF16).T


def refine(input_rows, projection, norm_gain):
    widened = input_rows.astype(jnp.float32)
    full_rows = lax.all_gather(input_rows, ("sec", "tp"), axis=1, tiled=True).astype(jnp.float32)
    squares = jnp.sum(full_rows * full_rows, axis=1, keepdims=True)
    normed = (full_rows * lax.rsqrt(squares / D + 1e-06) * norm_gain).astype(jnp.bfloat16)
    mixing = jnp.dot(
        normed,
        lax.all_gather(projection, "seq", axis=0, tiled=True),
        preferred_element_type=jnp.float32,
    )
    return (widened + mixing).astype(jnp.bfloat16)


def deliver(
    input_rows, token_terms, lengths, first_index, own_total, starts, seq_index, tile_rows, n_seq
):
    slot_count = input_rows.shape[0]
    slot_index = jnp.arange(slot_count, dtype=jnp.int32)
    offset = jnp.mod(slot_index - first_index, slot_count)
    filled = offset < own_total
    finish = jnp.cumsum(lengths)
    response = jnp.sum((finish[None, :] <= offset[:, None]).astype(jnp.int32), axis=1)
    response = jnp.minimum(response, lengths.shape[0] - 1)
    opening = jnp.take(finish - lengths, response)
    source = jnp.where(filled, response * LMAX + offset - opening, 0)
    send_rows = jnp.where(
        filled[:, None], jnp.take(input_rows, source, axis=0), jnp.zeros((), input_rows.dtype)
    )
    send_terms = jnp.where(
        filled[:, None], jnp.take(token_terms, source, axis=0), jnp.zeros((), token_terms.dtype)
    )
    arrived, arrived_terms = (
        lax.all_to_all(
            send_rows.reshape(n_seq, tile_rows, -1), "seq", split_axis=0, concat_axis=0, tiled=True
        ),
        lax.all_to_all(
            send_terms.reshape(n_seq, tile_rows, 2), "seq", split_axis=0, concat_axis=0, tiled=True
        ),
    )
    learner_row = jnp.arange(TOK_DEV, dtype=jnp.int32)
    packed = learner_row // tile_rows * slot_count + seq_index * tile_rows + learner_row % tile_rows
    sender = jnp.sum((starts[None, :] <= packed[:, None]).astype(jnp.int32), axis=1) - 1
    pick_index = sender * tile_rows + learner_row % tile_rows
    states = jnp.take(arrived.reshape(slot_count, -1), pick_index, axis=0)
    moved_terms = jnp.take(arrived_terms.reshape(slot_count, 2), pick_index, axis=0)
    return (states, moved_terms)


def shards(hidden, projection, norm_gain, old_logp, ref_logp, lengths, group_of, rewards):
    n_seq = lax.axis_size("seq")
    seq_index = lax.axis_index("seq")
    tile_rows = SLOTS // n_seq
    group_count = RESP_DEV * n_seq // GROUP
    member_table = (group_of[:, None] == jnp.arange(group_count, dtype=jnp.int32)[None, :]).astype(
        jnp.float32
    )
    reward_value = rewards.astype(jnp.float32)
    partial_value = jnp.stack(
        [
            jnp.dot(reward_value, member_table, precision=lax.Precision.HIGHEST),
            jnp.dot(reward_value * reward_value, member_table, precision=lax.Precision.HIGHEST),
        ]
    )
    own_total = jnp.sum(lengths)
    group_sums = lax.psum(partial_value, "seq")
    counts = lax.all_gather(jnp.reshape(own_total, (1,)), "seq", axis=0, tiled=True)
    group_mean = group_sums[0] / GROUP
    spread = jnp.maximum(jnp.sqrt(group_sums[1] / GROUP - group_mean * group_mean), 1.0)
    advantage = (
        reward_value - jnp.dot(member_table, group_mean, precision=lax.Precision.HIGHEST)
    ) / jnp.dot(member_table, spread, precision=lax.Precision.HIGHEST)
    log_ratio = ref_logp - old_logp
    penalty = jnp.exp(log_ratio) - log_ratio - 1.0
    token_terms = jnp.stack([jnp.repeat(advantage, LMAX), penalty], axis=1).astype(jnp.bfloat16)
    starts = jnp.cumsum(counts) - counts
    first_index = jnp.take(starts, seq_index)
    refined = refine(hidden, projection, norm_gain)
    return deliver(
        refined, token_terms, lengths, first_index, own_total, starts, seq_index, tile_rows, n_seq
    )


def solution(mesh):
    in_specs = (
        P("seq", ("sec", "tp")),
        P("seq", ("sec", "tp")),
        P(),
        P("seq"),
        P("seq"),
        P("seq"),
        P("seq"),
        P("seq"),
    )
    out_specs = (P("seq", ("sec", "tp")), P("seq", None))
    n = mesh.shape["seq"]
    in_place = mesh.shape["sec"] == n and n >= 4 and n & (n - 1) == 0
    body = shards_in_place if in_place else shards
    return jax.shard_map(body, mesh=mesh, in_specs=in_specs, out_specs=out_specs, check_vma=False)
```

```python
import functools

import jax
import jax.numpy as jnp
from jax import lax
from jax.experimental import pallas as pl
from jax.experimental.pallas import tpu as pltpu
from jax.sharding import PartitionSpec as P

D = 5120
TOK_DEV = 128
RESP_DEV = 4
GROUP = 8
LMAX = 64
TILE = 64
SLOTS = 256
EPS = 1e-06
BF16 = jnp.bfloat16
F32 = jnp.float32
I32 = jnp.int32
LANES = 128
INFO = 16

VMEM = pl.BlockSpec(memory_space=pltpu.VMEM)
SMEM = pl.BlockSpec(memory_space=pltpu.SMEM)
HBM = pl.BlockSpec(memory_space=pltpu.HBM)


def iota(shape, dim):
    return lax.broadcasted_iota(I32, shape, dim)


def bits(n):
    return n.bit_length() - 1


def div(x, n):
    return lax.shift_right_arithmetic(x, jnp.full(jnp.shape(x), bits(n), I32))


def mod(x, n):
    return x & (n - 1)


def swap(x, axis, k):
    n = lax.axis_size(axis)
    return lax.ppermute(x, axis, [(i, i ^ k) for i in range(n)])


def early_kernel(n_sec, n_tp, hidden, lengths, group_of, rewards, old_logp, ref_logp, gain, *refs):
    pick, mine, info, gain_out = refs[:4]
    rows_in, length, group, reward, old, ref, sems = refs[4:]
    copies = []
    for i, (src, dst) in enumerate(
        (
            (lengths, length),
            (hidden, rows_in),
            (old_logp, old),
            (ref_logp, ref),
            (group_of, group),
            (rewards, reward),
            (gain, gain_out),
        )
    ):
        copies.append(pltpu.make_async_copy(src, dst, sems.at[i]))
        copies[-1].start()
    a = lax.axis_index("sec")
    t = lax.axis_index("tp")
    n_class = n_sec * n_tp
    rows = rows_in.shape[0]
    n_resp = length.shape[0]
    total = pick.shape[0]
    slots = total // n_sec
    place = iota((total, rows), 0)
    index = mod(place, slots) * n_class + (div(place, slots) ^ a) * n_tp + t
    copies[0].wait()
    source, finish = index, 0
    for r in range(n_resp):
        finish = finish + length[r]
        source = source + jnp.where(index >= finish, LMAX - length[r], 0)
    source = jnp.where(index < finish, source, -1)
    chosen = (iota((total, rows), 1) == source).astype(BF16)
    pick[...] = chosen
    for copy in copies[1:]:
        copy.wait()
    mine[...] = jnp.dot(chosen, rows_in[...], preferred_element_type=F32).astype(BF16)
    log_ratio = ref[...] - old[...]
    penalty = jnp.exp(log_ratio) - log_ratio - 1.0
    lane = iota((1, LANES), 1)
    words = jnp.zeros((1, LANES), F32)
    for r in range(n_resp):
        for i, held in enumerate((length, group, reward)):
            words = jnp.where(lane == i * n_resp + r, held[r].astype(F32), words)
    n_pen = penalty.shape[0]
    filler = jnp.zeros((info.shape[0] - n_pen - 1, LANES), F32)
    info[...] = jnp.concatenate([penalty, words, filler], axis=0).astype(BF16)


def spread_kernel(n_tp, pick, mine, sibling, *outs):
    t = lax.axis_index("tp")
    slots, width = outs[0].shape[0], mine.shape[1]
    own = mine[...].astype(F32)
    other = jnp.dot(pick[...], sibling[...], preferred_element_type=F32)
    first = jnp.where(t == 0, own, other).astype(BF16)
    second = jnp.where(t == 0, other, own).astype(BF16)
    for k, out in enumerate(outs):
        out[:, 0:width] = first[k * slots : (k + 1) * slots]
        out[:, width : 2 * width] = second[k * slots : (k + 1) * slots]


def norm_kernel(n, gain, info, *refs):
    inputs, outs, held = refs[:n], refs[2 * n - 1 : n - 1 : -1], refs[2 * n]
    a = lax.axis_index("sec")
    s = lax.axis_index("seq")
    slots, width = inputs[0].shape
    squares = 0.0
    for ref in inputs:
        x = ref[...].astype(F32)
        squares = squares + jnp.sum(x * x, axis=1, keepdims=True)
    scale = lax.rsqrt(squares / D + EPS)
    for k, ref in enumerate(inputs):
        start = pl.multiple_of((a ^ k) * width, LANES)
        held[k] = (ref[...].astype(F32) * scale * gain[:, pl.ds(start, width)]).astype(BF16)
    beside = jnp.concatenate([info[...]] * (slots // info.shape[0]), axis=0)
    for m, out in enumerate(outs):
        out[:, 0:width] = held[a ^ s ^ m]
        out[:, width : width + LANES] = beside


def info_of(ref, width):
    return ref[0:INFO, width : width + LANES].astype(F32)


def word_sum(block, row, first, last):
    lane = iota(block.shape, 1)
    inside = (iota(block.shape, 0) == row) & (lane >= first) & (lane < last)
    return jnp.sum(jnp.where(inside, block, 0.0)).astype(I32)


def put_counts(moved, width, row, n_resp, counts):
    s = lax.axis_index("seq")
    for m, ref in enumerate(moved):
        counts[s ^ m] = word_sum(info_of(ref, width), row, 0, n_resp)


def class_rows(x, c, n_class):
    return div(x - c + n_class - 1, n_class)


def list_place(counts, n, n_class, tok, s, c, seq_of, position, packed):
    span = tok * n // 4
    edges = []
    for j in range(5):
        edge, start = 0, 0
        for b in range(n):
            edge = edge + class_rows(jnp.clip(j * span - start, 0, counts[b]), c, n_class)
            start = start + counts[b]
        edges.append(edge)
    size = [edges[j + 1] - edges[j] for j in range(4)]
    high = div(s, n // 2)
    far_first = jnp.where(high == 0, size[1], size[0])
    far_rows = jnp.where(high == 0, size[1] + size[3], size[0] + size[2])
    near_first = jnp.where(high == 0, size[0], size[1])
    prefix = 0
    before = jnp.zeros_like(position)
    for b in range(n):
        before = jnp.where(seq_of == b, prefix, before)
        prefix = prefix + class_rows(counts[b], c, n_class)
    group = div(packed, span)
    opening = jnp.where(group == 0, edges[0], jnp.where(group == 1, edges[1], jnp.where(group == 2, edges[2], edges[3])))
    within = before + position - opening
    later = group >= 2
    far = mod(group, 2) != high
    far_place = within + jnp.where(later, far_first, 0)
    near_place = far_rows + within + jnp.where(later, near_first, 0)
    return jnp.where(far, far_place, near_place)


def pack_kernel(n, n_class, n_resp, tok, row, *refs):
    moved, (out, held, counts) = refs[n - 1 :: -1], refs[n:]
    s = lax.axis_index("seq")
    c = lax.axis_index("sec") * lax.axis_size("tp") + lax.axis_index("tp")
    slots, width = moved[0].shape[0], out.shape[1]
    put_counts(moved, width, row, n_resp, counts)
    lane = iota((1, n * slots), 1)
    seq_of = div(lane, slots) ^ s
    q = mod(lane, slots)
    live = jnp.zeros(lane.shape, jnp.bool_)
    start = jnp.zeros(lane.shape, I32)
    total = 0
    for b in range(n):
        live = live | ((seq_of == b) & (q < class_rows(counts[b], c, n_class)))
        start = jnp.where(seq_of == b, total, start)
        total = total + counts[b]
    packed = start + q * n_class + c
    place = list_place(counts, n, n_class, tok, s, c, seq_of, q, packed)
    place = jnp.where(live, place, -1)
    for m, ref in enumerate(moved):
        held[m * slots : (m + 1) * slots, :] = ref[:, 0:width]
    pick = (iota((out.shape[0], n * slots), 0) == place).astype(BF16)
    out[...] = jnp.dot(pick, held[...], preferred_element_type=F32).astype(BF16)


def upright(x):
    return jnp.transpose(jnp.broadcast_to(x.astype(F32), (LANES, x.shape[1]))).astype(I32)


def one_hot(column, out):
    for j in range(out.shape[1] // LANES):
        out[:, j * LANES : (j + 1) * LANES] = (iota(column.shape, 1) + j * LANES == column).astype(BF16)


def index_kernel(n, n_class, n_resp, tok, row, listed, *refs):
    moved, hidden = refs[n - 1 :: -1], refs[n]
    pick_far, pick_near, rest_far, rest_near, counts, lens, own = refs[n + 1 :]
    a = lax.axis_index("sec")
    s = lax.axis_index("seq")
    t = lax.axis_index("tp")
    n_tp = lax.axis_size("tp")
    width = moved[0].shape[1] - LANES
    put_counts(moved, width, row, n_resp, counts)
    block = info_of(moved[0], width)
    for r in range(n_resp):
        lens[r] = word_sum(block, row, r, r + 1)
    half = n // 2 * tok
    for far, pick, rest in ((True, pick_far, rest_far), (False, pick_near, rest_near)):
        lane = iota((1, half), 1)
        w = mod(lane, tok)
        shard = (div(lane, tok) + (n // 2 if far else 0)) ^ s
        packed = div(w, TILE) * (TILE * n) + shard * TILE + mod(w, TILE)
        seq_of = jnp.zeros(lane.shape, I32)
        start = jnp.zeros(lane.shape, I32)
        finish = 0
        for b in range(n):
            finish = finish + counts[b]
            passed = packed >= finish
            seq_of = seq_of + passed.astype(I32)
            start = jnp.where(passed, finish, start)
        index = packed - start
        c = mod(index, n_class)
        place = list_place(counts, n, n_class, tok, s, c, seq_of, div(index, n_class), packed)
        column = ((mod(c, n_tp) ^ t) * n + (div(c, n_tp) ^ a)) * listed + place
        one_hot(upright(column), pick)
        source, ends = index, 0
        for r in range(n_resp):
            ends = ends + lens[r]
            source = source + jnp.where(index >= ends, LMAX - lens[r], 0)
        one_hot(upright(jnp.where(seq_of == s, source, -1)), own)
        rest[...] = jnp.dot(own[...], hidden[...], preferred_element_type=F32)


def mix_kernel(n_lists, pick, rest, projection, *refs):
    pieces, outs, held = refs[:n_lists], refs[n_lists:-1], refs[-1]
    listed = pieces[0].shape[0]
    for k, piece in enumerate(pieces):
        held[k * listed : (k + 1) * listed, :] = piece[...]
    tokens = jnp.dot(pick[...], held[...], preferred_element_type=F32).astype(BF16)
    total = jnp.dot(tokens, projection[...], preferred_element_type=F32) + rest[...]
    tok = outs[0].shape[0]
    for m, out in enumerate(outs):
        out[...] = total[m * tok : (m + 1) * tok].astype(out.dtype)


def terms_kernel(n, n_resp, row, *refs):
    moved, out, words, table = refs[n - 1 :: -1], refs[n], refs[n + 1], refs[n + 2]
    s = lax.axis_index("seq")
    width = moved[0].shape[1] - LANES
    tok = out.shape[1]
    group_count = n * n_resp // GROUP
    for m, ref in enumerate(moved):
        block = info_of(ref, width)
        table[pl.ds((s ^ m) * INFO, INFO), :] = block
        for r in range(3 * n_resp):
            words[s ^ m, r] = word_sum(block, row, r, r + 1)
    w = iota((1, tok), 1)
    packed = div(w, TILE) * (TILE * n) + s * TILE + mod(w, TILE)
    source, finish = packed, 0
    reward = jnp.zeros((1, tok), F32)
    group = jnp.zeros((1, tok), I32)
    total = [0] * group_count
    square = [0] * group_count
    for b in range(n):
        for r in range(n_resp):
            length, number, gain = words[b, r], words[b, n_resp + r], words[b, 2 * n_resp + r]
            within = packed >= finish
            reward = jnp.where(within, gain.astype(F32), reward)
            group = jnp.where(within, number, group)
            finish = finish + length
            source = source + jnp.where(packed >= finish, LMAX - length, 0)
            for g in range(group_count):
                total[g] = total[g] + jnp.where(number == g, gain, 0)
                square[g] = square[g] + jnp.where(number == g, gain * gain, 0)
    total_of = jnp.zeros((1, tok), F32)
    square_of = jnp.zeros((1, tok), F32)
    for g in range(group_count):
        total_of = jnp.where(group == g, total[g].astype(F32), total_of)
        square_of = jnp.where(group == g, square[g].astype(F32), square_of)
    mean = total_of / GROUP
    spread = jnp.maximum(jnp.sqrt(square_of / GROUP - mean * mean), 1.0)
    advantage = (reward - mean) / spread
    pick = (iota((LANES, tok), 0) == mod(source, LANES)).astype(BF16)
    found = jnp.dot(table[...].astype(BF16), pick, preferred_element_type=F32)
    line = div(source, LANES)
    chosen = iota(found.shape, 0) == div(line, row) * INFO + mod(line, row)
    penalty = jnp.sum(jnp.where(chosen, found, 0.0), axis=0, keepdims=True)
    out[0:1, :] = advantage
    out[1:2, :] = penalty


def call(kernel, out_shape, in_specs, out_specs, scratch=()):
    return pl.pallas_call(
        kernel,
        out_shape=out_shape,
        in_specs=in_specs,
        out_specs=out_specs,
        scratch_shapes=list(scratch),
        compiler_params=pltpu.CompilerParams(vmem_limit_bytes=48 * 1024 * 1024),
    )


def shards_in_place(hidden, projection, norm_gain, old_logp, ref_logp, lengths, group_of, rewards):
    n = lax.axis_size("seq")
    n_tp = lax.axis_size("tp")
    n_class = n * n_tp
    rows, cols = hidden.shape
    n_resp = lengths.shape[0]
    width = cols * n_tp
    slots = rows // n_class
    row = rows // LANES
    tok = TOK_DEV
    tokens = tok * n
    listed = -(-((tokens + (n_class - 1) * n) // n_class) // 16) * 16
    shape = jax.ShapeDtypeStruct
    info_like = shape((slots, width + LANES), BF16)

    sibling = swap(hidden, "tp", 1)
    pick, mine, info, gain = call(
        functools.partial(early_kernel, n, n_tp),
        [
            shape((rows // n_tp, rows), BF16),
            shape((rows // n_tp, cols), BF16),
            shape((INFO, LANES), BF16),
            shape((1, D), F32),
        ],
        [HBM] * 7,
        [VMEM] * 4,
        [
            pltpu.VMEM((rows, cols), BF16),
            pltpu.SMEM((n_resp,), I32),
            pltpu.SMEM((n_resp,), I32),
            pltpu.SMEM((n_resp,), I32),
            pltpu.VMEM((row, LANES), F32),
            pltpu.VMEM((row, LANES), F32),
            pltpu.SemaphoreType.DMA((7,)),
        ],
    )(
        *(
            pltpu.with_memory_space_constraint(x, pltpu.HBM)
            for x in (
                hidden,
                lengths,
                group_of,
                rewards,
                old_logp.reshape(row, LANES),
                ref_logp.reshape(row, LANES),
                norm_gain.reshape(1, D),
            )
        )
    )
    dealt = call(
        functools.partial(spread_kernel, n_tp), [shape((slots, width), BF16)] * n, [VMEM] * 3, [VMEM] * n
    )(pick, mine, sibling)
    whole = [dealt[0]] + [swap(dealt[k], "sec", k) for k in range(1, n)]
    normed = call(
        functools.partial(norm_kernel, n),
        [info_like] * n,
        [VMEM] * (n + 2),
        [VMEM] * n,
        [pltpu.VMEM((n, slots, width), BF16)],
    )(gain, info, *whole)[::-1]
    moved = [normed[0]] + [swap(normed[m], "seq", m) for m in range(n - 1, 0, -1)][::-1]
    mine = call(
        functools.partial(pack_kernel, n, n_class, n_resp, tok, row),
        shape((listed, width), BF16),
        [VMEM] * n,
        VMEM,
        [pltpu.VMEM((n * slots, width), BF16), pltpu.SMEM((n,), I32)],
    )(*moved[::-1])
    half = n // 2 * tok
    pick_far, pick_near, rest_far, rest_near = call(
        functools.partial(index_kernel, n, n_class, n_resp, tok, row, listed),
        [
            shape((half, n_class * listed), BF16),
            shape((half, n_class * listed), BF16),
            shape((half, cols), F32),
            shape((half, cols), F32),
        ],
        [VMEM] * (n + 1),
        [VMEM] * 4,
        [pltpu.SMEM((n,), I32), pltpu.SMEM((n_resp,), I32), pltpu.VMEM((half, rows), BF16)],
    )(*moved[::-1], hidden)
    terms = call(
        functools.partial(terms_kernel, n, n_resp, row),
        shape((2, tok), F32),
        [VMEM] * n,
        VMEM,
        [pltpu.SMEM((n, 3 * n_resp), I32), pltpu.VMEM((n * INFO, LANES), F32)],
    )(*moved[::-1])
    after = lambda x, *ys: lax.optimization_barrier((x, *ys))[0]
    same = [mine] + [swap(mine, "sec", k) for k in range(1, n)]
    lists = same + [swap(after(x, pick_far, terms), "tp", 1) for x in same]
    mix = lambda pick, rest, kind: call(
        functools.partial(mix_kernel, n_class),
        [shape((tok, cols), kind)] + [shape((tok, cols), BF16)] * (n // 2 - 1),
        [VMEM] * (n_class + 3),
        [VMEM] * (n // 2),
        [pltpu.VMEM((n_class * listed, width), BF16)],
    )(pick, rest, projection, *lists)
    far = mix(pick_far, rest_far, BF16)
    near = mix(after(pick_near, *far), rest_near, F32)
    partial = [*near, *far]
    arrived = [swap(partial[m], "seq", m) for m in range(n - 1, 0, -1)]
    states = partial[0]
    for part in arrived:
        states = states + part.astype(F32)
    return states.astype(BF16), terms.astype(BF16).T


def refine(input_rows, projection, norm_gain):
    widened = input_rows.astype(jnp.float32)
    full_rows = lax.all_gather(input_rows, ("sec", "tp"), axis=1, tiled=True).astype(jnp.float32)
    squares = jnp.sum(full_rows * full_rows, axis=1, keepdims=True)
    normed = (full_rows * lax.rsqrt(squares / D + 1e-06) * norm_gain).astype(jnp.bfloat16)
    mixing = jnp.dot(
        normed,
        lax.all_gather(projection, "seq", axis=0, tiled=True),
        preferred_element_type=jnp.float32,
    )
    return (widened + mixing).astype(jnp.bfloat16)


def deliver(
    input_rows, token_terms, lengths, first_index, own_total, starts, seq_index, tile_rows, n_seq
):
    slot_count = input_rows.shape[0]
    slot_index = jnp.arange(slot_count, dtype=jnp.int32)
    offset = jnp.mod(slot_index - first_index, slot_count)
    filled = offset < own_total
    finish = jnp.cumsum(lengths)
    response = jnp.sum((finish[None, :] <= offset[:, None]).astype(jnp.int32), axis=1)
    response = jnp.minimum(response, lengths.shape[0] - 1)
    opening = jnp.take(finish - lengths, response)
    source = jnp.where(filled, response * LMAX + offset - opening, 0)
    send_rows = jnp.where(
        filled[:, None], jnp.take(input_rows, source, axis=0), jnp.zeros((), input_rows.dtype)
    )
    send_terms = jnp.where(
        filled[:, None], jnp.take(token_terms, source, axis=0), jnp.zeros((), token_terms.dtype)
    )
    arrived, arrived_terms = (
        lax.all_to_all(
            send_rows.reshape(n_seq, tile_rows, -1), "seq", split_axis=0, concat_axis=0, tiled=True
        ),
        lax.all_to_all(
            send_terms.reshape(n_seq, tile_rows, 2), "seq", split_axis=0, concat_axis=0, tiled=True
        ),
    )
    learner_row = jnp.arange(TOK_DEV, dtype=jnp.int32)
    packed = learner_row // tile_rows * slot_count + seq_index * tile_rows + learner_row % tile_rows
    sender = jnp.sum((starts[None, :] <= packed[:, None]).astype(jnp.int32), axis=1) - 1
    pick_index = sender * tile_rows + learner_row % tile_rows
    states = jnp.take(arrived.reshape(slot_count, -1), pick_index, axis=0)
    moved_terms = jnp.take(arrived_terms.reshape(slot_count, 2), pick_index, axis=0)
    return (states, moved_terms)


def shards(hidden, projection, norm_gain, old_logp, ref_logp, lengths, group_of, rewards):
    n_seq = lax.axis_size("seq")
    seq_index = lax.axis_index("seq")
    tile_rows = SLOTS // n_seq
    group_count = RESP_DEV * n_seq // GROUP
    member_table = (group_of[:, None] == jnp.arange(group_count, dtype=jnp.int32)[None, :]).astype(
        jnp.float32
    )
    reward_value = rewards.astype(jnp.float32)
    partial_value = jnp.stack(
        [
            jnp.dot(reward_value, member_table, precision=lax.Precision.HIGHEST),
            jnp.dot(reward_value * reward_value, member_table, precision=lax.Precision.HIGHEST),
        ]
    )
    own_total = jnp.sum(lengths)
    group_sums = lax.psum(partial_value, "seq")
    counts = lax.all_gather(jnp.reshape(own_total, (1,)), "seq", axis=0, tiled=True)
    group_mean = group_sums[0] / GROUP
    spread = jnp.maximum(jnp.sqrt(group_sums[1] / GROUP - group_mean * group_mean), 1.0)
    advantage = (
        reward_value - jnp.dot(member_table, group_mean, precision=lax.Precision.HIGHEST)
    ) / jnp.dot(member_table, spread, precision=lax.Precision.HIGHEST)
    log_ratio = ref_logp - old_logp
    penalty = jnp.exp(log_ratio) - log_ratio - 1.0
    token_terms = jnp.stack([jnp.repeat(advantage, LMAX), penalty], axis=1).astype(jnp.bfloat16)
    starts = jnp.cumsum(counts) - counts
    first_index = jnp.take(starts, seq_index)
    refined = refine(hidden, projection, norm_gain)
    return deliver(
        refined, token_terms, lengths, first_index, own_total, starts, seq_index, tile_rows, n_seq
    )


def solution(mesh):
    in_specs = (
        P("seq", ("sec", "tp")),
        P("seq", ("sec", "tp")),
        P(),
        P("seq"),
        P("seq"),
        P("seq"),
        P("seq"),
        P("seq"),
    )
    out_specs = (P("seq", ("sec", "tp")), P("seq", None))
    n = mesh.shape["seq"]
    in_place = mesh.shape["sec"] == n and n >= 4 and n & (n - 1) == 0
    body = shards_in_place if in_place else shards
    return jax.shard_map(body, mesh=mesh, in_specs=in_specs, out_specs=out_specs, check_vma=False)
```

```python
import functools

import jax
import jax.numpy as jnp
from jax import lax
from jax.experimental import pallas as pl
from jax.experimental.pallas import tpu as pltpu
from jax.sharding import PartitionSpec as P

D = 5120
TOK_DEV = 128
RESP_DEV = 4
GROUP = 8
LMAX = 64
TILE = 64
SLOTS = 256
EPS = 1e-06
BF16 = jnp.bfloat16
F32 = jnp.float32
I32 = jnp.int32
LANES = 128
INFO = 16

VMEM = pl.BlockSpec(memory_space=pltpu.VMEM)
SMEM = pl.BlockSpec(memory_space=pltpu.SMEM)
HBM = pl.BlockSpec(memory_space=pltpu.HBM)


def iota(shape, dim):
    return lax.broadcasted_iota(I32, shape, dim)


def bits(n):
    return n.bit_length() - 1


def div(x, n):
    return lax.shift_right_arithmetic(x, jnp.full(jnp.shape(x), bits(n), I32))


def mod(x, n):
    return x & (n - 1)


def swap(x, axis, k):
    n = lax.axis_size(axis)
    return lax.ppermute(x, axis, [(i, i ^ k) for i in range(n)])


def early_kernel(n_sec, n_tp, hidden, lengths, group_of, rewards, old_logp, ref_logp, gain, *refs):
    pick, mine, info, gain_out = refs[:4]
    rows_in, length, group, reward, old, ref, sems = refs[4:]
    copies = []
    for i, (src, dst) in enumerate(
        (
            (lengths, length),
            (hidden, rows_in),
            (old_logp, old),
            (ref_logp, ref),
            (group_of, group),
            (rewards, reward),
            (gain, gain_out),
        )
    ):
        copies.append(pltpu.make_async_copy(src, dst, sems.at[i]))
        copies[-1].start()
    a = lax.axis_index("sec")
    t = lax.axis_index("tp")
    n_class = n_sec * n_tp
    rows = rows_in.shape[0]
    n_resp = length.shape[0]
    total = pick.shape[0]
    slots = total // n_sec
    place = iota((total, rows), 0)
    index = mod(place, slots) * n_class + (div(place, slots) ^ a) * n_tp + t
    copies[0].wait()
    source, finish = index, 0
    for r in range(n_resp):
        finish = finish + length[r]
        source = source + jnp.where(index >= finish, LMAX - length[r], 0)
    source = jnp.where(index < finish, source, -1)
    chosen = (iota((total, rows), 1) == source).astype(BF16)
    pick[...] = chosen
    for copy in copies[1:]:
        copy.wait()
    mine[...] = jnp.dot(chosen, rows_in[...], preferred_element_type=F32).astype(BF16)
    log_ratio = ref[...] - old[...]
    penalty = jnp.exp(log_ratio) - log_ratio - 1.0
    lane = iota((1, LANES), 1)
    words = jnp.zeros((1, LANES), F32)
    for r in range(n_resp):
        for i, held in enumerate((length, group, reward)):
            words = jnp.where(lane == i * n_resp + r, held[r].astype(F32), words)
    n_pen = penalty.shape[0]
    filler = jnp.zeros((info.shape[0] - n_pen - 1, LANES), F32)
    info[...] = jnp.concatenate([penalty, words, filler], axis=0).astype(BF16)


def spread_kernel(n_tp, pick, mine, sibling, *outs):
    t = lax.axis_index("tp")
    slots, width = outs[0].shape[0], mine.shape[1]
    own = mine[...].astype(F32)
    other = jnp.dot(pick[...], sibling[...], preferred_element_type=F32)
    first = jnp.where(t == 0, own, other).astype(BF16)
    second = jnp.where(t == 0, other, own).astype(BF16)
    for k, out in enumerate(outs):
        out[:, 0:width] = first[k * slots : (k + 1) * slots]
        out[:, width : 2 * width] = second[k * slots : (k + 1) * slots]


def norm_kernel(n, gain, info, *refs):
    inputs, outs, held = refs[:n], refs[2 * n - 1 : n - 1 : -1], refs[2 * n]
    a = lax.axis_index("sec")
    s = lax.axis_index("seq")
    slots, width = inputs[0].shape
    squares = 0.0
    for ref in inputs:
        x = ref[...].astype(F32)
        squares = squares + jnp.sum(x * x, axis=1, keepdims=True)
    scale = lax.rsqrt(squares / D + EPS)
    for k, ref in enumerate(inputs):
        start = pl.multiple_of((a ^ k) * width, LANES)
        held[k] = (ref[...].astype(F32) * scale * gain[:, pl.ds(start, width)]).astype(BF16)
    beside = jnp.concatenate([info[...]] * (slots // info.shape[0]), axis=0)
    for m, out in enumerate(outs):
        out[:, 0:width] = held[a ^ s ^ m]
        out[:, width : width + LANES] = beside


def info_of(ref, width):
    return ref[0:INFO, width : width + LANES].astype(F32)


def word_sum(block, row, first, last):
    lane = iota(block.shape, 1)
    inside = (iota(block.shape, 0) == row) & (lane >= first) & (lane < last)
    return jnp.sum(jnp.where(inside, block, 0.0)).astype(I32)


def put_counts(moved, width, row, n_resp, counts):
    s = lax.axis_index("seq")
    for m, ref in enumerate(moved):
        counts[s ^ m] = word_sum(info_of(ref, width), row, 0, n_resp)


def class_rows(x, c, n_class):
    return div(x - c + n_class - 1, n_class)


def list_place(counts, n, n_class, tok, s, c, seq_of, position, packed):
    span = tok * n // 4
    edges = []
    for j in range(5):
        edge, start = 0, 0
        for b in range(n):
            edge = edge + class_rows(jnp.clip(j * span - start, 0, counts[b]), c, n_class)
            start = start + counts[b]
        edges.append(edge)
    size = [edges[j + 1] - edges[j] for j in range(4)]
    high = div(s, n // 2)
    far_first = jnp.where(high == 0, size[1], size[0])
    far_rows = jnp.where(high == 0, size[1] + size[3], size[0] + size[2])
    near_first = jnp.where(high == 0, size[0], size[1])
    prefix = 0
    before = jnp.zeros_like(position)
    for b in range(n):
        before = jnp.where(seq_of == b, prefix, before)
        prefix = prefix + class_rows(counts[b], c, n_class)
    group = div(packed, span)
    opening = jnp.where(group == 0, edges[0], jnp.where(group == 1, edges[1], jnp.where(group == 2, edges[2], edges[3])))
    within = before + position - opening
    later = group >= 2
    far = mod(group, 2) != high
    far_place = within + jnp.where(later, far_first, 0)
    near_place = far_rows + within + jnp.where(later, near_first, 0)
    return jnp.where(far, far_place, near_place)


def pack_kernel(n, n_class, n_resp, tok, row, *refs):
    moved, (out, held, counts) = refs[n - 1 :: -1], refs[n:]
    s = lax.axis_index("seq")
    c = lax.axis_index("sec") * lax.axis_size("tp") + lax.axis_index("tp")
    slots, width = moved[0].shape[0], out.shape[1]
    put_counts(moved, width, row, n_resp, counts)
    lane = iota((1, n * slots), 1)
    seq_of = div(lane, slots) ^ s
    q = mod(lane, slots)
    live = jnp.zeros(lane.shape, jnp.bool_)
    start = jnp.zeros(lane.shape, I32)
    total = 0
    for b in range(n):
        live = live | ((seq_of == b) & (q < class_rows(counts[b], c, n_class)))
        start = jnp.where(seq_of == b, total, start)
        total = total + counts[b]
    packed = start + q * n_class + c
    place = list_place(counts, n, n_class, tok, s, c, seq_of, q, packed)
    place = jnp.where(live, place, -1)
    for m, ref in enumerate(moved):
        held[m * slots : (m + 1) * slots, :] = ref[:, 0:width]
    pick = (iota((out.shape[0], n * slots), 0) == place).astype(BF16)
    out[...] = jnp.dot(pick, held[...], preferred_element_type=F32).astype(BF16)


def upright(x):
    return jnp.transpose(jnp.broadcast_to(x.astype(F32), (LANES, x.shape[1]))).astype(I32)


def one_hot(column, out):
    for j in range(out.shape[1] // LANES):
        out[:, j * LANES : (j + 1) * LANES] = (iota(column.shape, 1) + j * LANES == column).astype(BF16)


def index_kernel(n, n_class, n_resp, tok, row, step, *refs):
    moved, hidden = refs[n - 1 :: -1], refs[n]
    pick_far, pick_near, rest_far, rest_near, counts, lens, own = refs[n + 1 :]
    a = lax.axis_index("sec")
    s = lax.axis_index("seq")
    t = lax.axis_index("tp")
    n_tp = lax.axis_size("tp")
    width = moved[0].shape[1] - LANES
    put_counts(moved, width, row, n_resp, counts)
    block = info_of(moved[0], width)
    for r in range(n_resp):
        lens[r] = word_sum(block, row, r, r + 1)
    half = n // 2 * tok
    for far, pick, rest in ((True, pick_far, rest_far), (False, pick_near, rest_near)):
        lane = iota((1, half), 1)
        w = mod(lane, tok)
        shard = (div(lane, tok) + (n // 2 if far else 0)) ^ s
        packed = div(w, TILE) * (TILE * n) + shard * TILE + mod(w, TILE)
        seq_of = jnp.zeros(lane.shape, I32)
        start = jnp.zeros(lane.shape, I32)
        finish = 0
        for b in range(n):
            finish = finish + counts[b]
            passed = packed >= finish
            seq_of = seq_of + passed.astype(I32)
            start = jnp.where(passed, finish, start)
        index = packed - start
        c = mod(index, n_class)
        place = list_place(counts, n, n_class, tok, s, c, seq_of, div(index, n_class), packed)
        column = ((mod(c, n_tp) ^ t) * n + (div(c, n_tp) ^ a)) * step + place
        one_hot(upright(column), pick)
        source, ends = index, 0
        for r in range(n_resp):
            ends = ends + lens[r]
            source = source + jnp.where(index >= ends, LMAX - lens[r], 0)
        one_hot(upright(jnp.where(seq_of == s, source, -1)), own)
        rest[...] = jnp.dot(own[...], hidden[...], preferred_element_type=F32)


def mix_kernel(n_lists, pick, rest, projection, *refs):
    pieces, outs, held = refs[:n_lists], refs[n_lists:-1], refs[-1]
    listed, step = pieces[0].shape[0], held.shape[0] // n_lists
    for k, piece in enumerate(pieces):
        rows = piece[...].astype(F32)
        if step > listed:
            rows = jnp.concatenate([rows, jnp.zeros((step - listed, rows.shape[1]), F32)], axis=0)
        held[k * step : (k + 1) * step, :] = rows.astype(BF16)
    tokens = jnp.dot(pick[...], held[...], preferred_element_type=F32).astype(BF16)
    total = jnp.dot(tokens, projection[...], preferred_element_type=F32) + rest[...]
    first = 0
    for out in outs:
        out[...] = total[first : first + out.shape[0]].astype(out.dtype)
        first += out.shape[0]


def join_kernel(own, other, out):
    out[...] = (own[...] + other[...].astype(F32)).astype(out.dtype)


def final_kernel(n_whole, n_first, *refs):
    own, parts, out = refs[0], refs[1:-1], refs[-1]
    half = out.shape[0] // 2
    total = own[...]
    for part in parts[:n_whole]:
        total = total + part[...].astype(F32)
    first, second = total[0:half], total[half:]
    for part in parts[n_whole : n_whole + n_first]:
        first = first + part[...].astype(F32)
    for part in parts[n_whole + n_first :]:
        second = second + part[...].astype(F32)
    out[0:half] = first.astype(out.dtype)
    out[half:] = second.astype(out.dtype)


def terms_kernel(n, n_resp, row, *refs):
    moved, out, words, table = refs[n - 1 :: -1], refs[n], refs[n + 1], refs[n + 2]
    s = lax.axis_index("seq")
    width = moved[0].shape[1] - LANES
    tok = out.shape[1]
    group_count = n * n_resp // GROUP
    for m, ref in enumerate(moved):
        block = info_of(ref, width)
        table[pl.ds((s ^ m) * INFO, INFO), :] = block
        for r in range(3 * n_resp):
            words[s ^ m, r] = word_sum(block, row, r, r + 1)
    w = iota((1, tok), 1)
    packed = div(w, TILE) * (TILE * n) + s * TILE + mod(w, TILE)
    source, finish = packed, 0
    reward = jnp.zeros((1, tok), F32)
    group = jnp.zeros((1, tok), I32)
    total = [0] * group_count
    square = [0] * group_count
    for b in range(n):
        for r in range(n_resp):
            length, number, gain = words[b, r], words[b, n_resp + r], words[b, 2 * n_resp + r]
            within = packed >= finish
            reward = jnp.where(within, gain.astype(F32), reward)
            group = jnp.where(within, number, group)
            finish = finish + length
            source = source + jnp.where(packed >= finish, LMAX - length, 0)
            for g in range(group_count):
                total[g] = total[g] + jnp.where(number == g, gain, 0)
                square[g] = square[g] + jnp.where(number == g, gain * gain, 0)
    total_of = jnp.zeros((1, tok), F32)
    square_of = jnp.zeros((1, tok), F32)
    for g in range(group_count):
        total_of = jnp.where(group == g, total[g].astype(F32), total_of)
        square_of = jnp.where(group == g, square[g].astype(F32), square_of)
    mean = total_of / GROUP
    spread = jnp.maximum(jnp.sqrt(square_of / GROUP - mean * mean), 1.0)
    advantage = (reward - mean) / spread
    pick = (iota((LANES, tok), 0) == mod(source, LANES)).astype(BF16)
    found = jnp.dot(table[...].astype(BF16), pick, preferred_element_type=F32)
    line = div(source, LANES)
    chosen = iota(found.shape, 0) == div(line, row) * INFO + mod(line, row)
    penalty = jnp.sum(jnp.where(chosen, found, 0.0), axis=0, keepdims=True)
    out[0:1, :] = advantage
    out[1:2, :] = penalty


def call(kernel, out_shape, in_specs, out_specs, scratch=()):
    return pl.pallas_call(
        kernel,
        out_shape=out_shape,
        in_specs=in_specs,
        out_specs=out_specs,
        scratch_shapes=list(scratch),
        compiler_params=pltpu.CompilerParams(vmem_limit_bytes=48 * 1024 * 1024),
    )


def shards_in_place(hidden, projection, norm_gain, old_logp, ref_logp, lengths, group_of, rewards):
    n = lax.axis_size("seq")
    n_tp = lax.axis_size("tp")
    n_class = n * n_tp
    rows, cols = hidden.shape
    n_resp = lengths.shape[0]
    width = cols * n_tp
    slots = rows // n_class
    row = rows // LANES
    tok = TOK_DEV
    tokens = tok * n
    up = lambda x, m: -(-x // m) * m
    listed = up((tokens + (n_class - 1) * n) // n_class, 8)
    step = up(listed, 16)
    shape = jax.ShapeDtypeStruct
    info_like = shape((slots, width + LANES), BF16)

    sibling = swap(hidden, "tp", 1)
    pick, mine, info, gain = call(
        functools.partial(early_kernel, n, n_tp),
        [
            shape((rows // n_tp, rows), BF16),
            shape((rows // n_tp, cols), BF16),
            shape((INFO, LANES), BF16),
            shape((1, D), F32),
        ],
        [HBM] * 7,
        [VMEM] * 4,
        [
            pltpu.VMEM((rows, cols), BF16),
            pltpu.SMEM((n_resp,), I32),
            pltpu.SMEM((n_resp,), I32),
            pltpu.SMEM((n_resp,), I32),
            pltpu.VMEM((row, LANES), F32),
            pltpu.VMEM((row, LANES), F32),
            pltpu.SemaphoreType.DMA((7,)),
        ],
    )(
        *(
            pltpu.with_memory_space_constraint(x, pltpu.HBM)
            for x in (
                hidden,
                lengths,
                group_of,
                rewards,
                old_logp.reshape(row, LANES),
                ref_logp.reshape(row, LANES),
                norm_gain.reshape(1, D),
            )
        )
    )
    dealt = call(
        functools.partial(spread_kernel, n_tp), [shape((slots, width), BF16)] * n, [VMEM] * 3, [VMEM] * n
    )(pick, mine, sibling)
    whole = [dealt[0]] + [swap(dealt[k], "sec", k) for k in range(1, n)]
    normed = call(
        functools.partial(norm_kernel, n),
        [info_like] * n,
        [VMEM] * (n + 2),
        [VMEM] * n,
        [pltpu.VMEM((n, slots, width), BF16)],
    )(gain, info, *whole)[::-1]
    moved = [normed[0]] + [swap(normed[m], "seq", m) for m in range(n - 1, 0, -1)][::-1]
    mine = call(
        functools.partial(pack_kernel, n, n_class, n_resp, tok, row),
        shape((listed, width), BF16),
        [VMEM] * n,
        VMEM,
        [pltpu.VMEM((n * slots, width), BF16), pltpu.SMEM((n,), I32)],
    )(*moved[::-1])
    half = n // 2 * tok
    pick_far, pick_near, rest_far, rest_near = call(
        functools.partial(index_kernel, n, n_class, n_resp, tok, row, step),
        [
            shape((half, n_class * step), BF16),
            shape((half, n_class * step), BF16),
            shape((half, cols), F32),
            shape((half, cols), F32),
        ],
        [VMEM] * (n + 1),
        [VMEM] * 4,
        [pltpu.SMEM((n,), I32), pltpu.SMEM((n_resp,), I32), pltpu.VMEM((half, rows), BF16)],
    )(*moved[::-1], hidden)
    terms = call(
        functools.partial(terms_kernel, n, n_resp, row),
        shape((2, tok), F32),
        [VMEM] * n,
        VMEM,
        [pltpu.SMEM((n, 3 * n_resp), I32), pltpu.VMEM((n * INFO, LANES), F32)],
    )(*moved[::-1])
    after = lambda x, *ys: lax.optimization_barrier((x, *ys))[0]
    same = [mine] + [swap(mine, "sec", k) for k in range(1, n)]
    lists = same + [swap(after(x, pick_far, terms), "tp", 1) for x in same]
    mix = lambda pick, rest, outs: call(
        functools.partial(mix_kernel, n_class),
        outs,
        [VMEM] * (n_class + 3),
        [VMEM] * len(outs),
        [pltpu.VMEM((n_class * step, width), BF16)],
    )(pick, rest, projection, *lists)
    part = tok // 2
    joined = n // 2
    far = mix(
        pick_far,
        rest_far,
        [shape((part, cols), F32 if m % 2 and h else BF16) for m in range(joined) for h in range(2)],
    )
    helped = [swap(far[2 * m + 1], "seq", 1) for m in range(0, joined, 2)]
    direct = [swap(far[2 * m], "seq", joined + m) for m in range(joined - 1, -1, -1)]
    sums = [
        call(join_kernel, shape((part, cols), BF16), [VMEM] * 2, VMEM)(far[2 * m + 3], got)
        for m, got in zip(range(0, joined, 2), helped, strict=True)
    ]
    passed = [swap(x, "seq", joined + m + 1) for m, x in zip(range(0, joined, 2), sums, strict=True)]
    near = mix(
        after(pick_near, *far), rest_near, [shape((tok, cols), F32)] + [shape((tok, cols), BF16)] * (joined - 1)
    )
    whole = [swap(near[m], "seq", m) for m in range(1, joined)]
    states = call(
        functools.partial(final_kernel, len(whole), len(direct)),
        shape((tok, cols), BF16),
        [VMEM] * (1 + len(whole) + len(direct) + len(passed)),
        VMEM,
    )(near[0], *whole, *direct, *passed)
    return states, terms.astype(BF16).T


def refine(input_rows, projection, norm_gain):
    widened = input_rows.astype(jnp.float32)
    full_rows = lax.all_gather(input_rows, ("sec", "tp"), axis=1, tiled=True).astype(jnp.float32)
    squares = jnp.sum(full_rows * full_rows, axis=1, keepdims=True)
    normed = (full_rows * lax.rsqrt(squares / D + 1e-06) * norm_gain).astype(jnp.bfloat16)
    mixing = jnp.dot(
        normed,
        lax.all_gather(projection, "seq", axis=0, tiled=True),
        preferred_element_type=jnp.float32,
    )
    return (widened + mixing).astype(jnp.bfloat16)


def deliver(
    input_rows, token_terms, lengths, first_index, own_total, starts, seq_index, tile_rows, n_seq
):
    slot_count = input_rows.shape[0]
    slot_index = jnp.arange(slot_count, dtype=jnp.int32)
    offset = jnp.mod(slot_index - first_index, slot_count)
    filled = offset < own_total
    finish = jnp.cumsum(lengths)
    response = jnp.sum((finish[None, :] <= offset[:, None]).astype(jnp.int32), axis=1)
    response = jnp.minimum(response, lengths.shape[0] - 1)
    opening = jnp.take(finish - lengths, response)
    source = jnp.where(filled, response * LMAX + offset - opening, 0)
    send_rows = jnp.where(
        filled[:, None], jnp.take(input_rows, source, axis=0), jnp.zeros((), input_rows.dtype)
    )
    send_terms = jnp.where(
        filled[:, None], jnp.take(token_terms, source, axis=0), jnp.zeros((), token_terms.dtype)
    )
    arrived, arrived_terms = (
        lax.all_to_all(
            send_rows.reshape(n_seq, tile_rows, -1), "seq", split_axis=0, concat_axis=0, tiled=True
        ),
        lax.all_to_all(
            send_terms.reshape(n_seq, tile_rows, 2), "seq", split_axis=0, concat_axis=0, tiled=True
        ),
    )
    learner_row = jnp.arange(TOK_DEV, dtype=jnp.int32)
    packed = learner_row // tile_rows * slot_count + seq_index * tile_rows + learner_row % tile_rows
    sender = jnp.sum((starts[None, :] <= packed[:, None]).astype(jnp.int32), axis=1) - 1
    pick_index = sender * tile_rows + learner_row % tile_rows
    states = jnp.take(arrived.reshape(slot_count, -1), pick_index, axis=0)
    moved_terms = jnp.take(arrived_terms.reshape(slot_count, 2), pick_index, axis=0)
    return (states, moved_terms)


def shards(hidden, projection, norm_gain, old_logp, ref_logp, lengths, group_of, rewards):
    n_seq = lax.axis_size("seq")
    seq_index = lax.axis_index("seq")
    tile_rows = SLOTS // n_seq
    group_count = RESP_DEV * n_seq // GROUP
    member_table = (group_of[:, None] == jnp.arange(group_count, dtype=jnp.int32)[None, :]).astype(
        jnp.float32
    )
    reward_value = rewards.astype(jnp.float32)
    partial_value = jnp.stack(
        [
            jnp.dot(reward_value, member_table, precision=lax.Precision.HIGHEST),
            jnp.dot(reward_value * reward_value, member_table, precision=lax.Precision.HIGHEST),
        ]
    )
    own_total = jnp.sum(lengths)
    group_sums = lax.psum(partial_value, "seq")
    counts = lax.all_gather(jnp.reshape(own_total, (1,)), "seq", axis=0, tiled=True)
    group_mean = group_sums[0] / GROUP
    spread = jnp.maximum(jnp.sqrt(group_sums[1] / GROUP - group_mean * group_mean), 1.0)
    advantage = (
        reward_value - jnp.dot(member_table, group_mean, precision=lax.Precision.HIGHEST)
    ) / jnp.dot(member_table, spread, precision=lax.Precision.HIGHEST)
    log_ratio = ref_logp - old_logp
    penalty = jnp.exp(log_ratio) - log_ratio - 1.0
    token_terms = jnp.stack([jnp.repeat(advantage, LMAX), penalty], axis=1).astype(jnp.bfloat16)
    starts = jnp.cumsum(counts) - counts
    first_index = jnp.take(starts, seq_index)
    refined = refine(hidden, projection, norm_gain)
    return deliver(
        refined, token_terms, lengths, first_index, own_total, starts, seq_index, tile_rows, n_seq
    )


def solution(mesh):
    in_specs = (
        P("seq", ("sec", "tp")),
        P("seq", ("sec", "tp")),
        P(),
        P("seq"),
        P("seq"),
        P("seq"),
        P("seq"),
        P("seq"),
    )
    out_specs = (P("seq", ("sec", "tp")), P("seq", None))
    n = mesh.shape["seq"]
    in_place = mesh.shape["sec"] == n and n >= 4 and n & (n - 1) == 0
    body = shards_in_place if in_place else shards
    return jax.shard_map(body, mesh=mesh, in_specs=in_specs, out_specs=out_specs, check_vma=False)
```

```python
import functools

import jax
import jax.numpy as jnp
from jax import lax
from jax.experimental import pallas as pl
from jax.experimental.pallas import tpu as pltpu
from jax.sharding import PartitionSpec as P

D = 5120
TOK_DEV = 128
RESP_DEV = 4
GROUP = 8
LMAX = 64
TILE = 64
SLOTS = 256
EPS = 1e-06
BF16 = jnp.bfloat16
F32 = jnp.float32
I32 = jnp.int32
LANES = 128
INFO = 16
ARRIVALS = (2, 1, 3, 0)

VMEM = pl.BlockSpec(memory_space=pltpu.VMEM)
SMEM = pl.BlockSpec(memory_space=pltpu.SMEM)
HBM = pl.BlockSpec(memory_space=pltpu.HBM)


def iota(shape, dim):
    return lax.broadcasted_iota(I32, shape, dim)


def bits(n):
    return n.bit_length() - 1


def div(x, n):
    return lax.shift_right_arithmetic(x, jnp.full(jnp.shape(x), bits(n), I32))


def mod(x, n):
    return x & (n - 1)


def swap(x, axis, k):
    n = lax.axis_size(axis)
    return lax.ppermute(x, axis, [(i, i ^ k) for i in range(n)])


def early_kernel(n_sec, n_tp, hidden, lengths, group_of, rewards, old_logp, ref_logp, gain, *refs):
    pick, mine, info, gain_out = refs[:4]
    rows_in, length, group, reward, old, ref, sems = refs[4:]
    copies = []
    for i, (src, dst) in enumerate(
        (
            (lengths, length),
            (hidden, rows_in),
            (old_logp, old),
            (ref_logp, ref),
            (group_of, group),
            (rewards, reward),
            (gain, gain_out),
        )
    ):
        copies.append(pltpu.make_async_copy(src, dst, sems.at[i]))
        copies[-1].start()
    a = lax.axis_index("sec")
    t = lax.axis_index("tp")
    n_class = n_sec * n_tp
    rows = rows_in.shape[0]
    n_resp = length.shape[0]
    total = pick.shape[0]
    slots = total // n_sec
    place = iota((total, rows), 0)
    index = mod(place, slots) * n_class + (div(place, slots) ^ a) * n_tp + t
    copies[0].wait()
    source, finish = index, 0
    for r in range(n_resp):
        finish = finish + length[r]
        source = source + jnp.where(index >= finish, LMAX - length[r], 0)
    source = jnp.where(index < finish, source, -1)
    chosen = (iota((total, rows), 1) == source).astype(BF16)
    pick[...] = chosen
    for copy in copies[1:]:
        copy.wait()
    mine[...] = jnp.dot(chosen, rows_in[...], preferred_element_type=F32).astype(BF16)
    log_ratio = ref[...] - old[...]
    penalty = jnp.exp(log_ratio) - log_ratio - 1.0
    lane = iota((1, LANES), 1)
    words = jnp.zeros((1, LANES), F32)
    for r in range(n_resp):
        for i, held in enumerate((length, group, reward)):
            words = jnp.where(lane == i * n_resp + r, held[r].astype(F32), words)
    n_pen = penalty.shape[0]
    filler = jnp.zeros((info.shape[0] - n_pen - 1, LANES), F32)
    info[...] = jnp.concatenate([penalty, words, filler], axis=0).astype(BF16)


def spread_kernel(n_tp, pick, mine, sibling, *outs):
    t = lax.axis_index("tp")
    slots, width = outs[0].shape[0], mine.shape[1]
    own = mine[...].astype(F32)
    other = jnp.dot(pick[...], sibling[...], preferred_element_type=F32)
    first = jnp.where(t == 0, own, other).astype(BF16)
    second = jnp.where(t == 0, other, own).astype(BF16)
    for k, out in enumerate(outs):
        out[:, 0:width] = first[k * slots : (k + 1) * slots]
        out[:, width : 2 * width] = second[k * slots : (k + 1) * slots]


def in_order(order, refs):
    return [refs[order.index(k)] for k in range(len(order))]


def norm_kernel(n, gain, info, *refs):
    inputs, outs, held = refs[:n], refs[2 * n - 1 : n - 1 : -1], refs[2 * n]
    a = lax.axis_index("sec")
    s = lax.axis_index("seq")
    slots, width = inputs[0].shape
    squares = 0.0
    for ref in inputs:
        x = ref[...].astype(F32)
        squares = squares + jnp.sum(x * x, axis=1, keepdims=True)
    scale = lax.rsqrt(squares / D + EPS)
    for k, ref in enumerate(inputs):
        start = pl.multiple_of((a ^ k) * width, LANES)
        held[k] = (ref[...].astype(F32) * scale * gain[:, pl.ds(start, width)]).astype(BF16)
    for m, out in enumerate(outs):
        for h in range(slots // INFO):
            out[:, h * width : (h + 1) * width] = held[a ^ s ^ m, h * INFO : (h + 1) * INFO, :]
        out[:, out.shape[1] - LANES :] = info[...]


def info_of(ref):
    return ref[:, ref.shape[1] - LANES :].astype(F32)


def word_sum(block, row, first, last):
    lane = iota(block.shape, 1)
    inside = (iota(block.shape, 0) == row) & (lane >= first) & (lane < last)
    return jnp.sum(jnp.where(inside, block, 0.0)).astype(I32)


def put_counts(moved, row, n_resp, counts):
    s = lax.axis_index("seq")
    for m, ref in enumerate(moved):
        counts[s ^ m] = word_sum(info_of(ref), row, 0, n_resp)


def class_rows(x, c, n_class):
    return div(x - c + n_class - 1, n_class)


def list_place(counts, n, n_class, tok, s, c, seq_of, position, packed):
    span = tok * n // 4
    edges = []
    for j in range(5):
        edge, start = 0, 0
        for b in range(n):
            edge = edge + class_rows(jnp.clip(j * span - start, 0, counts[b]), c, n_class)
            start = start + counts[b]
        edges.append(edge)
    size = [edges[j + 1] - edges[j] for j in range(4)]
    high = div(s, n // 2)
    far_first = jnp.where(high == 0, size[1], size[0])
    far_rows = jnp.where(high == 0, size[1] + size[3], size[0] + size[2])
    near_first = jnp.where(high == 0, size[0], size[1])
    prefix = 0
    before = jnp.zeros_like(position)
    for b in range(n):
        before = jnp.where(seq_of == b, prefix, before)
        prefix = prefix + class_rows(counts[b], c, n_class)
    group = div(packed, span)
    opening = jnp.where(group == 0, edges[0], jnp.where(group == 1, edges[1], jnp.where(group == 2, edges[2], edges[3])))
    within = before + position - opening
    later = group >= 2
    far = mod(group, 2) != high
    far_place = within + jnp.where(later, far_first, 0)
    near_place = far_rows + within + jnp.where(later, near_first, 0)
    return jnp.where(far, far_place, near_place)


def pack_kernel(n, n_class, n_resp, tok, row, *refs):
    moved, (out, held, counts) = in_order(ARRIVALS, refs[:n]), refs[n:]
    s = lax.axis_index("seq")
    c = lax.axis_index("sec") * lax.axis_size("tp") + lax.axis_index("tp")
    width = out.shape[1]
    slots = (moved[0].shape[1] - LANES) // width * INFO
    put_counts(moved, row, n_resp, counts)
    lane = iota((1, n * slots), 1)
    seq_of = div(lane, slots) ^ s
    q = mod(lane, slots)
    live = jnp.zeros(lane.shape, jnp.bool_)
    start = jnp.zeros(lane.shape, I32)
    total = 0
    for b in range(n):
        live = live | ((seq_of == b) & (q < class_rows(counts[b], c, n_class)))
        start = jnp.where(seq_of == b, total, start)
        total = total + counts[b]
    packed = start + q * n_class + c
    place = list_place(counts, n, n_class, tok, s, c, seq_of, q, packed)
    place = jnp.where(live, place, -1)
    for m, ref in enumerate(moved):
        for h in range(slots // INFO):
            first = m * slots + h * INFO
            held[first : first + INFO, :] = ref[:, h * width : (h + 1) * width]
    pick = (iota((out.shape[0], n * slots), 0) == place).astype(BF16)
    out[...] = jnp.dot(pick, held[...], preferred_element_type=F32).astype(BF16)


def upright(x):
    return jnp.transpose(jnp.broadcast_to(x.astype(F32), (LANES, x.shape[1]))).astype(I32)


def one_hot(column, out):
    for j in range(out.shape[1] // LANES):
        out[:, j * LANES : (j + 1) * LANES] = (iota(column.shape, 1) + j * LANES == column).astype(BF16)


def index_kernel(n, n_class, n_resp, tok, row, *refs):
    moved, hidden = in_order(ARRIVALS, refs[:n]), refs[n]
    pick_far, pick_near, rest_far, rest_near, counts, lens, own = refs[n + 1 :]
    a = lax.axis_index("sec")
    s = lax.axis_index("seq")
    t = lax.axis_index("tp")
    n_tp = lax.axis_size("tp")
    put_counts(moved, row, n_resp, counts)
    block = info_of(moved[0])
    for r in range(n_resp):
        lens[r] = word_sum(block, row, r, r + 1)
    half = n // 2 * tok
    for far, pick, rest in ((True, pick_far, rest_far), (False, pick_near, rest_near)):
        lane = iota((1, half), 1)
        w = mod(lane, tok)
        shard = (div(lane, tok) + (n // 2 if far else 0)) ^ s
        packed = div(w, TILE) * (TILE * n) + shard * TILE + mod(w, TILE)
        seq_of = jnp.zeros(lane.shape, I32)
        start = jnp.zeros(lane.shape, I32)
        finish = 0
        for b in range(n):
            finish = finish + counts[b]
            passed = packed >= finish
            seq_of = seq_of + passed.astype(I32)
            start = jnp.where(passed, finish, start)
        index = packed - start
        c = mod(index, n_class)
        place = list_place(counts, n, n_class, tok, s, c, seq_of, div(index, n_class), packed)
        column = ((mod(c, n_tp) ^ t) * n + (div(c, n_tp) ^ a)) * (pick.shape[1] // n_class) + place
        one_hot(upright(column), pick)
        source, ends = index, 0
        for r in range(n_resp):
            ends = ends + lens[r]
            source = source + jnp.where(index >= ends, LMAX - lens[r], 0)
        one_hot(upright(jnp.where(seq_of == s, source, -1)), own)
        rest[...] = jnp.dot(own[...], hidden[...], preferred_element_type=F32)


def mix_kernel(n_lists, pick, rest, projection, *refs):
    pieces, outs, held = refs[:n_lists], refs[n_lists:-1], refs[-1]
    listed, step = pieces[0].shape[0], held.shape[0] // n_lists
    for k, piece in enumerate(pieces):
        rows = piece[0 : min(step, listed), :].astype(F32)
        if step > listed:
            rows = jnp.concatenate([rows, jnp.zeros((step - listed, rows.shape[1]), F32)], axis=0)
        held[k * step : (k + 1) * step, :] = rows.astype(BF16)
    tokens = jnp.dot(pick[...], held[...], preferred_element_type=F32).astype(BF16)
    total = jnp.dot(tokens, projection[...], preferred_element_type=F32) + rest[...]
    first = 0
    for out in outs:
        out[...] = total[first : first + out.shape[0]].astype(out.dtype)
        first += out.shape[0]


def join_kernel(own, other, out):
    out[...] = (own[...] + other[...].astype(F32)).astype(out.dtype)


def final_kernel(n_whole, n_first, *refs):
    own, parts, out = refs[0], refs[1:-1], refs[-1]
    half = out.shape[0] // 2
    total = own[...]
    for part in parts[:n_whole]:
        total = total + part[...].astype(F32)
    first, second = total[0:half], total[half:]
    for part in parts[n_whole : n_whole + n_first]:
        first = first + part[...].astype(F32)
    for part in parts[n_whole + n_first :]:
        second = second + part[...].astype(F32)
    out[0:half] = first.astype(out.dtype)
    out[half:] = second.astype(out.dtype)


def terms_kernel(n, n_resp, row, *refs):
    moved, out, words, table = in_order(ARRIVALS, refs[:n]), refs[n], refs[n + 1], refs[n + 2]
    s = lax.axis_index("seq")
    tok = out.shape[1]
    group_count = n * n_resp // GROUP
    for m, ref in enumerate(moved):
        block = info_of(ref)
        table[pl.ds((s ^ m) * INFO, INFO), :] = block
        for r in range(3 * n_resp):
            words[s ^ m, r] = word_sum(block, row, r, r + 1)
    w = iota((1, tok), 1)
    packed = div(w, TILE) * (TILE * n) + s * TILE + mod(w, TILE)
    source, finish = packed, 0
    reward = jnp.zeros((1, tok), F32)
    group = jnp.zeros((1, tok), I32)
    total = [0] * group_count
    square = [0] * group_count
    for b in range(n):
        for r in range(n_resp):
            length, number, gain = words[b, r], words[b, n_resp + r], words[b, 2 * n_resp + r]
            within = packed >= finish
            reward = jnp.where(within, gain.astype(F32), reward)
            group = jnp.where(within, number, group)
            finish = finish + length
            source = source + jnp.where(packed >= finish, LMAX - length, 0)
            for g in range(group_count):
                total[g] = total[g] + jnp.where(number == g, gain, 0)
                square[g] = square[g] + jnp.where(number == g, gain * gain, 0)
    total_of = jnp.zeros((1, tok), F32)
    square_of = jnp.zeros((1, tok), F32)
    for g in range(group_count):
        total_of = jnp.where(group == g, total[g].astype(F32), total_of)
        square_of = jnp.where(group == g, square[g].astype(F32), square_of)
    mean = total_of / GROUP
    spread = jnp.maximum(jnp.sqrt(square_of / GROUP - mean * mean), 1.0)
    advantage = (reward - mean) / spread
    pick = (iota((LANES, tok), 0) == mod(source, LANES)).astype(BF16)
    found = jnp.dot(table[...].astype(BF16), pick, preferred_element_type=F32)
    line = div(source, LANES)
    chosen = iota(found.shape, 0) == div(line, row) * INFO + mod(line, row)
    penalty = jnp.sum(jnp.where(chosen, found, 0.0), axis=0, keepdims=True)
    out[0:1, :] = advantage
    out[1:2, :] = penalty


def call(kernel, out_shape, in_specs, out_specs, scratch=()):
    return pl.pallas_call(
        kernel,
        out_shape=out_shape,
        in_specs=in_specs,
        out_specs=out_specs,
        scratch_shapes=list(scratch),
        compiler_params=pltpu.CompilerParams(vmem_limit_bytes=48 * 1024 * 1024),
    )


def shards_in_place(hidden, projection, norm_gain, old_logp, ref_logp, lengths, group_of, rewards):
    n = lax.axis_size("seq")
    n_tp = lax.axis_size("tp")
    n_class = n * n_tp
    rows, cols = hidden.shape
    n_resp = lengths.shape[0]
    width = cols * n_tp
    slots = rows // n_class
    row = rows // LANES
    tok = TOK_DEV
    tokens = tok * n
    up = lambda x, m: -(-x // m) * m
    listed = up((tokens + (n_class - 1) * n) // n_class, 8)
    far_rows = up((tokens // 2 + (n_class - 1) * (n + 1)) // n_class, 16)
    shape = jax.ShapeDtypeStruct
    info_like = shape((INFO, slots // INFO * width + LANES), BF16)

    sibling = swap(hidden, "tp", 1)
    pick, mine, info, gain = call(
        functools.partial(early_kernel, n, n_tp),
        [
            shape((rows // n_tp, rows), BF16),
            shape((rows // n_tp, cols), BF16),
            shape((INFO, LANES), BF16),
            shape((1, D), F32),
        ],
        [HBM] * 7,
        [VMEM] * 4,
        [
            pltpu.VMEM((rows, cols), BF16),
            pltpu.SMEM((n_resp,), I32),
            pltpu.SMEM((n_resp,), I32),
            pltpu.SMEM((n_resp,), I32),
            pltpu.VMEM((row, LANES), F32),
            pltpu.VMEM((row, LANES), F32),
            pltpu.SemaphoreType.DMA((7,)),
        ],
    )(
        *(
            pltpu.with_memory_space_constraint(x, pltpu.HBM)
            for x in (
                hidden,
                lengths,
                group_of,
                rewards,
                old_logp.reshape(row, LANES),
                ref_logp.reshape(row, LANES),
                norm_gain.reshape(1, D),
            )
        )
    )
    dealt = call(
        functools.partial(spread_kernel, n_tp), [shape((slots, width), BF16)] * n, [VMEM] * 3, [VMEM] * n
    )(pick, mine, sibling)
    whole = [dealt[0]] + [swap(dealt[k], "sec", k) for k in range(1, n)]
    normed = call(
        functools.partial(norm_kernel, n),
        [info_like] * n,
        [VMEM] * (n + 2),
        [VMEM] * n,
        [pltpu.VMEM((n, slots, width), BF16)],
    )(gain, info, *whole)[::-1]
    moved = [normed[0]] + [swap(normed[m], "seq", m) for m in range(n - 1, 0, -1)][::-1]
    mine = call(
        functools.partial(pack_kernel, n, n_class, n_resp, tok, row),
        shape((listed, width), BF16),
        [VMEM] * n,
        VMEM,
        [pltpu.VMEM((n * slots, width), BF16), pltpu.SMEM((n,), I32)],
    )(*(moved[m] for m in ARRIVALS))
    half = n // 2 * tok
    pick_far, pick_near, rest_far, rest_near = call(
        functools.partial(index_kernel, n, n_class, n_resp, tok, row),
        [
            shape((half, n_class * far_rows), BF16),
            shape((half, n_class * up(listed, 16)), BF16),
            shape((half, cols), F32),
            shape((half, cols), F32),
        ],
        [VMEM] * (n + 1),
        [VMEM] * 4,
        [pltpu.SMEM((n,), I32), pltpu.SMEM((n_resp,), I32), pltpu.VMEM((half, rows), BF16)],
    )(*(moved[m] for m in ARRIVALS), hidden)
    terms = call(
        functools.partial(terms_kernel, n, n_resp, row),
        shape((2, tok), F32),
        [VMEM] * n,
        VMEM,
        [pltpu.SMEM((n, 3 * n_resp), I32), pltpu.VMEM((n * INFO, LANES), F32)],
    )(*(moved[m] for m in ARRIVALS))
    after = lambda x, *ys: lax.optimization_barrier((x, *ys))[0]
    same = [mine] + [swap(mine, "sec", k) for k in range(1, n)]
    lists = same + [swap(after(x, pick_far, terms), "tp", 1) for x in same]
    mix = lambda pick, rest, outs: call(
        functools.partial(mix_kernel, n_class),
        outs,
        [VMEM] * (n_class + 3),
        [VMEM] * len(outs),
        [pltpu.VMEM((pick.shape[1], width), BF16)],
    )(pick, rest, projection, *lists)
    part = tok // 2
    joined = n // 2
    far = mix(
        pick_far,
        rest_far,
        [shape((part, cols), F32 if m % 2 and h else BF16) for m in range(joined) for h in range(2)],
    )
    helped = [swap(far[2 * m + 1], "seq", 1) for m in range(0, joined, 2)]
    sums = [
        call(join_kernel, shape((part, cols), BF16), [VMEM] * 2, VMEM)(far[2 * m + 3], got)
        for m, got in zip(range(0, joined, 2), helped, strict=True)
    ]
    passed = [swap(x, "seq", joined + m + 1) for m, x in zip(range(0, joined, 2), sums, strict=True)]
    near = mix(
        after(pick_near, *far), rest_near, [shape((tok, cols), F32)] + [shape((tok, cols), BF16)] * (joined - 1)
    )
    direct = [swap(far[0], "seq", joined)] + [
        swap(after(far[2 * m], *near), "seq", joined + m) for m in range(1, joined)
    ]
    whole = [swap(near[m], "seq", m) for m in range(1, joined)]
    states = call(
        functools.partial(final_kernel, len(whole), len(direct)),
        shape((tok, cols), BF16),
        [VMEM] * (1 + len(whole) + len(direct) + len(passed)),
        VMEM,
    )(near[0], *whole, *direct, *passed)
    return states, terms.astype(BF16).T


def refine(input_rows, projection, norm_gain):
    widened = input_rows.astype(jnp.float32)
    full_rows = lax.all_gather(input_rows, ("sec", "tp"), axis=1, tiled=True).astype(jnp.float32)
    squares = jnp.sum(full_rows * full_rows, axis=1, keepdims=True)
    normed = (full_rows * lax.rsqrt(squares / D + 1e-06) * norm_gain).astype(jnp.bfloat16)
    mixing = jnp.dot(
        normed,
        lax.all_gather(projection, "seq", axis=0, tiled=True),
        preferred_element_type=jnp.float32,
    )
    return (widened + mixing).astype(jnp.bfloat16)


def deliver(
    input_rows, token_terms, lengths, first_index, own_total, starts, seq_index, tile_rows, n_seq
):
    slot_count = input_rows.shape[0]
    slot_index = jnp.arange(slot_count, dtype=jnp.int32)
    offset = jnp.mod(slot_index - first_index, slot_count)
    filled = offset < own_total
    finish = jnp.cumsum(lengths)
    response = jnp.sum((finish[None, :] <= offset[:, None]).astype(jnp.int32), axis=1)
    response = jnp.minimum(response, lengths.shape[0] - 1)
    opening = jnp.take(finish - lengths, response)
    source = jnp.where(filled, response * LMAX + offset - opening, 0)
    send_rows = jnp.where(
        filled[:, None], jnp.take(input_rows, source, axis=0), jnp.zeros((), input_rows.dtype)
    )
    send_terms = jnp.where(
        filled[:, None], jnp.take(token_terms, source, axis=0), jnp.zeros((), token_terms.dtype)
    )
    arrived, arrived_terms = (
        lax.all_to_all(
            send_rows.reshape(n_seq, tile_rows, -1), "seq", split_axis=0, concat_axis=0, tiled=True
        ),
        lax.all_to_all(
            send_terms.reshape(n_seq, tile_rows, 2), "seq", split_axis=0, concat_axis=0, tiled=True
        ),
    )
    learner_row = jnp.arange(TOK_DEV, dtype=jnp.int32)
    packed = learner_row // tile_rows * slot_count + seq_index * tile_rows + learner_row % tile_rows
    sender = jnp.sum((starts[None, :] <= packed[:, None]).astype(jnp.int32), axis=1) - 1
    pick_index = sender * tile_rows + learner_row % tile_rows
    states = jnp.take(arrived.reshape(slot_count, -1), pick_index, axis=0)
    moved_terms = jnp.take(arrived_terms.reshape(slot_count, 2), pick_index, axis=0)
    return (states, moved_terms)


def shards(hidden, projection, norm_gain, old_logp, ref_logp, lengths, group_of, rewards):
    n_seq = lax.axis_size("seq")
    seq_index = lax.axis_index("seq")
    tile_rows = SLOTS // n_seq
    group_count = RESP_DEV * n_seq // GROUP
    member_table = (group_of[:, None] == jnp.arange(group_count, dtype=jnp.int32)[None, :]).astype(
        jnp.float32
    )
    reward_value = rewards.astype(jnp.float32)
    partial_value = jnp.stack(
        [
            jnp.dot(reward_value, member_table, precision=lax.Precision.HIGHEST),
            jnp.dot(reward_value * reward_value, member_table, precision=lax.Precision.HIGHEST),
        ]
    )
    own_total = jnp.sum(lengths)
    group_sums = lax.psum(partial_value, "seq")
    counts = lax.all_gather(jnp.reshape(own_total, (1,)), "seq", axis=0, tiled=True)
    group_mean = group_sums[0] / GROUP
    spread = jnp.maximum(jnp.sqrt(group_sums[1] / GROUP - group_mean * group_mean), 1.0)
    advantage = (
        reward_value - jnp.dot(member_table, group_mean, precision=lax.Precision.HIGHEST)
    ) / jnp.dot(member_table, spread, precision=lax.Precision.HIGHEST)
    log_ratio = ref_logp - old_logp
    penalty = jnp.exp(log_ratio) - log_ratio - 1.0
    token_terms = jnp.stack([jnp.repeat(advantage, LMAX), penalty], axis=1).astype(jnp.bfloat16)
    starts = jnp.cumsum(counts) - counts
    first_index = jnp.take(starts, seq_index)
    refined = refine(hidden, projection, norm_gain)
    return deliver(
        refined, token_terms, lengths, first_index, own_total, starts, seq_index, tile_rows, n_seq
    )


def solution(mesh):
    in_specs = (
        P("seq", ("sec", "tp")),
        P("seq", ("sec", "tp")),
        P(),
        P("seq"),
        P("seq"),
        P("seq"),
        P("seq"),
        P("seq"),
    )
    out_specs = (P("seq", ("sec", "tp")), P("seq", None))
    n = mesh.shape["seq"]
    in_place = mesh.shape["sec"] == n and n >= 4 and n & (n - 1) == 0
    body = shards_in_place if in_place else shards
    return jax.shard_map(body, mesh=mesh, in_specs=in_specs, out_specs=out_specs, check_vma=False)
```

```python
import functools

import jax
import jax.numpy as jnp
from jax import lax
from jax.experimental import pallas as pl
from jax.experimental.pallas import tpu as pltpu
from jax.sharding import PartitionSpec as P

D = 5120
TOK_DEV = 128
RESP_DEV = 4
GROUP = 8
LMAX = 64
TILE = 64
SLOTS = 256
EPS = 1e-06
BF16 = jnp.bfloat16
F32 = jnp.float32
I32 = jnp.int32
LANES = 128
INFO = 16
ARRIVALS = (2, 1, 3, 0)

VMEM = pl.BlockSpec(memory_space=pltpu.VMEM)
SMEM = pl.BlockSpec(memory_space=pltpu.SMEM)
HBM = pl.BlockSpec(memory_space=pltpu.HBM)


def iota(shape, dim):
    return lax.broadcasted_iota(I32, shape, dim)


def bits(n):
    return n.bit_length() - 1


def div(x, n):
    return lax.shift_right_arithmetic(x, jnp.full(jnp.shape(x), bits(n), I32))


def mod(x, n):
    return x & (n - 1)


def swap(x, axis, k):
    n = lax.axis_size(axis)
    return lax.ppermute(x, axis, [(i, i ^ k) for i in range(n)])


def early_kernel(n_sec, n_tp, hidden, lengths, group_of, rewards, old_logp, ref_logp, gain, *refs):
    pick, mine, info, gain_out = refs[:4]
    rows_in, length, group, reward, old, ref, sems = refs[4:]
    copies = []
    for i, (src, dst) in enumerate(
        (
            (lengths, length),
            (hidden, rows_in),
            (old_logp, old),
            (ref_logp, ref),
            (group_of, group),
            (rewards, reward),
            (gain, gain_out),
        )
    ):
        copies.append(pltpu.make_async_copy(src, dst, sems.at[i]))
        copies[-1].start()
    a = lax.axis_index("sec")
    t = lax.axis_index("tp")
    n_class = n_sec * n_tp
    rows = rows_in.shape[0]
    n_resp = length.shape[0]
    total = pick.shape[0]
    slots = total // n_sec
    place = iota((total, rows), 0)
    index = mod(place, slots) * n_class + (div(place, slots) ^ a) * n_tp + t
    copies[0].wait()
    source, finish = index, 0
    for r in range(n_resp):
        finish = finish + length[r]
        source = source + jnp.where(index >= finish, LMAX - length[r], 0)
    source = jnp.where(index < finish, source, -1)
    chosen = (iota((total, rows), 1) == source).astype(BF16)
    pick[...] = chosen
    for copy in copies[1:]:
        copy.wait()
    mine[...] = jnp.dot(chosen, rows_in[...], preferred_element_type=F32).astype(BF16)
    log_ratio = ref[...] - old[...]
    penalty = jnp.exp(log_ratio) - log_ratio - 1.0
    lane = iota((1, LANES), 1)
    words = jnp.zeros((1, LANES), F32)
    for r in range(n_resp):
        for i, held in enumerate((length, group, reward)):
            words = jnp.where(lane == i * n_resp + r, held[r].astype(F32), words)
    n_pen = penalty.shape[0]
    filler = jnp.zeros((info.shape[0] - n_pen - 1, LANES), F32)
    info[...] = jnp.concatenate([penalty, words, filler], axis=0).astype(BF16)


def spread_kernel(n_tp, pick, mine, sibling, *outs):
    t = lax.axis_index("tp")
    slots, width = outs[0].shape[0], mine.shape[1]
    own = mine[...].astype(F32)
    other = jnp.dot(pick[...], sibling[...], preferred_element_type=F32)
    first = jnp.where(t == 0, own, other).astype(BF16)
    second = jnp.where(t == 0, other, own).astype(BF16)
    for k, out in enumerate(outs):
        out[:, 0:width] = first[k * slots : (k + 1) * slots]
        out[:, width : 2 * width] = second[k * slots : (k + 1) * slots]


def in_order(order, refs):
    return [refs[order.index(k)] for k in range(len(order))]


def norm_kernel(n, gain, info, *refs):
    inputs, outs, held = refs[:n], refs[2 * n - 1 : n - 1 : -1], refs[2 * n]
    a = lax.axis_index("sec")
    s = lax.axis_index("seq")
    slots, width = inputs[0].shape
    squares = 0.0
    for ref in inputs:
        x = ref[...].astype(F32)
        squares = squares + jnp.sum(x * x, axis=1, keepdims=True)
    scale = lax.rsqrt(squares / D + EPS)
    for k, ref in enumerate(inputs):
        start = pl.multiple_of((a ^ k) * width, LANES)
        held[k] = (ref[...].astype(F32) * scale * gain[:, pl.ds(start, width)]).astype(BF16)
    for m, out in enumerate(outs):
        for h in range(slots // INFO):
            out[:, h * width : (h + 1) * width] = held[a ^ s ^ m, h * INFO : (h + 1) * INFO, :]
        out[:, out.shape[1] - LANES :] = info[...]


def info_of(ref):
    return ref[:, ref.shape[1] - LANES :].astype(F32)


def word_sum(block, row, first, last):
    lane = iota(block.shape, 1)
    inside = (iota(block.shape, 0) == row) & (lane >= first) & (lane < last)
    return jnp.sum(jnp.where(inside, block, 0.0)).astype(I32)


def put_counts(moved, row, n_resp, counts):
    s = lax.axis_index("seq")
    for m, ref in enumerate(moved):
        counts[s ^ m] = word_sum(info_of(ref), row, 0, n_resp)


def class_rows(x, c, n_class):
    return div(x - c + n_class - 1, n_class)


def list_place(counts, n, n_class, tok, s, c, seq_of, position, packed):
    span = tok * n // 4
    edges = []
    for j in range(5):
        edge, start = 0, 0
        for b in range(n):
            edge = edge + class_rows(jnp.clip(j * span - start, 0, counts[b]), c, n_class)
            start = start + counts[b]
        edges.append(edge)
    size = [edges[j + 1] - edges[j] for j in range(4)]
    high = div(s, n // 2)
    far_first = jnp.where(high == 0, size[1], size[0])
    far_rows = jnp.where(high == 0, size[1] + size[3], size[0] + size[2])
    near_first = jnp.where(high == 0, size[0], size[1])
    prefix = 0
    before = jnp.zeros_like(position)
    for b in range(n):
        before = jnp.where(seq_of == b, prefix, before)
        prefix = prefix + class_rows(counts[b], c, n_class)
    group = div(packed, span)
    opening = jnp.where(group == 0, edges[0], jnp.where(group == 1, edges[1], jnp.where(group == 2, edges[2], edges[3])))
    within = before + position - opening
    later = group >= 2
    far = mod(group, 2) != high
    far_place = within + jnp.where(later, far_first, 0)
    near_place = far_rows + within + jnp.where(later, near_first, 0)
    return jnp.where(far, far_place, near_place)


def pack_kernel(n, n_class, n_resp, tok, row, *refs):
    moved, (out, held, counts) = in_order(ARRIVALS, refs[:n]), refs[n:]
    s = lax.axis_index("seq")
    c = lax.axis_index("sec") * lax.axis_size("tp") + lax.axis_index("tp")
    width = out.shape[1]
    slots = (moved[0].shape[1] - LANES) // width * INFO
    put_counts(moved, row, n_resp, counts)
    lane = iota((1, n * slots), 1)
    seq_of = div(lane, slots) ^ s
    q = mod(lane, slots)
    live = jnp.zeros(lane.shape, jnp.bool_)
    start = jnp.zeros(lane.shape, I32)
    total = 0
    for b in range(n):
        live = live | ((seq_of == b) & (q < class_rows(counts[b], c, n_class)))
        start = jnp.where(seq_of == b, total, start)
        total = total + counts[b]
    packed = start + q * n_class + c
    place = list_place(counts, n, n_class, tok, s, c, seq_of, q, packed)
    place = jnp.where(live, place, -1)
    for m, ref in enumerate(moved):
        for h in range(slots // INFO):
            first = m * slots + h * INFO
            held[first : first + INFO, :] = ref[:, h * width : (h + 1) * width]
    pick = (iota((out.shape[0], n * slots), 0) == place).astype(BF16)
    out[...] = jnp.dot(pick, held[...], preferred_element_type=F32).astype(BF16)


def upright(x):
    return jnp.transpose(jnp.broadcast_to(x.astype(F32), (LANES, x.shape[1]))).astype(I32)


def one_hot(column, out):
    for j in range(out.shape[1] // LANES):
        out[:, j * LANES : (j + 1) * LANES] = (iota(column.shape, 1) + j * LANES == column).astype(BF16)


def index_kernel(n, n_class, n_resp, tok, row, *refs):
    moved, hidden = in_order(ARRIVALS, refs[:n]), refs[n]
    pick_far, pick_near, rest_far, rest_near, counts, lens, own = refs[n + 1 :]
    a = lax.axis_index("sec")
    s = lax.axis_index("seq")
    t = lax.axis_index("tp")
    n_tp = lax.axis_size("tp")
    put_counts(moved, row, n_resp, counts)
    block = info_of(moved[0])
    for r in range(n_resp):
        lens[r] = word_sum(block, row, r, r + 1)
    half = n // 2 * tok
    for far, pick, rest in ((True, pick_far, rest_far), (False, pick_near, rest_near)):
        lane = iota((1, half), 1)
        w = mod(lane, tok)
        shard = (div(lane, tok) + (n // 2 if far else 0)) ^ s
        packed = div(w, TILE) * (TILE * n) + shard * TILE + mod(w, TILE)
        seq_of = jnp.zeros(lane.shape, I32)
        start = jnp.zeros(lane.shape, I32)
        finish = 0
        for b in range(n):
            finish = finish + counts[b]
            passed = packed >= finish
            seq_of = seq_of + passed.astype(I32)
            start = jnp.where(passed, finish, start)
        index = packed - start
        c = mod(index, n_class)
        place = list_place(counts, n, n_class, tok, s, c, seq_of, div(index, n_class), packed)
        column = ((mod(c, n_tp) ^ t) * n + (div(c, n_tp) ^ a)) * (pick.shape[1] // n_class) + place
        one_hot(upright(column), pick)
        source, ends = index, 0
        for r in range(n_resp):
            ends = ends + lens[r]
            source = source + jnp.where(index >= ends, LMAX - lens[r], 0)
        one_hot(upright(jnp.where(seq_of == s, source, -1)), own)
        rest[...] = jnp.dot(own[...], hidden[...], preferred_element_type=F32)


def mix_kernel(n_lists, pick, rest, projection, *refs):
    pieces, outs, held = refs[:n_lists], refs[n_lists:-1], refs[-1]
    listed, step = pieces[0].shape[0], held.shape[0] // n_lists
    for k, piece in enumerate(pieces):
        rows = piece[0 : min(step, listed), :].astype(F32)
        if step > listed:
            rows = jnp.concatenate([rows, jnp.zeros((step - listed, rows.shape[1]), F32)], axis=0)
        held[k * step : (k + 1) * step, :] = rows.astype(BF16)
    tokens = jnp.dot(pick[...], held[...], preferred_element_type=F32).astype(BF16)
    total = jnp.dot(tokens, projection[...], preferred_element_type=F32) + rest[...]
    first = 0
    for out in outs:
        out[...] = total[first : first + out.shape[0]].astype(out.dtype)
        first += out.shape[0]


def join_kernel(own, other, out):
    out[...] = (own[...] + other[...].astype(F32)).astype(out.dtype)


def final_kernel(n_whole, n_first, *refs):
    own, parts, out = refs[0], refs[1:-1], refs[-1]
    half = out.shape[0] // 2
    total = own[...]
    for part in parts[:n_whole]:
        total = total + part[...].astype(F32)
    first, second = total[0:half], total[half:]
    for part in parts[n_whole : n_whole + n_first]:
        first = first + part[...].astype(F32)
    for part in parts[n_whole + n_first :]:
        second = second + part[...].astype(F32)
    out[0:half] = first.astype(out.dtype)
    out[half:] = second.astype(out.dtype)


def terms_kernel(n, n_resp, row, *refs):
    moved, out, words, table = in_order(ARRIVALS, refs[:n]), refs[n], refs[n + 1], refs[n + 2]
    s = lax.axis_index("seq")
    tok = out.shape[1]
    group_count = n * n_resp // GROUP
    for m, ref in enumerate(moved):
        block = info_of(ref)
        table[pl.ds((s ^ m) * INFO, INFO), :] = block
        for r in range(3 * n_resp):
            words[s ^ m, r] = word_sum(block, row, r, r + 1)
    w = iota((1, tok), 1)
    packed = div(w, TILE) * (TILE * n) + s * TILE + mod(w, TILE)
    source, finish = packed, 0
    reward = jnp.zeros((1, tok), F32)
    group = jnp.zeros((1, tok), I32)
    total = [0] * group_count
    square = [0] * group_count
    for b in range(n):
        for r in range(n_resp):
            length, number, gain = words[b, r], words[b, n_resp + r], words[b, 2 * n_resp + r]
            within = packed >= finish
            reward = jnp.where(within, gain.astype(F32), reward)
            group = jnp.where(within, number, group)
            finish = finish + length
            source = source + jnp.where(packed >= finish, LMAX - length, 0)
            for g in range(group_count):
                total[g] = total[g] + jnp.where(number == g, gain, 0)
                square[g] = square[g] + jnp.where(number == g, gain * gain, 0)
    total_of = jnp.zeros((1, tok), F32)
    square_of = jnp.zeros((1, tok), F32)
    for g in range(group_count):
        total_of = jnp.where(group == g, total[g].astype(F32), total_of)
        square_of = jnp.where(group == g, square[g].astype(F32), square_of)
    mean = total_of / GROUP
    spread = jnp.maximum(jnp.sqrt(square_of / GROUP - mean * mean), 1.0)
    advantage = (reward - mean) / spread
    pick = (iota((LANES, tok), 0) == mod(source, LANES)).astype(BF16)
    found = jnp.dot(table[...].astype(BF16), pick, preferred_element_type=F32)
    line = div(source, LANES)
    chosen = iota(found.shape, 0) == div(line, row) * INFO + mod(line, row)
    penalty = jnp.sum(jnp.where(chosen, found, 0.0), axis=0, keepdims=True)
    out[0:1, :] = advantage
    out[1:2, :] = penalty


def call(kernel, out_shape, in_specs, out_specs, scratch=()):
    return pl.pallas_call(
        kernel,
        out_shape=out_shape,
        in_specs=in_specs,
        out_specs=out_specs,
        scratch_shapes=list(scratch),
        compiler_params=pltpu.CompilerParams(vmem_limit_bytes=48 * 1024 * 1024),
    )


def shards_in_place(hidden, projection, norm_gain, old_logp, ref_logp, lengths, group_of, rewards):
    n = lax.axis_size("seq")
    n_tp = lax.axis_size("tp")
    n_class = n * n_tp
    rows, cols = hidden.shape
    n_resp = lengths.shape[0]
    width = cols * n_tp
    slots = rows // n_class
    row = rows // LANES
    tok = TOK_DEV
    tokens = tok * n
    up = lambda x, m: -(-x // m) * m
    listed = up((tokens + (n_class - 1) * n) // n_class, 16)
    far_rows = up((tokens // 2 + (n_class - 1) * (n + 1)) // n_class, 16)
    shape = jax.ShapeDtypeStruct
    info_like = shape((INFO, slots // INFO * width + LANES), BF16)

    sibling = swap(hidden, "tp", 1)
    pick, mine, info, gain = call(
        functools.partial(early_kernel, n, n_tp),
        [
            shape((rows // n_tp, rows), BF16),
            shape((rows // n_tp, cols), BF16),
            shape((INFO, LANES), BF16),
            shape((1, D), F32),
        ],
        [HBM] * 7,
        [VMEM] * 4,
        [
            pltpu.VMEM((rows, cols), BF16),
            pltpu.SMEM((n_resp,), I32),
            pltpu.SMEM((n_resp,), I32),
            pltpu.SMEM((n_resp,), I32),
            pltpu.VMEM((row, LANES), F32),
            pltpu.VMEM((row, LANES), F32),
            pltpu.SemaphoreType.DMA((7,)),
        ],
    )(
        *(
            pltpu.with_memory_space_constraint(x, pltpu.HBM)
            for x in (
                hidden,
                lengths,
                group_of,
                rewards,
                old_logp.reshape(row, LANES),
                ref_logp.reshape(row, LANES),
                norm_gain.reshape(1, D),
            )
        )
    )
    dealt = call(
        functools.partial(spread_kernel, n_tp), [shape((slots, width), BF16)] * n, [VMEM] * 3, [VMEM] * n
    )(pick, mine, sibling)
    whole = [dealt[0]] + [swap(dealt[k], "sec", k) for k in range(1, n)]
    normed = call(
        functools.partial(norm_kernel, n),
        [info_like] * n,
        [VMEM] * (n + 2),
        [VMEM] * n,
        [pltpu.VMEM((n, slots, width), BF16)],
    )(gain, info, *whole)[::-1]
    moved = [normed[0]] + [swap(normed[m], "seq", m) for m in range(n - 1, 0, -1)][::-1]
    mine = call(
        functools.partial(pack_kernel, n, n_class, n_resp, tok, row),
        shape((listed, width), BF16),
        [VMEM] * n,
        VMEM,
        [pltpu.VMEM((n * slots, width), BF16), pltpu.SMEM((n,), I32)],
    )(*(moved[m] for m in ARRIVALS))
    half = n // 2 * tok
    pick_far, pick_near, rest_far, rest_near = call(
        functools.partial(index_kernel, n, n_class, n_resp, tok, row),
        [
            shape((half, n_class * far_rows), BF16),
            shape((half, n_class * up(listed, 16)), BF16),
            shape((half, cols), F32),
            shape((half, cols), F32),
        ],
        [VMEM] * (n + 1),
        [VMEM] * 4,
        [pltpu.SMEM((n,), I32), pltpu.SMEM((n_resp,), I32), pltpu.VMEM((half, rows), BF16)],
    )(*(moved[m] for m in ARRIVALS), hidden)
    terms = call(
        functools.partial(terms_kernel, n, n_resp, row),
        shape((2, tok), F32),
        [VMEM] * n,
        VMEM,
        [pltpu.SMEM((n, 3 * n_resp), I32), pltpu.VMEM((n * INFO, LANES), F32)],
    )(*(moved[m] for m in ARRIVALS))
    after = lambda x, *ys: lax.optimization_barrier((x, *ys))[0]
    same = [mine] + [swap(mine, "sec", k) for k in range(1, n)]
    lists = same + [swap(after(x, pick_far, terms), "tp", 1) for x in same]
    mix = lambda pick, rest, outs: call(
        functools.partial(mix_kernel, n_class),
        outs,
        [VMEM] * (n_class + 3),
        [VMEM] * len(outs),
        [pltpu.VMEM((pick.shape[1], width), BF16)],
    )(pick, rest, projection, *lists)
    part = tok // 2
    joined = n // 2
    far = mix(
        pick_far,
        rest_far,
        [shape((part, cols), F32 if m % 2 and h else BF16) for m in range(joined) for h in range(2)],
    )
    helped = [swap(far[2 * m + 1], "seq", 1) for m in range(0, joined, 2)]
    sums = [
        call(join_kernel, shape((part, cols), BF16), [VMEM] * 2, VMEM)(far[2 * m + 3], got)
        for m, got in zip(range(0, joined, 2), helped, strict=True)
    ]
    passed = [swap(x, "seq", joined + m + 1) for m, x in zip(range(0, joined, 2), sums, strict=True)]
    near = mix(
        after(pick_near, *far), rest_near, [shape((tok, cols), F32)] + [shape((tok, cols), BF16)] * (joined - 1)
    )
    direct = [swap(far[0], "seq", joined)] + [
        swap(after(far[2 * m], *near), "seq", joined + m) for m in range(1, joined)
    ]
    whole = [swap(near[m], "seq", m) for m in range(1, joined)]
    states = call(
        functools.partial(final_kernel, len(whole), len(direct)),
        shape((tok, cols), BF16),
        [VMEM] * (1 + len(whole) + len(direct) + len(passed)),
        VMEM,
    )(near[0], *whole, *direct, *passed)
    return states, terms.astype(BF16).T


def refine(input_rows, projection, norm_gain):
    widened = input_rows.astype(jnp.float32)
    full_rows = lax.all_gather(input_rows, ("sec", "tp"), axis=1, tiled=True).astype(jnp.float32)
    squares = jnp.sum(full_rows * full_rows, axis=1, keepdims=True)
    normed = (full_rows * lax.rsqrt(squares / D + 1e-06) * norm_gain).astype(jnp.bfloat16)
    mixing = jnp.dot(
        normed,
        lax.all_gather(projection, "seq", axis=0, tiled=True),
        preferred_element_type=jnp.float32,
    )
    return (widened + mixing).astype(jnp.bfloat16)


def deliver(
    input_rows, token_terms, lengths, first_index, own_total, starts, seq_index, tile_rows, n_seq
):
    slot_count = input_rows.shape[0]
    slot_index = jnp.arange(slot_count, dtype=jnp.int32)
    offset = jnp.mod(slot_index - first_index, slot_count)
    filled = offset < own_total
    finish = jnp.cumsum(lengths)
    response = jnp.sum((finish[None, :] <= offset[:, None]).astype(jnp.int32), axis=1)
    response = jnp.minimum(response, lengths.shape[0] - 1)
    opening = jnp.take(finish - lengths, response)
    source = jnp.where(filled, response * LMAX + offset - opening, 0)
    send_rows = jnp.where(
        filled[:, None], jnp.take(input_rows, source, axis=0), jnp.zeros((), input_rows.dtype)
    )
    send_terms = jnp.where(
        filled[:, None], jnp.take(token_terms, source, axis=0), jnp.zeros((), token_terms.dtype)
    )
    arrived, arrived_terms = (
        lax.all_to_all(
            send_rows.reshape(n_seq, tile_rows, -1), "seq", split_axis=0, concat_axis=0, tiled=True
        ),
        lax.all_to_all(
            send_terms.reshape(n_seq, tile_rows, 2), "seq", split_axis=0, concat_axis=0, tiled=True
        ),
    )
    learner_row = jnp.arange(TOK_DEV, dtype=jnp.int32)
    packed = learner_row // tile_rows * slot_count + seq_index * tile_rows + learner_row % tile_rows
    sender = jnp.sum((starts[None, :] <= packed[:, None]).astype(jnp.int32), axis=1) - 1
    pick_index = sender * tile_rows + learner_row % tile_rows
    states = jnp.take(arrived.reshape(slot_count, -1), pick_index, axis=0)
    moved_terms = jnp.take(arrived_terms.reshape(slot_count, 2), pick_index, axis=0)
    return (states, moved_terms)


def shards(hidden, projection, norm_gain, old_logp, ref_logp, lengths, group_of, rewards):
    n_seq = lax.axis_size("seq")
    seq_index = lax.axis_index("seq")
    tile_rows = SLOTS // n_seq
    group_count = RESP_DEV * n_seq // GROUP
    member_table = (group_of[:, None] == jnp.arange(group_count, dtype=jnp.int32)[None, :]).astype(
        jnp.float32
    )
    reward_value = rewards.astype(jnp.float32)
    partial_value = jnp.stack(
        [
            jnp.dot(reward_value, member_table, precision=lax.Precision.HIGHEST),
            jnp.dot(reward_value * reward_value, member_table, precision=lax.Precision.HIGHEST),
        ]
    )
    own_total = jnp.sum(lengths)
    group_sums = lax.psum(partial_value, "seq")
    counts = lax.all_gather(jnp.reshape(own_total, (1,)), "seq", axis=0, tiled=True)
    group_mean = group_sums[0] / GROUP
    spread = jnp.maximum(jnp.sqrt(group_sums[1] / GROUP - group_mean * group_mean), 1.0)
    advantage = (
        reward_value - jnp.dot(member_table, group_mean, precision=lax.Precision.HIGHEST)
    ) / jnp.dot(member_table, spread, precision=lax.Precision.HIGHEST)
    log_ratio = ref_logp - old_logp
    penalty = jnp.exp(log_ratio) - log_ratio - 1.0
    token_terms = jnp.stack([jnp.repeat(advantage, LMAX), penalty], axis=1).astype(jnp.bfloat16)
    starts = jnp.cumsum(counts) - counts
    first_index = jnp.take(starts, seq_index)
    refined = refine(hidden, projection, norm_gain)
    return deliver(
        refined, token_terms, lengths, first_index, own_total, starts, seq_index, tile_rows, n_seq
    )


def solution(mesh):
    in_specs = (
        P("seq", ("sec", "tp")),
        P("seq", ("sec", "tp")),
        P(),
        P("seq"),
        P("seq"),
        P("seq"),
        P("seq"),
        P("seq"),
    )
    out_specs = (P("seq", ("sec", "tp")), P("seq", None))
    n = mesh.shape["seq"]
    in_place = mesh.shape["sec"] == n and n >= 4 and n & (n - 1) == 0
    body = shards_in_place if in_place else shards
    return jax.shard_map(body, mesh=mesh, in_specs=in_specs, out_specs=out_specs, check_vma=False)
```

```python
import functools

import jax
import jax.numpy as jnp
from jax import lax
from jax.experimental import pallas as pl
from jax.experimental.pallas import tpu as pltpu
from jax.sharding import PartitionSpec as P

D = 5120
TOK_DEV = 128
RESP_DEV = 4
GROUP = 8
LMAX = 64
TILE = 64
SLOTS = 256
EPS = 1e-06
BF16 = jnp.bfloat16
F32 = jnp.float32
I32 = jnp.int32
LANES = 128
INFO = 16
ARRIVALS = (2, 1, 3, 0)

VMEM = pl.BlockSpec(memory_space=pltpu.VMEM)
SMEM = pl.BlockSpec(memory_space=pltpu.SMEM)
HBM = pl.BlockSpec(memory_space=pltpu.HBM)


def iota(shape, dim):
    return lax.broadcasted_iota(I32, shape, dim)


def bits(n):
    return n.bit_length() - 1


def div(x, n):
    return lax.shift_right_arithmetic(x, jnp.full(jnp.shape(x), bits(n), I32))


def mod(x, n):
    return x & (n - 1)


def swap(x, axis, k):
    n = lax.axis_size(axis)
    return lax.ppermute(x, axis, [(i, i ^ k) for i in range(n)])


def early_kernel(n_sec, n_tp, hidden, lengths, group_of, rewards, old_logp, ref_logp, gain, *refs):
    pick, mine, info, gain_out = refs[:4]
    rows_in, length, group, reward, old, ref, sems = refs[4:]
    copies = []
    for i, (src, dst) in enumerate(
        (
            (lengths, length),
            (hidden, rows_in),
            (old_logp, old),
            (ref_logp, ref),
            (group_of, group),
            (rewards, reward),
            (gain, gain_out),
        )
    ):
        copies.append(pltpu.make_async_copy(src, dst, sems.at[i]))
        copies[-1].start()
    a = lax.axis_index("sec")
    t = lax.axis_index("tp")
    n_class = n_sec * n_tp
    rows = rows_in.shape[0]
    n_resp = length.shape[0]
    total = pick.shape[0]
    slots = total // n_sec
    place = iota((total, rows), 0)
    index = mod(place, slots) * n_class + (div(place, slots) ^ a) * n_tp + t
    copies[0].wait()
    source, finish = index, 0
    for r in range(n_resp):
        finish = finish + length[r]
        source = source + jnp.where(index >= finish, LMAX - length[r], 0)
    source = jnp.where(index < finish, source, -1)
    chosen = (iota((total, rows), 1) == source).astype(BF16)
    pick[...] = chosen
    for copy in copies[1:]:
        copy.wait()
    mine[...] = jnp.dot(chosen, rows_in[...], preferred_element_type=F32).astype(BF16)
    log_ratio = ref[...] - old[...]
    penalty = jnp.exp(log_ratio) - log_ratio - 1.0
    lane = iota((1, LANES), 1)
    words = jnp.zeros((1, LANES), F32)
    for r in range(n_resp):
        for i, held in enumerate((length, group, reward)):
            words = jnp.where(lane == i * n_resp + r, held[r].astype(F32), words)
    n_pen = penalty.shape[0]
    filler = jnp.zeros((info.shape[0] - n_pen - 1, LANES), F32)
    info[...] = jnp.concatenate([penalty, words, filler], axis=0).astype(BF16)


def spread_kernel(n_tp, pick, mine, sibling, *outs):
    t = lax.axis_index("tp")
    slots, width = outs[0].shape[0], mine.shape[1]
    own = mine[...].astype(F32)
    other = jnp.dot(pick[...], sibling[...], preferred_element_type=F32)
    first = jnp.where(t == 0, own, other).astype(BF16)
    second = jnp.where(t == 0, other, own).astype(BF16)
    for k, out in enumerate(outs):
        out[:, 0:width] = first[k * slots : (k + 1) * slots]
        out[:, width : 2 * width] = second[k * slots : (k + 1) * slots]


def in_order(order, refs):
    return [refs[order.index(k)] for k in range(len(order))]


def norm_kernel(n, gain, info, *refs):
    inputs, outs, held = refs[:n], refs[2 * n - 1 : n - 1 : -1], refs[2 * n]
    a = lax.axis_index("sec")
    s = lax.axis_index("seq")
    slots, width = inputs[0].shape
    squares = 0.0
    for ref in inputs:
        x = ref[...].astype(F32)
        squares = squares + jnp.sum(x * x, axis=1, keepdims=True)
    scale = lax.rsqrt(squares / D + EPS)
    for k, ref in enumerate(inputs):
        start = pl.multiple_of((a ^ k) * width, LANES)
        held[k] = (ref[...].astype(F32) * scale * gain[:, pl.ds(start, width)]).astype(BF16)
    for m, out in enumerate(outs):
        for h in range(slots // INFO):
            out[:, h * width : (h + 1) * width] = held[a ^ s ^ m, h * INFO : (h + 1) * INFO, :]
        out[:, out.shape[1] - LANES :] = info[...]


def info_of(ref):
    return ref[:, ref.shape[1] - LANES :].astype(F32)


def word_sum(block, row, first, last):
    lane = iota(block.shape, 1)
    inside = (iota(block.shape, 0) == row) & (lane >= first) & (lane < last)
    return jnp.sum(jnp.where(inside, block, 0.0)).astype(I32)


def put_counts(moved, row, n_resp, counts):
    s = lax.axis_index("seq")
    for m, ref in enumerate(moved):
        counts[s ^ m] = word_sum(info_of(ref), row, 0, n_resp)


def class_rows(x, c, n_class):
    return div(x - c + n_class - 1, n_class)


def list_place(counts, n, n_class, tok, s, c, seq_of, position, packed):
    span = tok * n // 4
    edges = []
    for j in range(5):
        edge, start = 0, 0
        for b in range(n):
            edge = edge + class_rows(jnp.clip(j * span - start, 0, counts[b]), c, n_class)
            start = start + counts[b]
        edges.append(edge)
    size = [edges[j + 1] - edges[j] for j in range(4)]
    high = div(s, n // 2)
    far_first = jnp.where(high == 0, size[1], size[0])
    far_rows = jnp.where(high == 0, size[1] + size[3], size[0] + size[2])
    near_first = jnp.where(high == 0, size[0], size[1])
    prefix = 0
    before = jnp.zeros_like(position)
    for b in range(n):
        before = jnp.where(seq_of == b, prefix, before)
        prefix = prefix + class_rows(counts[b], c, n_class)
    group = div(packed, span)
    opening = jnp.where(group == 0, edges[0], jnp.where(group == 1, edges[1], jnp.where(group == 2, edges[2], edges[3])))
    within = before + position - opening
    later = group >= 2
    far = mod(group, 2) != high
    far_place = within + jnp.where(later, far_first, 0)
    near_place = far_rows + within + jnp.where(later, near_first, 0)
    return jnp.where(far, far_place, near_place)


def pack_kernel(n, n_class, n_resp, tok, row, *refs):
    moved, (out, held, counts) = in_order(ARRIVALS, refs[:n]), refs[n:]
    s = lax.axis_index("seq")
    c = lax.axis_index("sec") * lax.axis_size("tp") + lax.axis_index("tp")
    width = out.shape[1]
    slots = (moved[0].shape[1] - LANES) // width * INFO
    put_counts(moved, row, n_resp, counts)
    lane = iota((1, n * slots), 1)
    seq_of = div(lane, slots) ^ s
    q = mod(lane, slots)
    live = jnp.zeros(lane.shape, jnp.bool_)
    start = jnp.zeros(lane.shape, I32)
    total = 0
    for b in range(n):
        live = live | ((seq_of == b) & (q < class_rows(counts[b], c, n_class)))
        start = jnp.where(seq_of == b, total, start)
        total = total + counts[b]
    packed = start + q * n_class + c
    place = list_place(counts, n, n_class, tok, s, c, seq_of, q, packed)
    place = jnp.where(live, place, -1)
    for m, ref in enumerate(moved):
        for h in range(slots // INFO):
            first = m * slots + h * INFO
            held[first : first + INFO, :] = ref[:, h * width : (h + 1) * width]
    pick = (iota((out.shape[0], n * slots), 0) == place).astype(BF16)
    out[...] = jnp.dot(pick, held[...], preferred_element_type=F32).astype(BF16)


def upright(x):
    return jnp.transpose(jnp.broadcast_to(x.astype(F32), (LANES, x.shape[1]))).astype(I32)


def one_hot(column, out):
    for j in range(out.shape[1] // LANES):
        out[:, j * LANES : (j + 1) * LANES] = (iota(column.shape, 1) + j * LANES == column).astype(BF16)


def index_kernel(n, n_class, n_resp, tok, row, *refs):
    moved, hidden = in_order(ARRIVALS, refs[:n]), refs[n]
    pick_far, pick_near, rest_far, rest_near, counts, lens, own = refs[n + 1 :]
    a = lax.axis_index("sec")
    s = lax.axis_index("seq")
    t = lax.axis_index("tp")
    n_tp = lax.axis_size("tp")
    put_counts(moved, row, n_resp, counts)
    block = info_of(moved[0])
    for r in range(n_resp):
        lens[r] = word_sum(block, row, r, r + 1)
    half = n // 2 * tok
    for far, pick, rest in ((True, pick_far, rest_far), (False, pick_near, rest_near)):
        lane = iota((1, half), 1)
        w = mod(lane, tok)
        shard = (div(lane, tok) + (n // 2 if far else 0)) ^ s
        packed = div(w, TILE) * (TILE * n) + shard * TILE + mod(w, TILE)
        seq_of = jnp.zeros(lane.shape, I32)
        start = jnp.zeros(lane.shape, I32)
        finish = 0
        for b in range(n):
            finish = finish + counts[b]
            passed = packed >= finish
            seq_of = seq_of + passed.astype(I32)
            start = jnp.where(passed, finish, start)
        index = packed - start
        c = mod(index, n_class)
        place = list_place(counts, n, n_class, tok, s, c, seq_of, div(index, n_class), packed)
        column = ((mod(c, n_tp) ^ t) * n + (div(c, n_tp) ^ a)) * (pick.shape[1] // n_class) + place
        one_hot(upright(column), pick)
        source, ends = index, 0
        for r in range(n_resp):
            ends = ends + lens[r]
            source = source + jnp.where(index >= ends, LMAX - lens[r], 0)
        one_hot(upright(jnp.where(seq_of == s, source, -1)), own)
        rest[...] = jnp.dot(own[...], hidden[...], preferred_element_type=F32)


def hold(held, pieces):
    listed, step = pieces[0].shape[0], held.shape[0] // len(pieces)
    for k, piece in enumerate(pieces):
        rows = piece[0 : min(step, listed), :].astype(F32)
        if step > listed:
            rows = jnp.concatenate([rows, jnp.zeros((step - listed, rows.shape[1]), F32)], axis=0)
        held[k * step : (k + 1) * step, :] = rows.astype(BF16)


def own_kernel(pick, *refs):
    pieces, out, held = refs[:-2], refs[-2], refs[-1]
    hold(held, pieces)
    out[...] = jnp.dot(pick[:, 0 : held.shape[0]], held[...], preferred_element_type=F32).astype(BF16)


def mix_kernel(n_lists, pick, found, rest, projection, *refs):
    pieces, outs, held = refs[:n_lists], refs[n_lists:-1], refs[-1]
    hold(held, pieces)
    other = jnp.dot(pick[:, held.shape[0] :], held[...], preferred_element_type=F32)
    tokens = (other + found[...].astype(F32)).astype(BF16)
    total = jnp.dot(tokens, projection[...], preferred_element_type=F32) + rest[...]
    first = 0
    for out in outs:
        out[...] = total[first : first + out.shape[0]].astype(out.dtype)
        first += out.shape[0]


def join_kernel(own, other, out):
    out[...] = (own[...] + other[...].astype(F32)).astype(out.dtype)


def final_kernel(n_whole, n_first, *refs):
    own, parts, out = refs[0], refs[1:-1], refs[-1]
    half = out.shape[0] // 2
    total = own[...]
    for part in parts[:n_whole]:
        total = total + part[...].astype(F32)
    first, second = total[0:half], total[half:]
    for part in parts[n_whole : n_whole + n_first]:
        first = first + part[...].astype(F32)
    for part in parts[n_whole + n_first :]:
        second = second + part[...].astype(F32)
    out[0:half] = first.astype(out.dtype)
    out[half:] = second.astype(out.dtype)


def terms_kernel(n, n_resp, row, *refs):
    moved, out, words, table = in_order(ARRIVALS, refs[:n]), refs[n], refs[n + 1], refs[n + 2]
    s = lax.axis_index("seq")
    tok = out.shape[1]
    group_count = n * n_resp // GROUP
    for m, ref in enumerate(moved):
        block = info_of(ref)
        table[pl.ds((s ^ m) * INFO, INFO), :] = block
        for r in range(3 * n_resp):
            words[s ^ m, r] = word_sum(block, row, r, r + 1)
    w = iota((1, tok), 1)
    packed = div(w, TILE) * (TILE * n) + s * TILE + mod(w, TILE)
    source, finish = packed, 0
    reward = jnp.zeros((1, tok), F32)
    group = jnp.zeros((1, tok), I32)
    total = [0] * group_count
    square = [0] * group_count
    for b in range(n):
        for r in range(n_resp):
            length, number, gain = words[b, r], words[b, n_resp + r], words[b, 2 * n_resp + r]
            within = packed >= finish
            reward = jnp.where(within, gain.astype(F32), reward)
            group = jnp.where(within, number, group)
            finish = finish + length
            source = source + jnp.where(packed >= finish, LMAX - length, 0)
            for g in range(group_count):
                total[g] = total[g] + jnp.where(number == g, gain, 0)
                square[g] = square[g] + jnp.where(number == g, gain * gain, 0)
    total_of = jnp.zeros((1, tok), F32)
    square_of = jnp.zeros((1, tok), F32)
    for g in range(group_count):
        total_of = jnp.where(group == g, total[g].astype(F32), total_of)
        square_of = jnp.where(group == g, square[g].astype(F32), square_of)
    mean = total_of / GROUP
    spread = jnp.maximum(jnp.sqrt(square_of / GROUP - mean * mean), 1.0)
    advantage = (reward - mean) / spread
    pick = (iota((LANES, tok), 0) == mod(source, LANES)).astype(BF16)
    found = jnp.dot(table[...].astype(BF16), pick, preferred_element_type=F32)
    line = div(source, LANES)
    chosen = iota(found.shape, 0) == div(line, row) * INFO + mod(line, row)
    penalty = jnp.sum(jnp.where(chosen, found, 0.0), axis=0, keepdims=True)
    out[0:1, :] = advantage
    out[1:2, :] = penalty


def call(kernel, out_shape, in_specs, out_specs, scratch=()):
    return pl.pallas_call(
        kernel,
        out_shape=out_shape,
        in_specs=in_specs,
        out_specs=out_specs,
        scratch_shapes=list(scratch),
        compiler_params=pltpu.CompilerParams(vmem_limit_bytes=48 * 1024 * 1024),
    )


def shards_in_place(hidden, projection, norm_gain, old_logp, ref_logp, lengths, group_of, rewards):
    n = lax.axis_size("seq")
    n_tp = lax.axis_size("tp")
    n_class = n * n_tp
    rows, cols = hidden.shape
    n_resp = lengths.shape[0]
    width = cols * n_tp
    slots = rows // n_class
    row = rows // LANES
    tok = TOK_DEV
    tokens = tok * n
    up = lambda x, m: -(-x // m) * m
    listed = up((tokens + (n_class - 1) * n) // n_class, 8)
    far_rows = up((tokens // 2 + (n_class - 1) * (n + 1)) // n_class, 16)
    shape = jax.ShapeDtypeStruct
    info_like = shape((INFO, slots // INFO * width + LANES), BF16)

    sibling = swap(hidden, "tp", 1)
    pick, mine, info, gain = call(
        functools.partial(early_kernel, n, n_tp),
        [
            shape((rows // n_tp, rows), BF16),
            shape((rows // n_tp, cols), BF16),
            shape((INFO, LANES), BF16),
            shape((1, D), F32),
        ],
        [HBM] * 7,
        [VMEM] * 4,
        [
            pltpu.VMEM((rows, cols), BF16),
            pltpu.SMEM((n_resp,), I32),
            pltpu.SMEM((n_resp,), I32),
            pltpu.SMEM((n_resp,), I32),
            pltpu.VMEM((row, LANES), F32),
            pltpu.VMEM((row, LANES), F32),
            pltpu.SemaphoreType.DMA((7,)),
        ],
    )(
        *(
            pltpu.with_memory_space_constraint(x, pltpu.HBM)
            for x in (
                hidden,
                lengths,
                group_of,
                rewards,
                old_logp.reshape(row, LANES),
                ref_logp.reshape(row, LANES),
                norm_gain.reshape(1, D),
            )
        )
    )
    dealt = call(
        functools.partial(spread_kernel, n_tp), [shape((slots, width), BF16)] * n, [VMEM] * 3, [VMEM] * n
    )(pick, mine, sibling)
    whole = [dealt[0]] + [swap(dealt[k], "sec", k) for k in range(1, n)]
    normed = call(
        functools.partial(norm_kernel, n),
        [info_like] * n,
        [VMEM] * (n + 2),
        [VMEM] * n,
        [pltpu.VMEM((n, slots, width), BF16)],
    )(gain, info, *whole)[::-1]
    moved = [normed[0]] + [swap(normed[m], "seq", m) for m in range(n - 1, 0, -1)][::-1]
    mine = call(
        functools.partial(pack_kernel, n, n_class, n_resp, tok, row),
        shape((listed, width), BF16),
        [VMEM] * n,
        VMEM,
        [pltpu.VMEM((n * slots, width), BF16), pltpu.SMEM((n,), I32)],
    )(*(moved[m] for m in ARRIVALS))
    half = n // 2 * tok
    pick_far, pick_near, rest_far, rest_near = call(
        functools.partial(index_kernel, n, n_class, n_resp, tok, row),
        [
            shape((half, n_class * far_rows), BF16),
            shape((half, n_class * up(listed, 16)), BF16),
            shape((half, cols), F32),
            shape((half, cols), F32),
        ],
        [VMEM] * (n + 1),
        [VMEM] * 4,
        [pltpu.SMEM((n,), I32), pltpu.SMEM((n_resp,), I32), pltpu.VMEM((half, rows), BF16)],
    )(*(moved[m] for m in ARRIVALS), hidden)
    terms = call(
        functools.partial(terms_kernel, n, n_resp, row),
        shape((2, tok), F32),
        [VMEM] * n,
        VMEM,
        [pltpu.SMEM((n, 3 * n_resp), I32), pltpu.VMEM((n * INFO, LANES), F32)],
    )(*(moved[m] for m in ARRIVALS))
    after = lambda x, *ys: lax.optimization_barrier((x, *ys))[0]
    same = [mine] + [swap(mine, "sec", k) for k in range(1, n)]
    other = [swap(after(x, pick_far, terms), "tp", 1) for x in same]

    def held_lists(pick):
        return [pltpu.VMEM((pick.shape[1] // n_tp, width), BF16)]

    def own_part(pick):
        shapes = shape((half, width), BF16), [VMEM] * (n + 1), VMEM, held_lists(pick)
        return call(own_kernel, *shapes)(pick, *same)

    def mix(pick, found, rest, outs):
        return call(
            functools.partial(mix_kernel, n), outs, [VMEM] * (n + 4), [VMEM] * len(outs), held_lists(pick)
        )(pick, found, rest, projection, *other)

    found_far, found_near = own_part(pick_far), own_part(pick_near)
    part = tok // 2
    joined = n // 2
    far = mix(
        after(pick_far, found_near),
        found_far,
        rest_far,
        [shape((part, cols), F32 if m % 2 and h else BF16) for m in range(joined) for h in range(2)],
    )
    helped = [swap(far[2 * m + 1], "seq", 1) for m in range(0, joined, 2)]
    sums = [
        call(join_kernel, shape((part, cols), BF16), [VMEM] * 2, VMEM)(far[2 * m + 3], got)
        for m, got in zip(range(0, joined, 2), helped, strict=True)
    ]
    passed = [swap(x, "seq", joined + m + 1) for m, x in zip(range(0, joined, 2), sums, strict=True)]
    near = mix(
        after(pick_near, *far), found_near, rest_near, [shape((tok, cols), F32)] + [shape((tok, cols), BF16)] * (joined - 1)
    )
    direct = [swap(far[0], "seq", joined)] + [
        swap(after(far[2 * m], *near), "seq", joined + m) for m in range(1, joined)
    ]
    whole = [swap(near[m], "seq", m) for m in range(1, joined)]
    states = call(
        functools.partial(final_kernel, len(whole), len(direct)),
        shape((tok, cols), BF16),
        [VMEM] * (1 + len(whole) + len(direct) + len(passed)),
        VMEM,
    )(near[0], *whole, *direct, *passed)
    return states, terms.astype(BF16).T


def refine(input_rows, projection, norm_gain):
    widened = input_rows.astype(jnp.float32)
    full_rows = lax.all_gather(input_rows, ("sec", "tp"), axis=1, tiled=True).astype(jnp.float32)
    squares = jnp.sum(full_rows * full_rows, axis=1, keepdims=True)
    normed = (full_rows * lax.rsqrt(squares / D + 1e-06) * norm_gain).astype(jnp.bfloat16)
    mixing = jnp.dot(
        normed,
        lax.all_gather(projection, "seq", axis=0, tiled=True),
        preferred_element_type=jnp.float32,
    )
    return (widened + mixing).astype(jnp.bfloat16)


def deliver(
    input_rows, token_terms, lengths, first_index, own_total, starts, seq_index, tile_rows, n_seq
):
    slot_count = input_rows.shape[0]
    slot_index = jnp.arange(slot_count, dtype=jnp.int32)
    offset = jnp.mod(slot_index - first_index, slot_count)
    filled = offset < own_total
    finish = jnp.cumsum(lengths)
    response = jnp.sum((finish[None, :] <= offset[:, None]).astype(jnp.int32), axis=1)
    response = jnp.minimum(response, lengths.shape[0] - 1)
    opening = jnp.take(finish - lengths, response)
    source = jnp.where(filled, response * LMAX + offset - opening, 0)
    send_rows = jnp.where(
        filled[:, None], jnp.take(input_rows, source, axis=0), jnp.zeros((), input_rows.dtype)
    )
    send_terms = jnp.where(
        filled[:, None], jnp.take(token_terms, source, axis=0), jnp.zeros((), token_terms.dtype)
    )
    arrived, arrived_terms = (
        lax.all_to_all(
            send_rows.reshape(n_seq, tile_rows, -1), "seq", split_axis=0, concat_axis=0, tiled=True
        ),
        lax.all_to_all(
            send_terms.reshape(n_seq, tile_rows, 2), "seq", split_axis=0, concat_axis=0, tiled=True
        ),
    )
    learner_row = jnp.arange(TOK_DEV, dtype=jnp.int32)
    packed = learner_row // tile_rows * slot_count + seq_index * tile_rows + learner_row % tile_rows
    sender = jnp.sum((starts[None, :] <= packed[:, None]).astype(jnp.int32), axis=1) - 1
    pick_index = sender * tile_rows + learner_row % tile_rows
    states = jnp.take(arrived.reshape(slot_count, -1), pick_index, axis=0)
    moved_terms = jnp.take(arrived_terms.reshape(slot_count, 2), pick_index, axis=0)
    return (states, moved_terms)


def shards(hidden, projection, norm_gain, old_logp, ref_logp, lengths, group_of, rewards):
    n_seq = lax.axis_size("seq")
    seq_index = lax.axis_index("seq")
    tile_rows = SLOTS // n_seq
    group_count = RESP_DEV * n_seq // GROUP
    member_table = (group_of[:, None] == jnp.arange(group_count, dtype=jnp.int32)[None, :]).astype(
        jnp.float32
    )
    reward_value = rewards.astype(jnp.float32)
    partial_value = jnp.stack(
        [
            jnp.dot(reward_value, member_table, precision=lax.Precision.HIGHEST),
            jnp.dot(reward_value * reward_value, member_table, precision=lax.Precision.HIGHEST),
        ]
    )
    own_total = jnp.sum(lengths)
    group_sums = lax.psum(partial_value, "seq")
    counts = lax.all_gather(jnp.reshape(own_total, (1,)), "seq", axis=0, tiled=True)
    group_mean = group_sums[0] / GROUP
    spread = jnp.maximum(jnp.sqrt(group_sums[1] / GROUP - group_mean * group_mean), 1.0)
    advantage = (
        reward_value - jnp.dot(member_table, group_mean, precision=lax.Precision.HIGHEST)
    ) / jnp.dot(member_table, spread, precision=lax.Precision.HIGHEST)
    log_ratio = ref_logp - old_logp
    penalty = jnp.exp(log_ratio) - log_ratio - 1.0
    token_terms = jnp.stack([jnp.repeat(advantage, LMAX), penalty], axis=1).astype(jnp.bfloat16)
    starts = jnp.cumsum(counts) - counts
    first_index = jnp.take(starts, seq_index)
    refined = refine(hidden, projection, norm_gain)
    return deliver(
        refined, token_terms, lengths, first_index, own_total, starts, seq_index, tile_rows, n_seq
    )


def solution(mesh):
    in_specs = (
        P("seq", ("sec", "tp")),
        P("seq", ("sec", "tp")),
        P(),
        P("seq"),
        P("seq"),
        P("seq"),
        P("seq"),
        P("seq"),
    )
    out_specs = (P("seq", ("sec", "tp")), P("seq", None))
    n = mesh.shape["seq"]
    in_place = mesh.shape["sec"] == n and n >= 4 and n & (n - 1) == 0
    body = shards_in_place if in_place else shards
    return jax.shard_map(body, mesh=mesh, in_specs=in_specs, out_specs=out_specs, check_vma=False)
```

```python
import functools

import jax
import jax.numpy as jnp
from jax import lax
from jax.experimental import pallas as pl
from jax.experimental.pallas import tpu as pltpu
from jax.sharding import PartitionSpec as P

D = 5120
TOK_DEV = 128
RESP_DEV = 4
GROUP = 8
LMAX = 64
TILE = 64
SLOTS = 256
EPS = 1e-06
BF16 = jnp.bfloat16
F32 = jnp.float32
I32 = jnp.int32
LANES = 128
INFO = 16
ARRIVALS = (2, 1, 3, 0)

VMEM = pl.BlockSpec(memory_space=pltpu.VMEM)
SMEM = pl.BlockSpec(memory_space=pltpu.SMEM)
HBM = pl.BlockSpec(memory_space=pltpu.HBM)


def iota(shape, dim):
    return lax.broadcasted_iota(I32, shape, dim)


def bits(n):
    return n.bit_length() - 1


def div(x, n):
    return lax.shift_right_arithmetic(x, jnp.full(jnp.shape(x), bits(n), I32))


def mod(x, n):
    return x & (n - 1)


def swap(x, axis, k):
    n = lax.axis_size(axis)
    return lax.ppermute(x, axis, [(i, i ^ k) for i in range(n)])


def early_kernel(n_sec, n_tp, hidden, lengths, group_of, rewards, old_logp, ref_logp, gain, *refs):
    pick, mine, info, gain_out = refs[:4]
    rows_in, length, group, reward, old, ref, sems = refs[4:]
    copies = []
    for i, (src, dst) in enumerate(
        (
            (lengths, length),
            (hidden, rows_in),
            (old_logp, old),
            (ref_logp, ref),
            (group_of, group),
            (rewards, reward),
            (gain, gain_out),
        )
    ):
        copies.append(pltpu.make_async_copy(src, dst, sems.at[i]))
        copies[-1].start()
    a = lax.axis_index("sec")
    t = lax.axis_index("tp")
    n_class = n_sec * n_tp
    rows = rows_in.shape[0]
    n_resp = length.shape[0]
    total = pick.shape[0]
    slots = total // n_sec
    place = iota((total, rows), 0)
    index = mod(place, slots) * n_class + (div(place, slots) ^ a) * n_tp + t
    copies[0].wait()
    source, finish = index, 0
    for r in range(n_resp):
        finish = finish + length[r]
        source = source + jnp.where(index >= finish, LMAX - length[r], 0)
    source = jnp.where(index < finish, source, -1)
    chosen = (iota((total, rows), 1) == source).astype(BF16)
    pick[...] = chosen
    for copy in copies[1:]:
        copy.wait()
    mine[...] = jnp.dot(chosen, rows_in[...], preferred_element_type=F32).astype(BF16)
    log_ratio = ref[...] - old[...]
    penalty = jnp.exp(log_ratio) - log_ratio - 1.0
    lane = iota((1, LANES), 1)
    words = jnp.zeros((1, LANES), F32)
    for r in range(n_resp):
        for i, held in enumerate((length, group, reward)):
            words = jnp.where(lane == i * n_resp + r, held[r].astype(F32), words)
    n_pen = penalty.shape[0]
    filler = jnp.zeros((info.shape[0] - n_pen - 1, LANES), F32)
    info[...] = jnp.concatenate([penalty, words, filler], axis=0).astype(BF16)


def spread_kernel(n_tp, pick, mine, sibling, *outs):
    t = lax.axis_index("tp")
    slots, width = outs[0].shape[0], mine.shape[1]
    own = mine[...].astype(F32)
    other = jnp.dot(pick[...], sibling[...], preferred_element_type=F32)
    first = jnp.where(t == 0, own, other).astype(BF16)
    second = jnp.where(t == 0, other, own).astype(BF16)
    for k, out in enumerate(outs):
        out[:, 0:width] = first[k * slots : (k + 1) * slots]
        out[:, width : 2 * width] = second[k * slots : (k + 1) * slots]


def in_order(order, refs):
    return [refs[order.index(k)] for k in range(len(order))]


def norm_kernel(n, gain, info, *refs):
    inputs, outs, held = refs[:n], refs[2 * n - 1 : n - 1 : -1], refs[2 * n]
    a = lax.axis_index("sec")
    s = lax.axis_index("seq")
    slots, width = inputs[0].shape
    squares = 0.0
    for ref in inputs:
        x = ref[...].astype(F32)
        squares = squares + jnp.sum(x * x, axis=1, keepdims=True)
    scale = lax.rsqrt(squares / D + EPS)
    for k, ref in enumerate(inputs):
        start = pl.multiple_of((a ^ k) * width, LANES)
        held[k] = (ref[...].astype(F32) * scale * gain[:, pl.ds(start, width)]).astype(BF16)
    for m, out in enumerate(outs):
        for h in range(slots // INFO):
            out[:, h * width : (h + 1) * width] = held[a ^ s ^ m, h * INFO : (h + 1) * INFO, :]
        out[:, out.shape[1] - LANES :] = info[...]


def info_of(ref):
    return ref[:, ref.shape[1] - LANES :].astype(F32)


def word_sum(block, row, first, last):
    lane = iota(block.shape, 1)
    inside = (iota(block.shape, 0) == row) & (lane >= first) & (lane < last)
    return jnp.sum(jnp.where(inside, block, 0.0)).astype(I32)


def put_counts(moved, row, n_resp, counts):
    s = lax.axis_index("seq")
    for m, ref in enumerate(moved):
        counts[s ^ m] = word_sum(info_of(ref), row, 0, n_resp)


def class_rows(x, c, n_class):
    return div(x - c + n_class - 1, n_class)


def list_place(counts, n, n_class, tok, s, c, seq_of, position, packed):
    span = tok * n // 4
    edges = []
    for j in range(5):
        edge, start = 0, 0
        for b in range(n):
            edge = edge + class_rows(jnp.clip(j * span - start, 0, counts[b]), c, n_class)
            start = start + counts[b]
        edges.append(edge)
    size = [edges[j + 1] - edges[j] for j in range(4)]
    high = div(s, n // 2)
    far_first = jnp.where(high == 0, size[1], size[0])
    far_rows = jnp.where(high == 0, size[1] + size[3], size[0] + size[2])
    near_first = jnp.where(high == 0, size[0], size[1])
    prefix = 0
    before = jnp.zeros_like(position)
    for b in range(n):
        before = jnp.where(seq_of == b, prefix, before)
        prefix = prefix + class_rows(counts[b], c, n_class)
    group = div(packed, span)
    opening = jnp.where(group == 0, edges[0], jnp.where(group == 1, edges[1], jnp.where(group == 2, edges[2], edges[3])))
    within = before + position - opening
    later = group >= 2
    far = mod(group, 2) != high
    far_place = within + jnp.where(later, far_first, 0)
    near_place = far_rows + within + jnp.where(later, near_first, 0)
    return jnp.where(far, far_place, near_place)


def pack_kernel(n, n_class, n_resp, tok, row, *refs):
    moved, (out, held, counts) = in_order(ARRIVALS, refs[:n]), refs[n:]
    s = lax.axis_index("seq")
    c = lax.axis_index("sec") * lax.axis_size("tp") + lax.axis_index("tp")
    width = out.shape[1]
    slots = (moved[0].shape[1] - LANES) // width * INFO
    put_counts(moved, row, n_resp, counts)
    lane = iota((1, n * slots), 1)
    seq_of = div(lane, slots) ^ s
    q = mod(lane, slots)
    live = jnp.zeros(lane.shape, jnp.bool_)
    start = jnp.zeros(lane.shape, I32)
    total = 0
    for b in range(n):
        live = live | ((seq_of == b) & (q < class_rows(counts[b], c, n_class)))
        start = jnp.where(seq_of == b, total, start)
        total = total + counts[b]
    packed = start + q * n_class + c
    place = list_place(counts, n, n_class, tok, s, c, seq_of, q, packed)
    place = jnp.where(live, place, -1)
    for m, ref in enumerate(moved):
        for h in range(slots // INFO):
            first = m * slots + h * INFO
            held[first : first + INFO, :] = ref[:, h * width : (h + 1) * width]
    pick = (iota((out.shape[0], n * slots), 0) == place).astype(BF16)
    out[...] = jnp.dot(pick, held[...], preferred_element_type=F32).astype(BF16)


def upright(x):
    return jnp.transpose(jnp.broadcast_to(x.astype(F32), (LANES, x.shape[1]))).astype(I32)


def one_hot(column, out):
    for j in range(out.shape[1] // LANES):
        out[:, j * LANES : (j + 1) * LANES] = (iota(column.shape, 1) + j * LANES == column).astype(BF16)


def index_kernel(n, n_class, n_resp, tok, row, *refs):
    moved, hidden = in_order(ARRIVALS, refs[:n]), refs[n]
    refs = refs[: n + 1] + refs[n + 2 :]
    pick_far, pick_near, rest_far, rest_near, counts, lens, own = refs[n + 1 :]
    a = lax.axis_index("sec")
    s = lax.axis_index("seq")
    t = lax.axis_index("tp")
    n_tp = lax.axis_size("tp")
    put_counts(moved, row, n_resp, counts)
    block = info_of(moved[0])
    for r in range(n_resp):
        lens[r] = word_sum(block, row, r, r + 1)
    half = n // 2 * tok
    for far, pick, rest in ((True, pick_far, rest_far), (False, pick_near, rest_near)):
        lane = iota((1, half), 1)
        w = mod(lane, tok)
        shard = (div(lane, tok) + (n // 2 if far else 0)) ^ s
        packed = div(w, TILE) * (TILE * n) + shard * TILE + mod(w, TILE)
        seq_of = jnp.zeros(lane.shape, I32)
        start = jnp.zeros(lane.shape, I32)
        finish = 0
        for b in range(n):
            finish = finish + counts[b]
            passed = packed >= finish
            seq_of = seq_of + passed.astype(I32)
            start = jnp.where(passed, finish, start)
        index = packed - start
        c = mod(index, n_class)
        place = list_place(counts, n, n_class, tok, s, c, seq_of, div(index, n_class), packed)
        column = ((mod(c, n_tp) ^ t) * n + (div(c, n_tp) ^ a)) * (pick.shape[1] // n_class) + place
        one_hot(upright(column), pick)
        source, ends = index, 0
        for r in range(n_resp):
            ends = ends + lens[r]
            source = source + jnp.where(index >= ends, LMAX - lens[r], 0)
        one_hot(upright(jnp.where(seq_of == s, source, -1)), own)
        rest[...] = jnp.dot(own[...], hidden[...], preferred_element_type=F32)


def hold(held, pieces):
    listed, step = pieces[0].shape[0], held.shape[0] // len(pieces)
    for k, piece in enumerate(pieces):
        rows = piece[0 : min(step, listed), :].astype(F32)
        if step > listed:
            rows = jnp.concatenate([rows, jnp.zeros((step - listed, rows.shape[1]), F32)], axis=0)
        held[k * step : (k + 1) * step, :] = rows.astype(BF16)


def own_kernel(pick, *refs):
    pieces, out, held = refs[:-2], refs[-2], refs[-1]
    hold(held, pieces)
    out[...] = jnp.dot(pick[:, 0 : held.shape[0]], held[...], preferred_element_type=F32).astype(BF16)


def mix_kernel(n_lists, pick, found, rest, projection, *refs):
    pieces, outs, held = refs[:n_lists], refs[n_lists:-1], refs[-1]
    hold(held, pieces)
    other = jnp.dot(pick[:, held.shape[0] :], held[...], preferred_element_type=F32)
    tokens = (other + found[...].astype(F32)).astype(BF16)
    total = jnp.dot(tokens, projection[...], preferred_element_type=F32) + rest[...]
    first = 0
    for out in outs:
        out[...] = total[first : first + out.shape[0]].astype(out.dtype)
        first += out.shape[0]


def join_kernel(own, other, out):
    out[...] = (own[...] + other[...].astype(F32)).astype(out.dtype)


def final_kernel(n_whole, n_first, *refs):
    own, parts, out = refs[0], refs[1:-1], refs[-1]
    half = out.shape[0] // 2
    total = own[...]
    for part in parts[:n_whole]:
        total = total + part[...].astype(F32)
    first, second = total[0:half], total[half:]
    for part in parts[n_whole : n_whole + n_first]:
        first = first + part[...].astype(F32)
    for part in parts[n_whole + n_first :]:
        second = second + part[...].astype(F32)
    out[0:half] = first.astype(out.dtype)
    out[half:] = second.astype(out.dtype)


def terms_kernel(n, n_resp, row, *refs):
    moved, out, words, table = in_order(ARRIVALS, refs[:n]), refs[n], refs[n + 1], refs[n + 2]
    s = lax.axis_index("seq")
    tok = out.shape[1]
    group_count = n * n_resp // GROUP
    for m, ref in enumerate(moved):
        block = info_of(ref)
        table[pl.ds((s ^ m) * INFO, INFO), :] = block
        for r in range(3 * n_resp):
            words[s ^ m, r] = word_sum(block, row, r, r + 1)
    w = iota((1, tok), 1)
    packed = div(w, TILE) * (TILE * n) + s * TILE + mod(w, TILE)
    source, finish = packed, 0
    reward = jnp.zeros((1, tok), F32)
    group = jnp.zeros((1, tok), I32)
    total = [0] * group_count
    square = [0] * group_count
    for b in range(n):
        for r in range(n_resp):
            length, number, gain = words[b, r], words[b, n_resp + r], words[b, 2 * n_resp + r]
            within = packed >= finish
            reward = jnp.where(within, gain.astype(F32), reward)
            group = jnp.where(within, number, group)
            finish = finish + length
            source = source + jnp.where(packed >= finish, LMAX - length, 0)
            for g in range(group_count):
                total[g] = total[g] + jnp.where(number == g, gain, 0)
                square[g] = square[g] + jnp.where(number == g, gain * gain, 0)
    total_of = jnp.zeros((1, tok), F32)
    square_of = jnp.zeros((1, tok), F32)
    for g in range(group_count):
        total_of = jnp.where(group == g, total[g].astype(F32), total_of)
        square_of = jnp.where(group == g, square[g].astype(F32), square_of)
    mean = total_of / GROUP
    spread = jnp.maximum(jnp.sqrt(square_of / GROUP - mean * mean), 1.0)
    advantage = (reward - mean) / spread
    pick = (iota((LANES, tok), 0) == mod(source, LANES)).astype(BF16)
    found = jnp.dot(table[...].astype(BF16), pick, preferred_element_type=F32)
    line = div(source, LANES)
    chosen = iota(found.shape, 0) == div(line, row) * INFO + mod(line, row)
    penalty = jnp.sum(jnp.where(chosen, found, 0.0), axis=0, keepdims=True)
    out[0:1, :] = advantage
    out[1:2, :] = penalty


def call(kernel, out_shape, in_specs, out_specs, scratch=()):
    return pl.pallas_call(
        kernel,
        out_shape=out_shape,
        in_specs=in_specs,
        out_specs=out_specs,
        scratch_shapes=list(scratch),
        compiler_params=pltpu.CompilerParams(vmem_limit_bytes=48 * 1024 * 1024),
    )


def shards_in_place(hidden, projection, norm_gain, old_logp, ref_logp, lengths, group_of, rewards):
    n = lax.axis_size("seq")
    n_tp = lax.axis_size("tp")
    n_class = n * n_tp
    rows, cols = hidden.shape
    n_resp = lengths.shape[0]
    width = cols * n_tp
    slots = rows // n_class
    row = rows // LANES
    tok = TOK_DEV
    tokens = tok * n
    up = lambda x, m: -(-x // m) * m
    listed = up((tokens + (n_class - 1) * n) // n_class, 8)
    far_rows = up((tokens // 2 + (n_class - 1) * (n + 1)) // n_class, 16)
    shape = jax.ShapeDtypeStruct
    info_like = shape((INFO, slots // INFO * width + LANES), BF16)

    sibling = swap(hidden, "tp", 1)
    pick, mine, info, gain = call(
        functools.partial(early_kernel, n, n_tp),
        [
            shape((rows // n_tp, rows), BF16),
            shape((rows // n_tp, cols), BF16),
            shape((INFO, LANES), BF16),
            shape((1, D), F32),
        ],
        [HBM] * 7,
        [VMEM] * 4,
        [
            pltpu.VMEM((rows, cols), BF16),
            pltpu.SMEM((n_resp,), I32),
            pltpu.SMEM((n_resp,), I32),
            pltpu.SMEM((n_resp,), I32),
            pltpu.VMEM((row, LANES), F32),
            pltpu.VMEM((row, LANES), F32),
            pltpu.SemaphoreType.DMA((7,)),
        ],
    )(
        *(
            pltpu.with_memory_space_constraint(x, pltpu.HBM)
            for x in (
                hidden,
                lengths,
                group_of,
                rewards,
                old_logp.reshape(row, LANES),
                ref_logp.reshape(row, LANES),
                norm_gain.reshape(1, D),
            )
        )
    )
    dealt = call(
        functools.partial(spread_kernel, n_tp), [shape((slots, width), BF16)] * n, [VMEM] * 3, [VMEM] * n
    )(pick, mine, sibling)
    whole = [dealt[0]] + [swap(dealt[k], "sec", k) for k in range(1, n)]
    normed = call(
        functools.partial(norm_kernel, n),
        [info_like] * n,
        [VMEM] * (n + 2),
        [VMEM] * n,
        [pltpu.VMEM((n, slots, width), BF16)],
    )(gain, info, *whole)[::-1]
    moved = [normed[0]] + [swap(normed[m], "seq", m) for m in range(n - 1, 0, -1)][::-1]
    mine = call(
        functools.partial(pack_kernel, n, n_class, n_resp, tok, row),
        shape((listed, width), BF16),
        [VMEM] * n,
        VMEM,
        [pltpu.VMEM((n * slots, width), BF16), pltpu.SMEM((n,), I32)],
    )(*(moved[m] for m in ARRIVALS))
    half = n // 2 * tok
    pick_far, pick_near, rest_far, rest_near = call(
        functools.partial(index_kernel, n, n_class, n_resp, tok, row),
        [
            shape((half, n_class * far_rows), BF16),
            shape((half, n_class * up(listed, 16)), BF16),
            shape((half, cols), F32),
            shape((half, cols), F32),
        ],
        [VMEM] * (n + 2),
        [VMEM] * 4,
        [pltpu.SMEM((n,), I32), pltpu.SMEM((n_resp,), I32), pltpu.VMEM((half, rows), BF16)],
    )(*(moved[m] for m in ARRIVALS), hidden, projection)
    terms = call(
        functools.partial(terms_kernel, n, n_resp, row),
        shape((2, tok), F32),
        [VMEM] * n,
        VMEM,
        [pltpu.SMEM((n, 3 * n_resp), I32), pltpu.VMEM((n * INFO, LANES), F32)],
    )(*(moved[m] for m in ARRIVALS))
    after = lambda x, *ys: lax.optimization_barrier((x, *ys))[0]
    same = [mine] + [swap(mine, "sec", k) for k in range(1, n)]
    other = [swap(after(x, pick_far, terms), "tp", 1) for x in same]

    def held_lists(pick):
        return [pltpu.VMEM((pick.shape[1] // n_tp, width), BF16)]

    def own_part(pick):
        shapes = shape((half, width), BF16), [VMEM] * (n + 1), VMEM, held_lists(pick)
        return call(own_kernel, *shapes)(pick, *same)

    def mix(pick, found, rest, outs):
        return call(
            functools.partial(mix_kernel, n), outs, [VMEM] * (n + 4), [VMEM] * len(outs), held_lists(pick)
        )(pick, found, rest, projection, *other)

    found_far, found_near = own_part(pick_far), own_part(pick_near)
    part = tok // 2
    joined = n // 2
    far = mix(
        after(pick_far, found_near),
        found_far,
        rest_far,
        [shape((part, cols), F32 if m % 2 and h else BF16) for m in range(joined) for h in range(2)],
    )
    helped = [swap(far[2 * m + 1], "seq", 1) for m in range(0, joined, 2)]
    sums = [
        call(join_kernel, shape((part, cols), BF16), [VMEM] * 2, VMEM)(far[2 * m + 3], got)
        for m, got in zip(range(0, joined, 2), helped, strict=True)
    ]
    passed = [swap(x, "seq", joined + m + 1) for m, x in zip(range(0, joined, 2), sums, strict=True)]
    near = mix(
        after(pick_near, *far), found_near, rest_near, [shape((tok, cols), F32)] + [shape((tok, cols), BF16)] * (joined - 1)
    )
    direct = [swap(far[0], "seq", joined)] + [
        swap(after(far[2 * m], *near), "seq", joined + m) for m in range(1, joined)
    ]
    whole = [swap(near[m], "seq", m) for m in range(1, joined)]
    states = call(
        functools.partial(final_kernel, len(whole), len(direct)),
        shape((tok, cols), BF16),
        [VMEM] * (1 + len(whole) + len(direct) + len(passed)),
        VMEM,
    )(near[0], *whole, *direct, *passed)
    return states, terms.astype(BF16).T


def refine(input_rows, projection, norm_gain):
    widened = input_rows.astype(jnp.float32)
    full_rows = lax.all_gather(input_rows, ("sec", "tp"), axis=1, tiled=True).astype(jnp.float32)
    squares = jnp.sum(full_rows * full_rows, axis=1, keepdims=True)
    normed = (full_rows * lax.rsqrt(squares / D + 1e-06) * norm_gain).astype(jnp.bfloat16)
    mixing = jnp.dot(
        normed,
        lax.all_gather(projection, "seq", axis=0, tiled=True),
        preferred_element_type=jnp.float32,
    )
    return (widened + mixing).astype(jnp.bfloat16)


def deliver(
    input_rows, token_terms, lengths, first_index, own_total, starts, seq_index, tile_rows, n_seq
):
    slot_count = input_rows.shape[0]
    slot_index = jnp.arange(slot_count, dtype=jnp.int32)
    offset = jnp.mod(slot_index - first_index, slot_count)
    filled = offset < own_total
    finish = jnp.cumsum(lengths)
    response = jnp.sum((finish[None, :] <= offset[:, None]).astype(jnp.int32), axis=1)
    response = jnp.minimum(response, lengths.shape[0] - 1)
    opening = jnp.take(finish - lengths, response)
    source = jnp.where(filled, response * LMAX + offset - opening, 0)
    send_rows = jnp.where(
        filled[:, None], jnp.take(input_rows, source, axis=0), jnp.zeros((), input_rows.dtype)
    )
    send_terms = jnp.where(
        filled[:, None], jnp.take(token_terms, source, axis=0), jnp.zeros((), token_terms.dtype)
    )
    arrived, arrived_terms = (
        lax.all_to_all(
            send_rows.reshape(n_seq, tile_rows, -1), "seq", split_axis=0, concat_axis=0, tiled=True
        ),
        lax.all_to_all(
            send_terms.reshape(n_seq, tile_rows, 2), "seq", split_axis=0, concat_axis=0, tiled=True
        ),
    )
    learner_row = jnp.arange(TOK_DEV, dtype=jnp.int32)
    packed = learner_row // tile_rows * slot_count + seq_index * tile_rows + learner_row % tile_rows
    sender = jnp.sum((starts[None, :] <= packed[:, None]).astype(jnp.int32), axis=1) - 1
    pick_index = sender * tile_rows + learner_row % tile_rows
    states = jnp.take(arrived.reshape(slot_count, -1), pick_index, axis=0)
    moved_terms = jnp.take(arrived_terms.reshape(slot_count, 2), pick_index, axis=0)
    return (states, moved_terms)


def shards(hidden, projection, norm_gain, old_logp, ref_logp, lengths, group_of, rewards):
    n_seq = lax.axis_size("seq")
    seq_index = lax.axis_index("seq")
    tile_rows = SLOTS // n_seq
    group_count = RESP_DEV * n_seq // GROUP
    member_table = (group_of[:, None] == jnp.arange(group_count, dtype=jnp.int32)[None, :]).astype(
        jnp.float32
    )
    reward_value = rewards.astype(jnp.float32)
    partial_value = jnp.stack(
        [
            jnp.dot(reward_value, member_table, precision=lax.Precision.HIGHEST),
            jnp.dot(reward_value * reward_value, member_table, precision=lax.Precision.HIGHEST),
        ]
    )
    own_total = jnp.sum(lengths)
    group_sums = lax.psum(partial_value, "seq")
    counts = lax.all_gather(jnp.reshape(own_total, (1,)), "seq", axis=0, tiled=True)
    group_mean = group_sums[0] / GROUP
    spread = jnp.maximum(jnp.sqrt(group_sums[1] / GROUP - group_mean * group_mean), 1.0)
    advantage = (
        reward_value - jnp.dot(member_table, group_mean, precision=lax.Precision.HIGHEST)
    ) / jnp.dot(member_table, spread, precision=lax.Precision.HIGHEST)
    log_ratio = ref_logp - old_logp
    penalty = jnp.exp(log_ratio) - log_ratio - 1.0
    token_terms = jnp.stack([jnp.repeat(advantage, LMAX), penalty], axis=1).astype(jnp.bfloat16)
    starts = jnp.cumsum(counts) - counts
    first_index = jnp.take(starts, seq_index)
    refined = refine(hidden, projection, norm_gain)
    return deliver(
        refined, token_terms, lengths, first_index, own_total, starts, seq_index, tile_rows, n_seq
    )


def solution(mesh):
    in_specs = (
        P("seq", ("sec", "tp")),
        P("seq", ("sec", "tp")),
        P(),
        P("seq"),
        P("seq"),
        P("seq"),
        P("seq"),
        P("seq"),
    )
    out_specs = (P("seq", ("sec", "tp")), P("seq", None))
    n = mesh.shape["seq"]
    in_place = mesh.shape["sec"] == n and n >= 4 and n & (n - 1) == 0
    body = shards_in_place if in_place else shards
    return jax.shard_map(body, mesh=mesh, in_specs=in_specs, out_specs=out_specs, check_vma=False)
```

```python
import functools

import jax
import jax.numpy as jnp
from jax import lax
from jax.experimental import pallas as pl
from jax.experimental.pallas import tpu as pltpu
from jax.sharding import PartitionSpec as P

D = 5120
TOK_DEV = 128
RESP_DEV = 4
GROUP = 8
LMAX = 64
TILE = 64
SLOTS = 256
EPS = 1e-06
BF16 = jnp.bfloat16
F32 = jnp.float32
I32 = jnp.int32
LANES = 128
INFO = 16
ARRIVALS = (2, 1, 3, 0)

VMEM = pl.BlockSpec(memory_space=pltpu.VMEM)
SMEM = pl.BlockSpec(memory_space=pltpu.SMEM)
HBM = pl.BlockSpec(memory_space=pltpu.HBM)


def iota(shape, dim):
    return lax.broadcasted_iota(I32, shape, dim)


def bits(n):
    return n.bit_length() - 1


def div(x, n):
    return lax.shift_right_arithmetic(x, jnp.full(jnp.shape(x), bits(n), I32))


def mod(x, n):
    return x & (n - 1)


def swap(x, axis, k):
    n = lax.axis_size(axis)
    return lax.ppermute(x, axis, [(i, i ^ k) for i in range(n)])


def early_kernel(n_sec, n_tp, hidden, lengths, group_of, rewards, old_logp, ref_logp, gain, *refs):
    pick, mine, info, gain_out = refs[:4]
    rows_in, length, group, reward, old, ref, sems = refs[4:]
    copies = []
    for i, (src, dst) in enumerate(
        (
            (lengths, length),
            (hidden, rows_in),
            (old_logp, old),
            (ref_logp, ref),
            (group_of, group),
            (rewards, reward),
            (gain, gain_out),
        )
    ):
        copies.append(pltpu.make_async_copy(src, dst, sems.at[i]))
        copies[-1].start()
    a = lax.axis_index("sec")
    t = lax.axis_index("tp")
    n_class = n_sec * n_tp
    rows = rows_in.shape[0]
    n_resp = length.shape[0]
    total = pick.shape[0]
    slots = total // n_sec
    place = iota((total, rows), 0)
    index = mod(place, slots) * n_class + (div(place, slots) ^ a) * n_tp + t
    copies[0].wait()
    source, finish = index, 0
    for r in range(n_resp):
        finish = finish + length[r]
        source = source + jnp.where(index >= finish, LMAX - length[r], 0)
    source = jnp.where(index < finish, source, -1)
    chosen = (iota((total, rows), 1) == source).astype(BF16)
    pick[...] = chosen
    for copy in copies[1:]:
        copy.wait()
    mine[...] = jnp.dot(chosen, rows_in[...], preferred_element_type=F32).astype(BF16)
    log_ratio = ref[...] - old[...]
    penalty = jnp.exp(log_ratio) - log_ratio - 1.0
    lane = iota((1, LANES), 1)
    words = jnp.zeros((1, LANES), F32)
    for r in range(n_resp):
        for i, held in enumerate((length, group, reward)):
            words = jnp.where(lane == i * n_resp + r, held[r].astype(F32), words)
    n_pen = penalty.shape[0]
    filler = jnp.zeros((info.shape[0] - n_pen - 1, LANES), F32)
    info[...] = jnp.concatenate([penalty, words, filler], axis=0).astype(BF16)


def spread_kernel(n_tp, pick, mine, sibling, *outs):
    t = lax.axis_index("tp")
    slots, width = outs[0].shape[0], mine.shape[1]
    own = mine[...].astype(F32)
    other = jnp.dot(pick[...], sibling[...], preferred_element_type=F32)
    first = jnp.where(t == 0, own, other).astype(BF16)
    second = jnp.where(t == 0, other, own).astype(BF16)
    for k, out in enumerate(outs):
        out[:, 0:width] = first[k * slots : (k + 1) * slots]
        out[:, width : 2 * width] = second[k * slots : (k + 1) * slots]


def in_order(order, refs):
    return [refs[order.index(k)] for k in range(len(order))]


def norm_kernel(n, gain, info, *refs):
    inputs, outs, held = refs[:n], refs[2 * n - 1 : n - 1 : -1], refs[2 * n]
    a = lax.axis_index("sec")
    s = lax.axis_index("seq")
    slots, width = inputs[0].shape
    squares = 0.0
    for ref in inputs:
        x = ref[...].astype(F32)
        squares = squares + jnp.sum(x * x, axis=1, keepdims=True)
    scale = lax.rsqrt(squares / D + EPS)
    for k, ref in enumerate(inputs):
        start = pl.multiple_of((a ^ k) * width, LANES)
        held[k] = (ref[...].astype(F32) * scale * gain[:, pl.ds(start, width)]).astype(BF16)
    for m, out in enumerate(outs):
        for h in range(slots // INFO):
            out[:, h * width : (h + 1) * width] = held[a ^ s ^ m, h * INFO : (h + 1) * INFO, :]
        out[:, out.shape[1] - LANES :] = info[...]


def info_of(ref):
    return ref[:, ref.shape[1] - LANES :].astype(F32)


def word_sum(block, row, first, last):
    lane = iota(block.shape, 1)
    inside = (iota(block.shape, 0) == row) & (lane >= first) & (lane < last)
    return jnp.sum(jnp.where(inside, block, 0.0)).astype(I32)


def put_counts(moved, row, n_resp, counts):
    s = lax.axis_index("seq")
    for m, ref in enumerate(moved):
        counts[s ^ m] = word_sum(info_of(ref), row, 0, n_resp)


def class_rows(x, c, n_class):
    return div(x - c + n_class - 1, n_class)


def list_place(counts, n, n_class, tok, s, c, seq_of, position, packed):
    span = tok * n // 4
    edges = []
    for j in range(5):
        edge, start = 0, 0
        for b in range(n):
            edge = edge + class_rows(jnp.clip(j * span - start, 0, counts[b]), c, n_class)
            start = start + counts[b]
        edges.append(edge)
    size = [edges[j + 1] - edges[j] for j in range(4)]
    high = div(s, n // 2)
    far_first = jnp.where(high == 0, size[1], size[0])
    far_rows = jnp.where(high == 0, size[1] + size[3], size[0] + size[2])
    near_first = jnp.where(high == 0, size[0], size[1])
    prefix = 0
    before = jnp.zeros_like(position)
    for b in range(n):
        before = jnp.where(seq_of == b, prefix, before)
        prefix = prefix + class_rows(counts[b], c, n_class)
    group = div(packed, span)
    opening = jnp.where(group == 0, edges[0], jnp.where(group == 1, edges[1], jnp.where(group == 2, edges[2], edges[3])))
    within = before + position - opening
    later = group >= 2
    far = mod(group, 2) != high
    far_place = within + jnp.where(later, far_first, 0)
    near_place = far_rows + within + jnp.where(later, near_first, 0)
    return jnp.where(far, far_place, near_place)


def pack_kernel(n, n_class, n_resp, tok, row, *refs):
    moved, (out, held, counts) = in_order(ARRIVALS, refs[:n]), refs[n:]
    s = lax.axis_index("seq")
    c = lax.axis_index("sec") * lax.axis_size("tp") + lax.axis_index("tp")
    width = out.shape[1]
    slots = (moved[0].shape[1] - LANES) // width * INFO
    put_counts(moved, row, n_resp, counts)
    lane = iota((1, n * slots), 1)
    seq_of = div(lane, slots) ^ s
    q = mod(lane, slots)
    live = jnp.zeros(lane.shape, jnp.bool_)
    start = jnp.zeros(lane.shape, I32)
    total = 0
    for b in range(n):
        live = live | ((seq_of == b) & (q < class_rows(counts[b], c, n_class)))
        start = jnp.where(seq_of == b, total, start)
        total = total + counts[b]
    packed = start + q * n_class + c
    place = list_place(counts, n, n_class, tok, s, c, seq_of, q, packed)
    place = jnp.where(live, place, -1)
    for m, ref in enumerate(moved):
        for h in range(slots // INFO):
            first = m * slots + h * INFO
            held[first : first + INFO, :] = ref[:, h * width : (h + 1) * width]
    pick = (iota((out.shape[0], n * slots), 0) == place).astype(BF16)
    out[...] = jnp.dot(pick, held[...], preferred_element_type=F32).astype(BF16)


def upright(x):
    return jnp.transpose(jnp.broadcast_to(x.astype(F32), (LANES, x.shape[1]))).astype(I32)


def one_hot(column, out):
    for j in range(out.shape[1] // LANES):
        out[:, j * LANES : (j + 1) * LANES] = (iota(column.shape, 1) + j * LANES == column).astype(BF16)


def index_kernel(n, n_class, n_resp, tok, row, *refs):
    moved, hidden = in_order(ARRIVALS, refs[:n]), refs[n]
    refs = refs[: n + 1] + refs[n + 2 :]
    pick_far, pick_near, rest_far, rest_near, counts, lens, own = refs[n + 1 :]
    a = lax.axis_index("sec")
    s = lax.axis_index("seq")
    t = lax.axis_index("tp")
    n_tp = lax.axis_size("tp")
    put_counts(moved, row, n_resp, counts)
    block = info_of(moved[0])
    for r in range(n_resp):
        lens[r] = word_sum(block, row, r, r + 1)
    half = n // 2 * tok
    for far, pick, rest in ((True, pick_far, rest_far), (False, pick_near, rest_near)):
        lane = iota((1, half), 1)
        w = mod(lane, tok)
        shard = (div(lane, tok) + (n // 2 if far else 0)) ^ s
        packed = div(w, TILE) * (TILE * n) + shard * TILE + mod(w, TILE)
        seq_of = jnp.zeros(lane.shape, I32)
        start = jnp.zeros(lane.shape, I32)
        finish = 0
        for b in range(n):
            finish = finish + counts[b]
            passed = packed >= finish
            seq_of = seq_of + passed.astype(I32)
            start = jnp.where(passed, finish, start)
        index = packed - start
        c = mod(index, n_class)
        place = list_place(counts, n, n_class, tok, s, c, seq_of, div(index, n_class), packed)
        column = ((mod(c, n_tp) ^ t) * n + (div(c, n_tp) ^ a)) * (pick.shape[1] // n_class) + place
        one_hot(upright(column), pick)
        source, ends = index, 0
        for r in range(n_resp):
            ends = ends + lens[r]
            source = source + jnp.where(index >= ends, LMAX - lens[r], 0)
        one_hot(upright(jnp.where(seq_of == s, source, -1)), own)
        rest[...] = jnp.dot(own[...], hidden[...], preferred_element_type=F32)


def hold(held, pieces):
    listed, step = pieces[0].shape[0], held.shape[0] // len(pieces)
    for k, piece in enumerate(pieces):
        rows = piece[0 : min(step, listed), :].astype(F32)
        if step > listed:
            rows = jnp.concatenate([rows, jnp.zeros((step - listed, rows.shape[1]), F32)], axis=0)
        held[k * step : (k + 1) * step, :] = rows.astype(BF16)


def own_kernel(pick, *refs):
    pieces, out, held = refs[:-2], refs[-2], refs[-1]
    hold(held, pieces)
    out[...] = jnp.dot(pick[:, 0 : held.shape[0]], held[...], preferred_element_type=F32).astype(BF16)


def mix_kernel(n_lists, pick, found, rest, projection, *refs):
    pieces, outs, held = refs[:n_lists], refs[n_lists:-1], refs[-1]
    hold(held, pieces)
    other = jnp.dot(pick[:, held.shape[0] :], held[...], preferred_element_type=F32)
    tokens = (other + found[...].astype(F32)).astype(BF16)
    total = jnp.dot(tokens, projection[...], preferred_element_type=F32) + rest[...]
    first = 0
    for out in outs:
        out[...] = total[first : first + out.shape[0]].astype(out.dtype)
        first += out.shape[0]


def join_kernel(own, other, out):
    out[...] = (own[...] + other[...].astype(F32)).astype(out.dtype)


def final_kernel(n_whole, n_first, *refs):
    own, parts, out = refs[0], refs[1:-1], refs[-1]
    half = parts[n_whole].shape[0]
    total = own[...]
    for part in parts[:n_whole]:
        total = total + part[...].astype(F32)
    first, second = total[0:half], total[half:]
    for part in parts[n_whole : n_whole + n_first]:
        first = first + part[...].astype(F32)
    for part in parts[n_whole + n_first :]:
        second = second + part[...].astype(F32)
    out[0:half] = first.astype(out.dtype)
    out[half:] = second.astype(out.dtype)


def terms_kernel(n, n_resp, row, *refs):
    moved, out, words, table = in_order(ARRIVALS, refs[:n]), refs[n], refs[n + 1], refs[n + 2]
    s = lax.axis_index("seq")
    tok = out.shape[1]
    group_count = n * n_resp // GROUP
    for m, ref in enumerate(moved):
        block = info_of(ref)
        table[pl.ds((s ^ m) * INFO, INFO), :] = block
        for r in range(3 * n_resp):
            words[s ^ m, r] = word_sum(block, row, r, r + 1)
    w = iota((1, tok), 1)
    packed = div(w, TILE) * (TILE * n) + s * TILE + mod(w, TILE)
    source, finish = packed, 0
    reward = jnp.zeros((1, tok), F32)
    group = jnp.zeros((1, tok), I32)
    total = [0] * group_count
    square = [0] * group_count
    for b in range(n):
        for r in range(n_resp):
            length, number, gain = words[b, r], words[b, n_resp + r], words[b, 2 * n_resp + r]
            within = packed >= finish
            reward = jnp.where(within, gain.astype(F32), reward)
            group = jnp.where(within, number, group)
            finish = finish + length
            source = source + jnp.where(packed >= finish, LMAX - length, 0)
            for g in range(group_count):
                total[g] = total[g] + jnp.where(number == g, gain, 0)
                square[g] = square[g] + jnp.where(number == g, gain * gain, 0)
    total_of = jnp.zeros((1, tok), F32)
    square_of = jnp.zeros((1, tok), F32)
    for g in range(group_count):
        total_of = jnp.where(group == g, total[g].astype(F32), total_of)
        square_of = jnp.where(group == g, square[g].astype(F32), square_of)
    mean = total_of / GROUP
    spread = jnp.maximum(jnp.sqrt(square_of / GROUP - mean * mean), 1.0)
    advantage = (reward - mean) / spread
    pick = (iota((LANES, tok), 0) == mod(source, LANES)).astype(BF16)
    found = jnp.dot(table[...].astype(BF16), pick, preferred_element_type=F32)
    line = div(source, LANES)
    chosen = iota(found.shape, 0) == div(line, row) * INFO + mod(line, row)
    penalty = jnp.sum(jnp.where(chosen, found, 0.0), axis=0, keepdims=True)
    out[0:1, :] = advantage
    out[1:2, :] = penalty


def call(kernel, out_shape, in_specs, out_specs, scratch=()):
    return pl.pallas_call(
        kernel,
        out_shape=out_shape,
        in_specs=in_specs,
        out_specs=out_specs,
        scratch_shapes=list(scratch),
        compiler_params=pltpu.CompilerParams(vmem_limit_bytes=48 * 1024 * 1024),
    )


def shards_in_place(hidden, projection, norm_gain, old_logp, ref_logp, lengths, group_of, rewards):
    n = lax.axis_size("seq")
    n_tp = lax.axis_size("tp")
    n_class = n * n_tp
    rows, cols = hidden.shape
    n_resp = lengths.shape[0]
    width = cols * n_tp
    slots = rows // n_class
    row = rows // LANES
    tok = TOK_DEV
    tokens = tok * n
    up = lambda x, m: -(-x // m) * m
    listed = up((tokens + (n_class - 1) * n) // n_class, 8)
    far_rows = up((tokens // 2 + (n_class - 1) * (n + 1)) // n_class, 16)
    shape = jax.ShapeDtypeStruct
    info_like = shape((INFO, slots // INFO * width + LANES), BF16)

    sibling = swap(hidden, "tp", 1)
    pick, mine, info, gain = call(
        functools.partial(early_kernel, n, n_tp),
        [
            shape((rows // n_tp, rows), BF16),
            shape((rows // n_tp, cols), BF16),
            shape((INFO, LANES), BF16),
            shape((1, D), F32),
        ],
        [HBM] * 7,
        [VMEM] * 4,
        [
            pltpu.VMEM((rows, cols), BF16),
            pltpu.SMEM((n_resp,), I32),
            pltpu.SMEM((n_resp,), I32),
            pltpu.SMEM((n_resp,), I32),
            pltpu.VMEM((row, LANES), F32),
            pltpu.VMEM((row, LANES), F32),
            pltpu.SemaphoreType.DMA((7,)),
        ],
    )(
        *(
            pltpu.with_memory_space_constraint(x, pltpu.HBM)
            for x in (
                hidden,
                lengths,
                group_of,
                rewards,
                old_logp.reshape(row, LANES),
                ref_logp.reshape(row, LANES),
                norm_gain.reshape(1, D),
            )
        )
    )
    dealt = call(
        functools.partial(spread_kernel, n_tp), [shape((slots, width), BF16)] * n, [VMEM] * 3, [VMEM] * n
    )(pick, mine, sibling)
    whole = [dealt[0]] + [swap(dealt[k], "sec", k) for k in range(1, n)]
    normed = call(
        functools.partial(norm_kernel, n),
        [info_like] * n,
        [VMEM] * (n + 2),
        [VMEM] * n,
        [pltpu.VMEM((n, slots, width), BF16)],
    )(gain, info, *whole)[::-1]
    moved = [normed[0]] + [swap(normed[m], "seq", m) for m in range(n - 1, 0, -1)][::-1]
    mine = call(
        functools.partial(pack_kernel, n, n_class, n_resp, tok, row),
        shape((listed, width), BF16),
        [VMEM] * n,
        VMEM,
        [pltpu.VMEM((n * slots, width), BF16), pltpu.SMEM((n,), I32)],
    )(*(moved[m] for m in ARRIVALS))
    half = n // 2 * tok
    pick_far, pick_near, rest_far, rest_near = call(
        functools.partial(index_kernel, n, n_class, n_resp, tok, row),
        [
            shape((half, n_class * far_rows), BF16),
            shape((half, n_class * up(listed, 16)), BF16),
            shape((half, cols), F32),
            shape((half, cols), F32),
        ],
        [VMEM] * (n + 2),
        [VMEM] * 4,
        [pltpu.SMEM((n,), I32), pltpu.SMEM((n_resp,), I32), pltpu.VMEM((half, rows), BF16)],
    )(*(moved[m] for m in ARRIVALS), hidden, projection)
    terms = call(
        functools.partial(terms_kernel, n, n_resp, row),
        shape((2, tok), F32),
        [VMEM] * n,
        VMEM,
        [pltpu.SMEM((n, 3 * n_resp), I32), pltpu.VMEM((n * INFO, LANES), F32)],
    )(*(moved[m] for m in ARRIVALS))
    after = lambda x, *ys: lax.optimization_barrier((x, *ys))[0]
    same = [mine] + [swap(mine, "sec", k) for k in range(1, n)]
    other = [swap(after(x, pick_far, terms), "tp", 1) for x in same]

    def held_lists(pick):
        return [pltpu.VMEM((pick.shape[1] // n_tp, width), BF16)]

    def own_part(pick):
        shapes = shape((half, width), BF16), [VMEM] * (n + 1), VMEM, held_lists(pick)
        return call(own_kernel, *shapes)(pick, *same)

    def mix(pick, found, rest, outs):
        return call(
            functools.partial(mix_kernel, n), outs, [VMEM] * (n + 4), [VMEM] * len(outs), held_lists(pick)
        )(pick, found, rest, projection, *other)

    found_far, found_near = own_part(pick_far), own_part(pick_near)
    parts = (tok * 5 // 8, tok * 3 // 8)
    joined = n // 2
    far = mix(
        after(pick_far, found_near),
        found_far,
        rest_far,
        [shape((parts[h], cols), F32 if m % 2 and h else BF16) for m in range(joined) for h in range(2)],
    )
    helped = [swap(far[2 * m + 1], "seq", 1) for m in range(0, joined, 2)]
    sums = [
        call(join_kernel, shape((parts[1], cols), BF16), [VMEM] * 2, VMEM)(far[2 * m + 3], got)
        for m, got in zip(range(0, joined, 2), helped, strict=True)
    ]
    passed = [swap(x, "seq", joined + m + 1) for m, x in zip(range(0, joined, 2), sums, strict=True)]
    near = mix(
        after(pick_near, *far), found_near, rest_near, [shape((tok, cols), F32)] + [shape((tok, cols), BF16)] * (joined - 1)
    )
    direct = [swap(far[0], "seq", joined)] + [
        swap(after(far[2 * m], *near), "seq", joined + m) for m in range(1, joined)
    ]
    whole = [swap(near[m], "seq", m) for m in range(1, joined)]
    states = call(
        functools.partial(final_kernel, len(whole), len(direct)),
        shape((tok, cols), BF16),
        [VMEM] * (1 + len(whole) + len(direct) + len(passed)),
        VMEM,
    )(near[0], *whole, *direct, *passed)
    return states, terms.astype(BF16).T


def refine(input_rows, projection, norm_gain):
    widened = input_rows.astype(jnp.float32)
    full_rows = lax.all_gather(input_rows, ("sec", "tp"), axis=1, tiled=True).astype(jnp.float32)
    squares = jnp.sum(full_rows * full_rows, axis=1, keepdims=True)
    normed = (full_rows * lax.rsqrt(squares / D + 1e-06) * norm_gain).astype(jnp.bfloat16)
    mixing = jnp.dot(
        normed,
        lax.all_gather(projection, "seq", axis=0, tiled=True),
        preferred_element_type=jnp.float32,
    )
    return (widened + mixing).astype(jnp.bfloat16)


def deliver(
    input_rows, token_terms, lengths, first_index, own_total, starts, seq_index, tile_rows, n_seq
):
    slot_count = input_rows.shape[0]
    slot_index = jnp.arange(slot_count, dtype=jnp.int32)
    offset = jnp.mod(slot_index - first_index, slot_count)
    filled = offset < own_total
    finish = jnp.cumsum(lengths)
    response = jnp.sum((finish[None, :] <= offset[:, None]).astype(jnp.int32), axis=1)
    response = jnp.minimum(response, lengths.shape[0] - 1)
    opening = jnp.take(finish - lengths, response)
    source = jnp.where(filled, response * LMAX + offset - opening, 0)
    send_rows = jnp.where(
        filled[:, None], jnp.take(input_rows, source, axis=0), jnp.zeros((), input_rows.dtype)
    )
    send_terms = jnp.where(
        filled[:, None], jnp.take(token_terms, source, axis=0), jnp.zeros((), token_terms.dtype)
    )
    arrived, arrived_terms = (
        lax.all_to_all(
            send_rows.reshape(n_seq, tile_rows, -1), "seq", split_axis=0, concat_axis=0, tiled=True
        ),
        lax.all_to_all(
            send_terms.reshape(n_seq, tile_rows, 2), "seq", split_axis=0, concat_axis=0, tiled=True
        ),
    )
    learner_row = jnp.arange(TOK_DEV, dtype=jnp.int32)
    packed = learner_row // tile_rows * slot_count + seq_index * tile_rows + learner_row % tile_rows
    sender = jnp.sum((starts[None, :] <= packed[:, None]).astype(jnp.int32), axis=1) - 1
    pick_index = sender * tile_rows + learner_row % tile_rows
    states = jnp.take(arrived.reshape(slot_count, -1), pick_index, axis=0)
    moved_terms = jnp.take(arrived_terms.reshape(slot_count, 2), pick_index, axis=0)
    return (states, moved_terms)


def shards(hidden, projection, norm_gain, old_logp, ref_logp, lengths, group_of, rewards):
    n_seq = lax.axis_size("seq")
    seq_index = lax.axis_index("seq")
    tile_rows = SLOTS // n_seq
    group_count = RESP_DEV * n_seq // GROUP
    member_table = (group_of[:, None] == jnp.arange(group_count, dtype=jnp.int32)[None, :]).astype(
        jnp.float32
    )
    reward_value = rewards.astype(jnp.float32)
    partial_value = jnp.stack(
        [
            jnp.dot(reward_value, member_table, precision=lax.Precision.HIGHEST),
            jnp.dot(reward_value * reward_value, member_table, precision=lax.Precision.HIGHEST),
        ]
    )
    own_total = jnp.sum(lengths)
    group_sums = lax.psum(partial_value, "seq")
    counts = lax.all_gather(jnp.reshape(own_total, (1,)), "seq", axis=0, tiled=True)
    group_mean = group_sums[0] / GROUP
    spread = jnp.maximum(jnp.sqrt(group_sums[1] / GROUP - group_mean * group_mean), 1.0)
    advantage = (
        reward_value - jnp.dot(member_table, group_mean, precision=lax.Precision.HIGHEST)
    ) / jnp.dot(member_table, spread, precision=lax.Precision.HIGHEST)
    log_ratio = ref_logp - old_logp
    penalty = jnp.exp(log_ratio) - log_ratio - 1.0
    token_terms = jnp.stack([jnp.repeat(advantage, LMAX), penalty], axis=1).astype(jnp.bfloat16)
    starts = jnp.cumsum(counts) - counts
    first_index = jnp.take(starts, seq_index)
    refined = refine(hidden, projection, norm_gain)
    return deliver(
        refined, token_terms, lengths, first_index, own_total, starts, seq_index, tile_rows, n_seq
    )


def solution(mesh):
    in_specs = (
        P("seq", ("sec", "tp")),
        P("seq", ("sec", "tp")),
        P(),
        P("seq"),
        P("seq"),
        P("seq"),
        P("seq"),
        P("seq"),
    )
    out_specs = (P("seq", ("sec", "tp")), P("seq", None))
    n = mesh.shape["seq"]
    in_place = mesh.shape["sec"] == n and n >= 4 and n & (n - 1) == 0
    body = shards_in_place if in_place else shards
    return jax.shard_map(body, mesh=mesh, in_specs=in_specs, out_specs=out_specs, check_vma=False)
```

```python
import functools

import jax
import jax.numpy as jnp
from jax import lax
from jax.experimental import pallas as pl
from jax.experimental.pallas import tpu as pltpu
from jax.sharding import PartitionSpec as P

D = 5120
TOK_DEV = 128
RESP_DEV = 4
GROUP = 8
LMAX = 64
TILE = 64
SLOTS = 256
EPS = 1e-06
BF16 = jnp.bfloat16
F32 = jnp.float32
I32 = jnp.int32
LANES = 128
INFO = 16
ARRIVALS = (2, 1, 3, 0)

VMEM = pl.BlockSpec(memory_space=pltpu.VMEM)
SMEM = pl.BlockSpec(memory_space=pltpu.SMEM)
HBM = pl.BlockSpec(memory_space=pltpu.HBM)


def iota(shape, dim):
    return lax.broadcasted_iota(I32, shape, dim)


def bits(n):
    return n.bit_length() - 1


def div(x, n):
    return lax.shift_right_arithmetic(x, jnp.full(jnp.shape(x), bits(n), I32))


def mod(x, n):
    return x & (n - 1)


def swap(x, axis, k):
    n = lax.axis_size(axis)
    return lax.ppermute(x, axis, [(i, i ^ k) for i in range(n)])


def early_kernel(n_sec, n_tp, hidden, lengths, group_of, rewards, old_logp, ref_logp, gain, *refs):
    pick, mine, info, gain_out = refs[:4]
    rows_in, length, group, reward, old, ref, sems = refs[4:]
    copies = []
    for i, (src, dst) in enumerate(
        (
            (lengths, length),
            (hidden, rows_in),
            (old_logp, old),
            (ref_logp, ref),
            (group_of, group),
            (rewards, reward),
            (gain, gain_out),
        )
    ):
        copies.append(pltpu.make_async_copy(src, dst, sems.at[i]))
        copies[-1].start()
    a = lax.axis_index("sec")
    t = lax.axis_index("tp")
    n_class = n_sec * n_tp
    rows = rows_in.shape[0]
    n_resp = length.shape[0]
    total = pick.shape[0]
    slots = total // n_sec
    place = iota((total, rows), 0)
    index = mod(place, slots) * n_class + (div(place, slots) ^ a) * n_tp + t
    copies[0].wait()
    source, finish = index, 0
    for r in range(n_resp):
        finish = finish + length[r]
        source = source + jnp.where(index >= finish, LMAX - length[r], 0)
    source = jnp.where(index < finish, source, -1)
    chosen = (iota((total, rows), 1) == source).astype(BF16)
    pick[...] = chosen
    for copy in copies[1:]:
        copy.wait()
    mine[...] = jnp.dot(chosen, rows_in[...], preferred_element_type=F32).astype(BF16)
    log_ratio = ref[...] - old[...]
    penalty = jnp.exp(log_ratio) - log_ratio - 1.0
    lane = iota((1, LANES), 1)
    words = jnp.zeros((1, LANES), F32)
    for r in range(n_resp):
        for i, held in enumerate((length, group, reward)):
            words = jnp.where(lane == i * n_resp + r, held[r].astype(F32), words)
    n_pen = penalty.shape[0]
    filler = jnp.zeros((info.shape[0] - n_pen - 1, LANES), F32)
    info[...] = jnp.concatenate([penalty, words, filler], axis=0).astype(BF16)


def spread_kernel(n_tp, pick, mine, sibling, *outs):
    t = lax.axis_index("tp")
    slots, width = outs[0].shape[0], mine.shape[1]
    own = mine[...].astype(F32)
    other = jnp.dot(pick[...], sibling[...], preferred_element_type=F32)
    first = jnp.where(t == 0, own, other).astype(BF16)
    second = jnp.where(t == 0, other, own).astype(BF16)
    for k, out in enumerate(outs):
        out[:, 0:width] = first[k * slots : (k + 1) * slots]
        out[:, width : 2 * width] = second[k * slots : (k + 1) * slots]


def in_order(order, refs):
    return [refs[order.index(k)] for k in range(len(order))]


def norm_kernel(n, gain, info, *refs):
    inputs, outs, held = refs[:n], refs[2 * n - 1 : n - 1 : -1], refs[2 * n]
    a = lax.axis_index("sec")
    s = lax.axis_index("seq")
    slots, width = inputs[0].shape
    squares = 0.0
    for ref in inputs:
        x = ref[...].astype(F32)
        squares = squares + jnp.sum(x * x, axis=1, keepdims=True)
    scale = lax.rsqrt(squares / D + EPS)
    for k, ref in enumerate(inputs):
        start = pl.multiple_of((a ^ k) * width, LANES)
        held[k] = (ref[...].astype(F32) * scale * gain[:, pl.ds(start, width)]).astype(BF16)
    for m, out in enumerate(outs):
        for h in range(slots // INFO):
            out[:, h * width : (h + 1) * width] = held[a ^ s ^ m, h * INFO : (h + 1) * INFO, :]
        out[:, out.shape[1] - LANES :] = info[...]


def info_of(ref):
    return ref[:, ref.shape[1] - LANES :].astype(F32)


def word_sum(block, row, first, last):
    lane = iota(block.shape, 1)
    inside = (iota(block.shape, 0) == row) & (lane >= first) & (lane < last)
    return jnp.sum(jnp.where(inside, block, 0.0)).astype(I32)


def put_counts(moved, row, n_resp, counts):
    s = lax.axis_index("seq")
    for m, ref in enumerate(moved):
        counts[s ^ m] = word_sum(info_of(ref), row, 0, n_resp)


def class_rows(x, c, n_class):
    return div(x - c + n_class - 1, n_class)


def list_place(counts, n, n_class, tok, s, c, seq_of, position, packed):
    span = tok * n // 4
    edges = []
    for j in range(5):
        edge, start = 0, 0
        for b in range(n):
            edge = edge + class_rows(jnp.clip(j * span - start, 0, counts[b]), c, n_class)
            start = start + counts[b]
        edges.append(edge)
    size = [edges[j + 1] - edges[j] for j in range(4)]
    high = div(s, n // 2)
    far_first = jnp.where(high == 0, size[1], size[0])
    far_rows = jnp.where(high == 0, size[1] + size[3], size[0] + size[2])
    near_first = jnp.where(high == 0, size[0], size[1])
    prefix = 0
    before = jnp.zeros_like(position)
    for b in range(n):
        before = jnp.where(seq_of == b, prefix, before)
        prefix = prefix + class_rows(counts[b], c, n_class)
    group = div(packed, span)
    opening = jnp.where(group == 0, edges[0], jnp.where(group == 1, edges[1], jnp.where(group == 2, edges[2], edges[3])))
    within = before + position - opening
    later = group >= 2
    far = mod(group, 2) != high
    far_place = within + jnp.where(later, far_first, 0)
    near_place = far_rows + within + jnp.where(later, near_first, 0)
    return jnp.where(far, far_place, near_place)


def pack_kernel(n, n_class, n_resp, tok, row, *refs):
    moved, (out, held, counts) = in_order(ARRIVALS, refs[:n]), refs[n:]
    s = lax.axis_index("seq")
    c = lax.axis_index("sec") * lax.axis_size("tp") + lax.axis_index("tp")
    width = out.shape[1]
    slots = (moved[0].shape[1] - LANES) // width * INFO
    put_counts(moved, row, n_resp, counts)
    lane = iota((1, n * slots), 1)
    seq_of = div(lane, slots) ^ s
    q = mod(lane, slots)
    live = jnp.zeros(lane.shape, jnp.bool_)
    start = jnp.zeros(lane.shape, I32)
    total = 0
    for b in range(n):
        live = live | ((seq_of == b) & (q < class_rows(counts[b], c, n_class)))
        start = jnp.where(seq_of == b, total, start)
        total = total + counts[b]
    packed = start + q * n_class + c
    place = list_place(counts, n, n_class, tok, s, c, seq_of, q, packed)
    place = jnp.where(live, place, -1)
    for m, ref in enumerate(moved):
        for h in range(slots // INFO):
            first = m * slots + h * INFO
            held[first : first + INFO, :] = ref[:, h * width : (h + 1) * width]
    pick = (iota((out.shape[0], n * slots), 0) == place).astype(BF16)
    out[...] = jnp.dot(pick, held[...], preferred_element_type=F32).astype(BF16)


def upright(x):
    return jnp.transpose(jnp.broadcast_to(x.astype(F32), (LANES, x.shape[1]))).astype(I32)


def one_hot(column, out):
    for j in range(out.shape[1] // LANES):
        out[:, j * LANES : (j + 1) * LANES] = (iota(column.shape, 1) + j * LANES == column).astype(BF16)


def index_kernel(n, n_class, n_resp, tok, row, *refs):
    moved, hidden = in_order(ARRIVALS, refs[:n]), refs[n]
    refs = refs[: n + 1] + refs[n + 2 :]
    pick_far, pick_near, rest_far, rest_near, counts, lens, own = refs[n + 1 :]
    a = lax.axis_index("sec")
    s = lax.axis_index("seq")
    t = lax.axis_index("tp")
    n_tp = lax.axis_size("tp")
    put_counts(moved, row, n_resp, counts)
    block = info_of(moved[0])
    for r in range(n_resp):
        lens[r] = word_sum(block, row, r, r + 1)
    half = n // 2 * tok
    for far, pick, rest in ((True, pick_far, rest_far), (False, pick_near, rest_near)):
        lane = iota((1, half), 1)
        w = mod(lane, tok)
        shard = (div(lane, tok) + (n // 2 if far else 0)) ^ s
        packed = div(w, TILE) * (TILE * n) + shard * TILE + mod(w, TILE)
        seq_of = jnp.zeros(lane.shape, I32)
        start = jnp.zeros(lane.shape, I32)
        finish = 0
        for b in range(n):
            finish = finish + counts[b]
            passed = packed >= finish
            seq_of = seq_of + passed.astype(I32)
            start = jnp.where(passed, finish, start)
        index = packed - start
        c = mod(index, n_class)
        place = list_place(counts, n, n_class, tok, s, c, seq_of, div(index, n_class), packed)
        column = ((mod(c, n_tp) ^ t) * n + (div(c, n_tp) ^ a)) * (pick.shape[1] // n_class) + place
        one_hot(upright(column), pick)
        source, ends = index, 0
        for r in range(n_resp):
            ends = ends + lens[r]
            source = source + jnp.where(index >= ends, LMAX - lens[r], 0)
        one_hot(upright(jnp.where(seq_of == s, source, -1)), own)
        rest[...] = jnp.dot(own[...], hidden[...], preferred_element_type=F32)


def hold(held, pieces):
    listed, step = pieces[0].shape[0], held.shape[0] // len(pieces)
    for k, piece in enumerate(pieces):
        rows = piece[0 : min(step, listed), :].astype(F32)
        if step > listed:
            rows = jnp.concatenate([rows, jnp.zeros((step - listed, rows.shape[1]), F32)], axis=0)
        held[k * step : (k + 1) * step, :] = rows.astype(BF16)


def own_kernel(pick, *refs):
    pieces, out, held = refs[:-2], refs[-2], refs[-1]
    hold(held, pieces)
    out[...] = jnp.dot(pick[:, 0 : held.shape[0]], held[...], preferred_element_type=F32).astype(BF16)


def mix_kernel(n_lists, pick, found, rest, projection, *refs):
    pieces, outs, held = refs[:n_lists], refs[n_lists:-1], refs[-1]
    hold(held, pieces)
    other = jnp.dot(pick[:, held.shape[0] :], held[...], preferred_element_type=F32)
    tokens = (other + found[...].astype(F32)).astype(BF16)
    total = jnp.dot(tokens, projection[...], preferred_element_type=F32) + rest[...]
    first = 0
    for out in outs:
        out[...] = total[first : first + out.shape[0]].astype(out.dtype)
        first += out.shape[0]


def join_kernel(own, other, out):
    out[...] = (own[...] + other[...].astype(F32)).astype(out.dtype)


def final_kernel(n_whole, n_first, *refs):
    own, parts, out = refs[0], refs[1:-1], refs[-1]
    half = out.shape[0] // 2
    total = own[...]
    for part in parts[:n_whole]:
        total = total + part[...].astype(F32)
    first, second = total[0:half], total[half:]
    for part in parts[n_whole : n_whole + n_first]:
        first = first + part[...].astype(F32)
    for part in parts[n_whole + n_first :]:
        second = second + part[...].astype(F32)
    out[0:half] = first.astype(out.dtype)
    out[half:] = second.astype(out.dtype)


def terms_kernel(n, n_resp, row, *refs):
    moved, out, words, table = in_order(ARRIVALS, refs[:n]), refs[n], refs[n + 1], refs[n + 2]
    s = lax.axis_index("seq")
    tok = out.shape[1]
    group_count = n * n_resp // GROUP
    for m, ref in enumerate(moved):
        block = info_of(ref)
        table[pl.ds((s ^ m) * INFO, INFO), :] = block
        for r in range(3 * n_resp):
            words[s ^ m, r] = word_sum(block, row, r, r + 1)
    w = iota((1, tok), 1)
    packed = div(w, TILE) * (TILE * n) + s * TILE + mod(w, TILE)
    source, finish = packed, 0
    reward = jnp.zeros((1, tok), F32)
    group = jnp.zeros((1, tok), I32)
    total = [0] * group_count
    square = [0] * group_count
    for b in range(n):
        for r in range(n_resp):
            length, number, gain = words[b, r], words[b, n_resp + r], words[b, 2 * n_resp + r]
            within = packed >= finish
            reward = jnp.where(within, gain.astype(F32), reward)
            group = jnp.where(within, number, group)
            finish = finish + length
            source = source + jnp.where(packed >= finish, LMAX - length, 0)
            for g in range(group_count):
                total[g] = total[g] + jnp.where(number == g, gain, 0)
                square[g] = square[g] + jnp.where(number == g, gain * gain, 0)
    total_of = jnp.zeros((1, tok), F32)
    square_of = jnp.zeros((1, tok), F32)
    for g in range(group_count):
        total_of = jnp.where(group == g, total[g].astype(F32), total_of)
        square_of = jnp.where(group == g, square[g].astype(F32), square_of)
    mean = total_of / GROUP
    spread = jnp.maximum(jnp.sqrt(square_of / GROUP - mean * mean), 1.0)
    advantage = (reward - mean) / spread
    pick = (iota((LANES, tok), 0) == mod(source, LANES)).astype(BF16)
    found = jnp.dot(table[...].astype(BF16), pick, preferred_element_type=F32)
    line = div(source, LANES)
    chosen = iota(found.shape, 0) == div(line, row) * INFO + mod(line, row)
    penalty = jnp.sum(jnp.where(chosen, found, 0.0), axis=0, keepdims=True)
    out[0:1, :] = advantage
    out[1:2, :] = penalty


def call(kernel, out_shape, in_specs, out_specs, scratch=()):
    return pl.pallas_call(
        kernel,
        out_shape=out_shape,
        in_specs=in_specs,
        out_specs=out_specs,
        scratch_shapes=list(scratch),
        compiler_params=pltpu.CompilerParams(vmem_limit_bytes=48 * 1024 * 1024),
    )


def shards_in_place(hidden, projection, norm_gain, old_logp, ref_logp, lengths, group_of, rewards):
    n = lax.axis_size("seq")
    n_tp = lax.axis_size("tp")
    n_class = n * n_tp
    rows, cols = hidden.shape
    n_resp = lengths.shape[0]
    width = cols * n_tp
    slots = rows // n_class
    row = rows // LANES
    tok = TOK_DEV
    tokens = tok * n
    up = lambda x, m: -(-x // m) * m
    listed = up((tokens + (n_class - 1) * n) // n_class, 8)
    far_rows = up((tokens // 2 + (n_class - 1) * (n + 1)) // n_class, 16)
    shape = jax.ShapeDtypeStruct
    info_like = shape((INFO, slots // INFO * width + LANES), BF16)

    sibling = swap(hidden, "tp", 1)
    pick, mine, info, gain = call(
        functools.partial(early_kernel, n, n_tp),
        [
            shape((rows // n_tp, rows), BF16),
            shape((rows // n_tp, cols), BF16),
            shape((INFO, LANES), BF16),
            shape((1, D), F32),
        ],
        [HBM] * 7,
        [VMEM] * 4,
        [
            pltpu.VMEM((rows, cols), BF16),
            pltpu.SMEM((n_resp,), I32),
            pltpu.SMEM((n_resp,), I32),
            pltpu.SMEM((n_resp,), I32),
            pltpu.VMEM((row, LANES), F32),
            pltpu.VMEM((row, LANES), F32),
            pltpu.SemaphoreType.DMA((7,)),
        ],
    )(
        *(
            pltpu.with_memory_space_constraint(x, pltpu.HBM)
            for x in (
                hidden,
                lengths,
                group_of,
                rewards,
                old_logp.reshape(row, LANES),
                ref_logp.reshape(row, LANES),
                norm_gain.reshape(1, D),
            )
        )
    )
    dealt = call(
        functools.partial(spread_kernel, n_tp), [shape((slots, width), BF16)] * n, [VMEM] * 3, [VMEM] * n
    )(pick, mine, sibling)
    whole = [dealt[0]] + [swap(dealt[k], "sec", k) for k in range(1, n)]
    normed = call(
        functools.partial(norm_kernel, n),
        [info_like] * n,
        [VMEM] * (n + 2),
        [VMEM] * n,
        [pltpu.VMEM((n, slots, width), BF16)],
    )(gain, info, *whole)[::-1]
    moved = [normed[0]] + [swap(normed[m], "seq", m) for m in range(n - 1, 0, -1)][::-1]
    mine = call(
        functools.partial(pack_kernel, n, n_class, n_resp, tok, row),
        shape((listed, width), BF16),
        [VMEM] * n,
        VMEM,
        [pltpu.VMEM((n * slots, width), BF16), pltpu.SMEM((n,), I32)],
    )(*(moved[m] for m in ARRIVALS))
    half = n // 2 * tok
    pick_far, pick_near, rest_far, rest_near = call(
        functools.partial(index_kernel, n, n_class, n_resp, tok, row),
        [
            shape((half, n_class * far_rows), BF16),
            shape((half, n_class * up(listed, 16)), BF16),
            shape((half, cols), F32),
            shape((half, cols), F32),
        ],
        [VMEM] * (n + 2),
        [VMEM] * 4,
        [pltpu.SMEM((n,), I32), pltpu.SMEM((n_resp,), I32), pltpu.VMEM((half, rows), BF16)],
    )(*(moved[m] for m in ARRIVALS), hidden, projection)
    terms = call(
        functools.partial(terms_kernel, n, n_resp, row),
        shape((2, tok), F32),
        [VMEM] * n,
        VMEM,
        [pltpu.SMEM((n, 3 * n_resp), I32), pltpu.VMEM((n * INFO, LANES), F32)],
    )(*(moved[m] for m in ARRIVALS))
    after = lambda x, *ys: lax.optimization_barrier((x, *ys))[0]
    same = [mine] + [swap(mine, "sec", k) for k in range(1, n)]
    other = [swap(after(x, pick_far, terms), "tp", 1) for x in same]

    def held_lists(pick):
        return [pltpu.VMEM((pick.shape[1] // n_tp, width), BF16)]

    def own_part(pick):
        shapes = shape((half, width), BF16), [VMEM] * (n + 1), VMEM, held_lists(pick)
        return call(own_kernel, *shapes)(pick, *same)

    def mix(pick, found, rest, outs):
        return call(
            functools.partial(mix_kernel, n), outs, [VMEM] * (n + 4), [VMEM] * len(outs), held_lists(pick)
        )(pick, found, rest, projection, *other)

    found_far, found_near = own_part(pick_far), own_part(pick_near)
    part = tok // 2
    joined = n // 2
    far = mix(
        after(pick_far, found_near),
        found_far,
        rest_far,
        [shape((part, cols), F32 if m % 2 and h else BF16) for m in range(joined) for h in range(2)],
    )
    helped = [swap(far[2 * m + 1], "seq", 1) for m in range(0, joined, 2)]
    sums = [
        call(join_kernel, shape((part, cols), BF16), [VMEM] * 2, VMEM)(far[2 * m + 3], got)
        for m, got in zip(range(0, joined, 2), helped, strict=True)
    ]
    passed = [swap(x, "seq", joined + m + 1) for m, x in zip(range(0, joined, 2), sums, strict=True)]
    near = mix(
        after(pick_near, *far), found_near, rest_near, [shape((tok, cols), F32)] + [shape((tok, cols), BF16)] * (joined - 1)
    )
    direct = [swap(far[0], "seq", joined)] + [
        swap(after(far[2 * m], *near, *sums), "seq", joined + m) for m in range(1, joined)
    ]
    whole = [swap(near[m], "seq", m) for m in range(1, joined)]
    states = call(
        functools.partial(final_kernel, len(whole), len(direct)),
        shape((tok, cols), BF16),
        [VMEM] * (1 + len(whole) + len(direct) + len(passed)),
        VMEM,
    )(near[0], *whole, *direct, *passed)
    return states, terms.astype(BF16).T


def refine(input_rows, projection, norm_gain):
    widened = input_rows.astype(jnp.float32)
    full_rows = lax.all_gather(input_rows, ("sec", "tp"), axis=1, tiled=True).astype(jnp.float32)
    squares = jnp.sum(full_rows * full_rows, axis=1, keepdims=True)
    normed = (full_rows * lax.rsqrt(squares / D + 1e-06) * norm_gain).astype(jnp.bfloat16)
    mixing = jnp.dot(
        normed,
        lax.all_gather(projection, "seq", axis=0, tiled=True),
        preferred_element_type=jnp.float32,
    )
    return (widened + mixing).astype(jnp.bfloat16)


def deliver(
    input_rows, token_terms, lengths, first_index, own_total, starts, seq_index, tile_rows, n_seq
):
    slot_count = input_rows.shape[0]
    slot_index = jnp.arange(slot_count, dtype=jnp.int32)
    offset = jnp.mod(slot_index - first_index, slot_count)
    filled = offset < own_total
    finish = jnp.cumsum(lengths)
    response = jnp.sum((finish[None, :] <= offset[:, None]).astype(jnp.int32), axis=1)
    response = jnp.minimum(response, lengths.shape[0] - 1)
    opening = jnp.take(finish - lengths, response)
    source = jnp.where(filled, response * LMAX + offset - opening, 0)
    send_rows = jnp.where(
        filled[:, None], jnp.take(input_rows, source, axis=0), jnp.zeros((), input_rows.dtype)
    )
    send_terms = jnp.where(
        filled[:, None], jnp.take(token_terms, source, axis=0), jnp.zeros((), token_terms.dtype)
    )
    arrived, arrived_terms = (
        lax.all_to_all(
            send_rows.reshape(n_seq, tile_rows, -1), "seq", split_axis=0, concat_axis=0, tiled=True
        ),
        lax.all_to_all(
            send_terms.reshape(n_seq, tile_rows, 2), "seq", split_axis=0, concat_axis=0, tiled=True
        ),
    )
    learner_row = jnp.arange(TOK_DEV, dtype=jnp.int32)
    packed = learner_row // tile_rows * slot_count + seq_index * tile_rows + learner_row % tile_rows
    sender = jnp.sum((starts[None, :] <= packed[:, None]).astype(jnp.int32), axis=1) - 1
    pick_index = sender * tile_rows + learner_row % tile_rows
    states = jnp.take(arrived.reshape(slot_count, -1), pick_index, axis=0)
    moved_terms = jnp.take(arrived_terms.reshape(slot_count, 2), pick_index, axis=0)
    return (states, moved_terms)


def shards(hidden, projection, norm_gain, old_logp, ref_logp, lengths, group_of, rewards):
    n_seq = lax.axis_size("seq")
    seq_index = lax.axis_index("seq")
    tile_rows = SLOTS // n_seq
    group_count = RESP_DEV * n_seq // GROUP
    member_table = (group_of[:, None] == jnp.arange(group_count, dtype=jnp.int32)[None, :]).astype(
        jnp.float32
    )
    reward_value = rewards.astype(jnp.float32)
    partial_value = jnp.stack(
        [
            jnp.dot(reward_value, member_table, precision=lax.Precision.HIGHEST),
            jnp.dot(reward_value * reward_value, member_table, precision=lax.Precision.HIGHEST),
        ]
    )
    own_total = jnp.sum(lengths)
    group_sums = lax.psum(partial_value, "seq")
    counts = lax.all_gather(jnp.reshape(own_total, (1,)), "seq", axis=0, tiled=True)
    group_mean = group_sums[0] / GROUP
    spread = jnp.maximum(jnp.sqrt(group_sums[1] / GROUP - group_mean * group_mean), 1.0)
    advantage = (
        reward_value - jnp.dot(member_table, group_mean, precision=lax.Precision.HIGHEST)
    ) / jnp.dot(member_table, spread, precision=lax.Precision.HIGHEST)
    log_ratio = ref_logp - old_logp
    penalty = jnp.exp(log_ratio) - log_ratio - 1.0
    token_terms = jnp.stack([jnp.repeat(advantage, LMAX), penalty], axis=1).astype(jnp.bfloat16)
    starts = jnp.cumsum(counts) - counts
    first_index = jnp.take(starts, seq_index)
    refined = refine(hidden, projection, norm_gain)
    return deliver(
        refined, token_terms, lengths, first_index, own_total, starts, seq_index, tile_rows, n_seq
    )


def solution(mesh):
    in_specs = (
        P("seq", ("sec", "tp")),
        P("seq", ("sec", "tp")),
        P(),
        P("seq"),
        P("seq"),
        P("seq"),
        P("seq"),
        P("seq"),
    )
    out_specs = (P("seq", ("sec", "tp")), P("seq", None))
    n = mesh.shape["seq"]
    in_place = mesh.shape["sec"] == n and n >= 4 and n & (n - 1) == 0
    body = shards_in_place if in_place else shards
    return jax.shard_map(body, mesh=mesh, in_specs=in_specs, out_specs=out_specs, check_vma=False)
```
